128 devices in a mesh: group: 4 (over z), dev: 32 (over x, y, core).
Axes of the slice: x: 4, y: 4, z: 4, core: 2. Of those that a mesh axis runs over, the one named last changes fastest.
Arguments:
- charges: bfloat16 [524288, 128], P(('group', 'dev')), may hold values from -6 to 6
- panel_coords: bfloat16 [2048, 3, 256], P(('group', 'dev')), may hold values from 0 to 1
- cluster_basis: bfloat16 [2048, 32, 256], P(('group', 'dev')), may hold values from -0.75 to 0.75
- trans_leaf: bfloat16 [2048, 32, 32], P(('group', 'dev')), may hold values from -0.75 to 0.75
- trans_pair: bfloat16 [128, 32, 32], P(('group', 'dev')), may hold values from -0.75 to 0.75
- trans_quad: bfloat16 [128, 32, 32], P(('group', 'dev')), may hold values from -0.5 to 0.5
- skel_points: bfloat16 [128, 3, 32], P(('group', 'dev')), may hold values from 0 to 1
- send_slots: int32 [4096, 1], P(('group', 'dev')), may hold values from 0 to 15
- pair_first: int32 [32768], P(('group', 'dev')), may hold values from 0 to 15
- pair_second: int32 [32768], P(('group', 'dev')), may hold values from 0 to 47
- pair_count: int32 [128], P(('group', 'dev')), may hold values from 64 to 256, as said below
- far_one: int32 [128, 8], P(('group', 'dev')), may hold values from 0 to 127
- far_two: int32 [128, 8], P(('group', 'dev')), may hold values from 0 to 63
- far_three: int32 [128, 8], P(('group', 'dev')), may hold values from 0 to 31
Outputs:
- potential: float32 [524288, 128], P(('group', 'dev'))
The draws below stay inside these ranges and needn't reach their ends.
Inputs may be any that keep to these rules, and one draw needn't show every extreme that they name: `send_slots`: row s * 32 + h holds local cluster indices of owner s sent to member h of its team; every slot is used. `pair_count`: some owner has all 256 pairs live.
All inputs are finite; a program needn't handle non-finite values.
Results may differ from the reference program's by a relative error of at most 0.0051.
Values may be sent and summed in bfloat16 or wider, within the bound.
A program may use at most 128 MiB of HBM per device.

```python
import jax
import jax.numpy as jnp
from jax import lax

CSIZE = 256
RANK = 32
RHS = 128
CL_DEV = 16
NP_DEV = 256
CAP = 1
FAR = 8
OWNERS = 128
TEAM = 32
SLOTS = 48
CLUSTERS = 2048
PANELS = 524288
N_GROUP = 4
N_DEV = 32


def draw_pair_count(key, part):
    key = jax.random.fold_in(key, 11)
    count_key, spot_key = jax.random.split(key)
    owners = N_GROUP * N_DEV
    counts = jax.random.randint(count_key, (owners,), NP_DEV // 4, NP_DEV + 1)
    spot = jax.random.randint(spot_key, (), 0, owners)
    return jnp.where(jnp.arange(owners) == spot, NP_DEV, counts).astype(jnp.int32)


def place_ends(array, stream_key, smallest, high):
    shape = array.shape
    spot = [jax.random.randint(jax.random.fold_in(stream_key, axis), (), 0, shape[axis]) for axis in range(len(shape))]
    array = array.at[tuple(spot)].set(smallest)
    longest = shape.index(max(shape))
    spot[longest] = (spot[longest] + 1) % shape[longest]
    return array.at[tuple(spot)].set(high)


def shard_levels(own_key, dims, shards, low, high):
    level, own = 1.0, jax.random.fold_in(own_key, 6)
    for dim, parts in shards:
        draws = jnp.exp(jax.random.uniform(jax.random.fold_in(own, dim), (parts,), jnp.float32, low / len(shards), high / len(shards)))
        level = level * jnp.repeat(draws, dims[dim] // parts).reshape([-1 if axis == dim else 1 for axis in range(len(dims))])
    return level


def noise(stream_key, extent, spread, limit, shards=(), held_as=jnp.bfloat16):
    level = shard_levels(stream_key, extent, shards, -0.22, 0.18) if shards else 1.0
    array = jax.random.normal(stream_key, extent, jnp.float32) * spread * level
    return jnp.minimum(jnp.maximum(array, -limit), limit).astype(held_as)


def setup_inputs(seed: int = 0) -> dict:
    arg_keys = jax.random.split(jax.random.key(seed), 15)
    return {
        "charges": noise(arg_keys[0], (PANELS, RHS), 1.0, 6.0, ((0, 128),)),
        "panel_coords": jnp.clip(1.0 * jax.random.uniform(arg_keys[1], (CLUSTERS, 3, CSIZE), jnp.float32) ** shard_levels(arg_keys[1], (CLUSTERS, 3, CSIZE), ((0, 128),), -0.2, 0.2), 0.0, 1.0).astype(jnp.bfloat16),
        "cluster_basis": noise(arg_keys[2], (CLUSTERS, RANK, CSIZE), 64 ** -0.5, 0.75, ((0, 128),)),
        "trans_leaf": noise(arg_keys[3], (CLUSTERS, RANK, RANK), 64 ** -0.5, 0.75, ((0, 128),)),
        "trans_pair": noise(arg_keys[4], (OWNERS, RANK, RANK), 64 ** -0.5, 0.75, ((0, 128),)),
        "trans_quad": noise(arg_keys[5], (OWNERS, RANK, RANK), 128 ** -0.5, 0.5, ((0, 128),)),
        "skel_points": jnp.clip(1.0 * jax.random.uniform(arg_keys[6], (OWNERS, 3, RANK), jnp.float32) ** shard_levels(arg_keys[6], (OWNERS, 3, RANK), ((0, 128),), -0.2, 0.2), 0.0, 1.0).astype(jnp.bfloat16),
        "send_slots": place_ends(jax.random.randint(arg_keys[7], (OWNERS * TEAM, CAP), 0, CL_DEV), jax.random.fold_in(arg_keys[7], 1), 0, CL_DEV - 1).astype(jnp.int32),
        "pair_first": place_ends(jax.random.randint(arg_keys[8], (OWNERS * NP_DEV,), 0, CL_DEV), jax.random.fold_in(arg_keys[8], 1), 0, CL_DEV - 1).astype(jnp.int32),
        "pair_second": place_ends(jax.random.randint(arg_keys[9], (OWNERS * NP_DEV,), 0, SLOTS), jax.random.fold_in(arg_keys[9], 1), 0, SLOTS - 1).astype(jnp.int32),
        "pair_count": draw_pair_count(jax.random.fold_in(arg_keys[14], 71), 0),
        "far_one": place_ends(jax.random.randint(arg_keys[11], (OWNERS, FAR), 0, OWNERS), jax.random.fold_in(arg_keys[11], 1), 0, OWNERS - 1).astype(jnp.int32),
        "far_two": place_ends(jax.random.randint(arg_keys[12], (OWNERS, FAR), 0, OWNERS // 2), jax.random.fold_in(arg_keys[12], 1), 0, (OWNERS // 2) - 1).astype(jnp.int32),
        "far_three": place_ends(jax.random.randint(arg_keys[13], (OWNERS, FAR), 0, OWNERS // 4), jax.random.fold_in(arg_keys[13], 1), 0, (OWNERS // 4) - 1).astype(jnp.int32),
    }


KCOEF = 0.005
DELTA = 0.02
HIGH = lax.Precision.HIGHEST

def coulomb(left, right):
    total = DELTA * DELTA
    for axis_id in range(3):
        source = left[..., axis_id, :].astype(jnp.float32)
        target = right[..., axis_id, :].astype(jnp.float32)
        gap = source[..., :, None] - target[..., None, :]
        total = total + gap * gap
    return KCOEF / jnp.sqrt(total)

def near_field(blocks, panel_coords, send_slots, pair_first, pair_second, pair_count):
    slot_ids = send_slots.reshape(OWNERS, TEAM, CAP)
    members = jnp.arange(TEAM, dtype=jnp.int32)
    local_index = jnp.arange(CL_DEV, dtype=jnp.int32)
    firsts_all = pair_first.reshape(OWNERS, NP_DEV // 16, 16)
    seconds_all = pair_second.reshape(OWNERS, NP_DEV // 16, 16)
    orders = jnp.arange(NP_DEV, dtype=jnp.int32).reshape(NP_DEV // 16, 16)

    def one_owner(phi, owner):
        team = owner // TEAM
        member = owner % TEAM
        senders = team * TEAM + members
        sent = slot_ids[senders, member, :]
        remote = (senders[:, None] * CL_DEV + sent).reshape(-1).astype(jnp.int32)
        own = (owner * CL_DEV + local_index).astype(jnp.int32)
        ids = jnp.concatenate([own, remote])
        table = blocks[ids]
        table_xyz = panel_coords[ids]
        count = pair_count[owner]
        firsts = firsts_all[owner]
        seconds = seconds_all[owner]

        def block_terms(inputs):
            first, second, index = inputs
            tile = coulomb(table_xyz[first], table_xyz[second]).astype(jnp.bfloat16)
            tile = lax.optimization_barrier(tile).astype(jnp.float32)
            to_first = jnp.einsum('pij,pjr->pir', tile, table[second].astype(jnp.float32), precision=HIGH)
            to_second = jnp.einsum('pij,pir->pjr', tile, table[first].astype(jnp.float32), precision=HIGH)
            live = (index < count).astype(jnp.float32)
            back = live * (first != second).astype(jnp.float32)
            return (to_first * live[:, None, None], to_second * back[:, None, None])
        to_first, to_second = lax.map(block_terms, (firsts, seconds, orders))
        sums = jax.ops.segment_sum(to_first.reshape(-1, CSIZE, RHS), firsts.reshape(-1), num_segments=SLOTS)
        sums = sums + jax.ops.segment_sum(to_second.reshape(-1, CSIZE, RHS), seconds.reshape(-1), num_segments=SLOTS)
        rounded = lax.optimization_barrier(sums[CL_DEV:].astype(jnp.bfloat16)).astype(jnp.float32)
        phi = phi.at[own].add(sums[:CL_DEV])
        phi = phi.at[remote].add(rounded)
        return (phi, None)
    start = jnp.zeros((CLUSTERS, CSIZE, RHS), jnp.float32)
    phi, _ = lax.scan(one_owner, start, jnp.arange(OWNERS, dtype=jnp.int32))
    return phi

def level_far(own_points, all_points, skeleton, far_ids):
    tiles = coulomb(own_points[:, None], all_points[far_ids])
    sources = skeleton[far_ids].astype(jnp.float32)
    return jnp.einsum('dfab,dfbr->dar', tiles, sources, precision=HIGH)

def reference(charges, panel_coords, cluster_basis, trans_leaf, trans_pair, trans_quad, skel_points, send_slots, pair_first, pair_second, pair_count, far_one, far_two, far_three):
    blocks = charges.reshape(CLUSTERS, CSIZE, RHS)
    near = near_field(blocks, panel_coords, send_slots, pair_first, pair_second, pair_count)
    leaf_skel = jnp.einsum('cak,ckr->car', cluster_basis.astype(jnp.float32), blocks.astype(jnp.float32), precision=HIGH).astype(jnp.bfloat16)
    leaf_skel = lax.optimization_barrier(leaf_skel)
    leaf_trans = trans_leaf.astype(jnp.float32).reshape(OWNERS, CL_DEV, RANK, RANK)
    top_skel = jnp.einsum('dcab,dcbr->dar', leaf_trans, leaf_skel.astype(jnp.float32).reshape(OWNERS, CL_DEV, RANK, RHS), precision=HIGH).astype(jnp.bfloat16)
    top_skel = lax.optimization_barrier(top_skel)
    top_wide = top_skel.astype(jnp.float32)
    pair_terms = jnp.einsum('dab,dbr->dar', trans_pair.astype(jnp.float32), top_wide, precision=HIGH)
    quad_terms = jnp.einsum('dab,dbr->dar', trans_quad.astype(jnp.float32), top_wide, precision=HIGH)
    pair_skel = (pair_terms[0::2] + pair_terms[1::2]).astype(jnp.bfloat16)
    quad_skel = (quad_terms[0::4] + quad_terms[1::4] + (quad_terms[2::4] + quad_terms[3::4])).astype(jnp.bfloat16)
    points_one = skel_points.astype(jnp.float32)
    points_two = 0.5 * (points_one[0::2] + points_one[1::2])
    points_three = 0.5 * (points_two[0::2] + points_two[1::2])
    far_top = level_far(points_one, points_one, top_skel, far_one)
    far_pair = level_far(jnp.repeat(points_two, 2, axis=0), points_two, pair_skel, far_two)
    far_quad = level_far(jnp.repeat(points_three, 4, axis=0), points_three, quad_skel, far_three)
    pair_down = jnp.repeat(far_pair[0::2] + far_pair[1::2], 2, axis=0)
    quad_down = jnp.repeat(far_quad[0::4] + far_quad[1::4] + (far_quad[2::4] + far_quad[3::4]), 4, axis=0)
    down = far_top + jnp.einsum('dba,dbr->dar', trans_pair.astype(jnp.float32), pair_down, precision=HIGH)
    down = down + jnp.einsum('dba,dbr->dar', trans_quad.astype(jnp.float32), quad_down, precision=HIGH)
    leaf_down = jnp.einsum('dcba,dbr->dcar', leaf_trans, down, precision=HIGH).astype(jnp.bfloat16)
    leaf_down = lax.optimization_barrier(leaf_down).astype(jnp.float32).reshape(CLUSTERS, RANK, RHS)
    far_pot = jnp.einsum('cak,car->ckr', cluster_basis.astype(jnp.float32), leaf_down, precision=HIGH)
    return (near + far_pot).reshape(PANELS, RHS)
```

```python
import functools

import jax
import jax.numpy as jnp
from jax import lax
from jax.experimental import pallas as pl
from jax.experimental.pallas import tpu as pltpu
from jax.sharding import PartitionSpec as P

KCOEF = 0.005
DELTA = 0.02
F32 = jnp.float32
BF16 = jnp.bfloat16
GROUP = 8
FEAT = 16
VMEM = pl.BlockSpec(memory_space=pltpu.VMEM)
SMEM = pl.BlockSpec(memory_space=pltpu.SMEM)
PARAMS = pltpu.CompilerParams(vmem_limit_bytes=56 << 20)


def dot(left, right, dims=((1,), (0,))):
    return lax.dot_general(left, right, (dims, ((), ())), preferred_element_type=F32)


def halves(value):
    high = value.astype(BF16)
    return high, (value - high.astype(F32)).astype(BF16)


def thirds(value):
    high = value.astype(BF16)
    rest = value - high.astype(F32)
    mid = rest.astype(BF16)
    return high.astype(F32), mid.astype(F32), (rest - mid.astype(F32))


def prep_kernel(slots, charges, coords, basis, trans, qt, fa, fb, outgoing, top, rows_a, rows_b):
    clusters = coords.shape[0]
    x = coords[...].astype(F32)
    axes = [x[:, d, :] for d in range(3)]
    norm = axes[0] * axes[0] + axes[1] * axes[1] + axes[2] * axes[2]
    one = jnp.ones_like(norm)
    rows_a[...] = jnp.zeros_like(rows_a)
    rows_b[...] = jnp.zeros_like(rows_b)
    for d, row in enumerate((*axes, *thirds(norm + DELTA * DELTA), one, one, one)):
        rows_a[:, d, :] = row
    for d, row in enumerate((*(-2.0 * a for a in axes), one, one, one, *thirds(norm))):
        rows_b[:, d, :] = row
    total = jnp.zeros(top.shape, F32)
    for c in range(clusters):
        fb[c] = rows_b[c].astype(BF16)
        fa[c] = rows_a[c].T.astype(BF16)
        block = charges[c]
        qt[c] = block.T
        leaf = dot(basis[c], block).astype(BF16)
        total += dot(trans[c], leaf)
    top[...] = total.astype(BF16)

    def send(h, carry):
        c = slots[h]
        outgoing[h, : qt.shape[1], :] = qt[c]
        outgoing[h, qt.shape[1] :, :] = fb[c]
        return carry

    lax.fori_loop(0, outgoing.shape[0], send, 0)


def prep(slots, charges, coords, basis, trans, peers):
    clusters, width, conductors = charges.shape
    rank = basis.shape[1]
    return pl.pallas_call(
        prep_kernel,
        out_shape=(
            jax.ShapeDtypeStruct((clusters, conductors, width), BF16),
            jax.ShapeDtypeStruct((clusters, width, FEAT), BF16),
            jax.ShapeDtypeStruct((clusters, FEAT, width), BF16),
            jax.ShapeDtypeStruct((peers, conductors + FEAT, width), BF16),
            jax.ShapeDtypeStruct((rank, conductors), BF16),
        ),
        in_specs=[SMEM] + [VMEM] * 4,
        out_specs=(VMEM,) * 5,
        scratch_shapes=[pltpu.VMEM((clusters, FEAT, width), F32)] * 2,
        compiler_params=PARAMS,
        name="prep",
    )(slots, charges, coords, basis, trans)


def tiles(count, table, weight, fa, feat, left, right, add_first, add_second, kbuf):
    def tile(j):
        key = table[j]
        s = dot(fa[lax.rem(key, 16)], feat(key // 16))
        return lax.rsqrt(s.astype(BF16)) * weight[j].astype(BF16)

    for g in range(GROUP):
        kbuf[0, g] = tile(g)

    def body(i, carry):
        now = lax.rem(i, 2)
        for g in range(GROUP):
            j = i * GROUP + g
            key = table[j]
            a, b = lax.rem(key, 16), key // 16
            k = kbuf[now, g]
            add_first(a, dot(right(b), k, ((1,), (1,))))
            add_second(b, dot(left(a), k))
            kbuf[1 - now, g] = tile(j + GROUP)
        return carry

    lax.fori_loop(0, pl.cdiv(count, GROUP), body, 0)


def own_kernel(count, table, weight, qt, fa, fb, acc, kbuf):
    acc[...] = jnp.zeros_like(acc)

    def add(i, value):
        acc[i] += value

    tiles(count[0], table, weight, fa, lambda b: fb[b], lambda a: qt[a], lambda b: qt[b], add, add, kbuf)


def own_near(count, table, weight, qt, fa, fb):
    width = qt.shape[2]
    return pl.pallas_call(
        own_kernel,
        out_shape=jax.ShapeDtypeStruct(qt.shape, F32),
        in_specs=[SMEM] * 3 + [VMEM] * 3,
        out_specs=VMEM,
        scratch_shapes=[pltpu.VMEM((2, GROUP, width, width), BF16)],
        compiler_params=PARAMS,
        cost_estimate=pl.CostEstimate(flops=6 << 30, bytes_accessed=4 << 20, transcendentals=0),
        name="own_near",
    )(count, table, weight, qt, fa, fb)


def remote_kernel(count, table, weight, qt, fa, incoming, acc_in, acc, back, sums, kbuf):
    conductors = qt.shape[1]
    acc[...] = acc_in[...]
    sums[...] = jnp.zeros_like(sums)

    def add_own(i, value):
        acc[i] += value

    def add_remote(i, value):
        sums[i] += value

    tiles(
        count[0],
        table,
        weight,
        fa,
        lambda b: incoming[b, conductors:, :],
        lambda a: qt[a],
        lambda b: incoming[b, :conductors, :],
        add_own,
        add_remote,
        kbuf,
    )

    def finish(b, carry):
        back[b] = (sums[b] * KCOEF).astype(BF16)
        return carry

    lax.fori_loop(0, back.shape[0], finish, 0)


def remote_near(count, table, weight, qt, fa, incoming, acc):
    peers = incoming.shape[0]
    _, conductors, width = qt.shape
    return pl.pallas_call(
        remote_kernel,
        out_shape=(
            jax.ShapeDtypeStruct(acc.shape, F32),
            jax.ShapeDtypeStruct((peers, conductors, width), BF16),
        ),
        in_specs=[SMEM] * 3 + [VMEM] * 4,
        out_specs=(VMEM, VMEM),
        scratch_shapes=[
            pltpu.VMEM((peers, conductors, width), F32),
            pltpu.VMEM((2, GROUP, width, width), BF16),
        ],
        compiler_params=PARAMS,
        cost_estimate=pl.CostEstimate(flops=12 << 30, bytes_accessed=8 << 20, transcendentals=0),
        name="remote_near",
    )(count, table, weight, qt, fa, incoming, acc)


def far_kernel(ids, own_points, nodes, trans, leaf, sources):
    rank = 32

    def skel(n):
        return nodes[n, :rank, :]

    def transfer(n, which):
        rows = nodes[n, rank : rank + 16, :]
        lo = 64 * which
        return jnp.concatenate([rows[:, lo : lo + 32], rows[:, lo + 32 : lo + 64]], axis=0)

    def points(n):
        return nodes[n, rank + 16 : rank + 32, :].astype(F32)[:1]

    def kernel_tile(mine, theirs):
        gap = mine - theirs
        sq = gap * gap
        s = ((DELTA * DELTA + sq[:, :32]) + sq[:, 32:64]) + sq[:, 64:96]
        return halves(KCOEF * lax.rsqrt(s))

    def apply(tile, source):
        return dot(tile[0], source) + dot(tile[1], source)

    mine = [own_points[level] for level in range(3)]
    zero = jnp.zeros((rank, nodes.shape[2]), F32)

    def one(f, total):
        n = ids[f]
        return total + apply(kernel_tile(mine[0], points(n)), skel(n))

    def two(f, total):
        n = 2 * ids[8 + f]
        source = dot(transfer(n, 0), skel(n)) + dot(transfer(n + 1, 0), skel(n + 1))
        theirs = 0.5 * (points(n) + points(n + 1))
        return total + apply(kernel_tile(mine[1], theirs), source.astype(BF16))

    def three(f, total):
        n = 4 * ids[24 + f]
        terms = [dot(transfer(n + i, 1), skel(n + i)) for i in range(4)]
        source = (terms[0] + terms[1]) + (terms[2] + terms[3])
        left = 0.5 * (points(n) + points(n + 1))
        right = 0.5 * (points(n + 2) + points(n + 3))
        return total + apply(kernel_tile(mine[2], 0.5 * (left + right)), source.astype(BF16))

    far_one = lax.fori_loop(0, 8, one, zero, unroll=True)
    far_two = lax.fori_loop(0, 16, two, zero, unroll=4)
    far_three = lax.fori_loop(0, 32, three, zero, unroll=4)
    me = ids[56]

    def down_by(which, value):
        high, low = halves(value)
        mat = transfer(me, which)
        return dot(mat, high, ((0,), (0,))) + dot(mat, low, ((0,), (0,)))

    down = far_one + down_by(0, far_two) + down_by(1, far_three)
    high, low = halves(down.T)
    for c in range(trans.shape[0]):
        leaf[c] = (dot(high, trans[c]) + dot(low, trans[c])).astype(BF16)


def far_field(ids, own_points, nodes, trans):
    clusters, rank, _ = trans.shape
    return pl.pallas_call(
        far_kernel,
        out_shape=jax.ShapeDtypeStruct((clusters, nodes.shape[2], rank), BF16),
        in_specs=[SMEM] + [VMEM] * 3,
        out_specs=VMEM,
        scratch_shapes=[pltpu.VMEM((8, 128), F32)],
        compiler_params=PARAMS,
        cost_estimate=pl.CostEstimate(flops=6 << 30, bytes_accessed=4 << 20, transcendentals=0),
        name="far_field",
    )(ids, own_points, nodes, trans)


def final_kernel(slots, acc, returned, leaf, basis, out, sums):
    def scale(c, carry):
        sums[c] = acc[c] * KCOEF + dot(leaf[c], basis[c])
        return carry

    lax.fori_loop(0, acc.shape[0], scale, 0)

    def collect(h, carry):
        sums[slots[h]] += returned[h].astype(F32)
        return carry

    lax.fori_loop(0, returned.shape[0], collect, 0)

    def turn(c, carry):
        out[c] = sums[c].T
        return carry

    lax.fori_loop(0, acc.shape[0], turn, 0)


def finish(slots, acc, returned, leaf, basis):
    clusters, conductors, width = acc.shape
    return pl.pallas_call(
        final_kernel,
        out_shape=jax.ShapeDtypeStruct((clusters, width, conductors), F32),
        in_specs=[SMEM] + [VMEM] * 4,
        out_specs=VMEM,
        scratch_shapes=[pltpu.VMEM(acc.shape, F32)],
        compiler_params=PARAMS,
        name="finish",
    )(slots, acc, returned, leaf, basis)


def pair_lists(first, second, count, clusters, entries):
    live = jnp.arange(first.shape[0], dtype=jnp.int32) < count
    own = second < clusters
    a = jnp.where(own, jnp.minimum(first, second), first)
    b = jnp.where(own, jnp.maximum(first, second), second)
    key = jnp.where(live, b * clusters + a, -1)
    keys = jnp.arange(entries * clusters, dtype=jnp.int32)
    times = jnp.sum((keys[:, None] == key[None, :]).astype(F32), axis=1)
    times = jnp.where(keys % clusters == keys // clusters, 0.5 * times, times)
    lists = []
    for lo, hi in ((0, clusters * clusters), (clusters * clusters, entries * clusters)):
        part = times[lo:hi]
        held = part > 0
        spots = jnp.arange(hi - lo, dtype=jnp.int32)
        rank = jnp.sum(((spots[None, :] < spots[:, None]) & held[None, :]).astype(jnp.int32), axis=1)
        slots = jnp.arange(256 + 2 * GROUP, dtype=jnp.int32)
        match = (rank[None, :] == slots[:, None]) & held[None, :]
        table = jnp.sum(jnp.where(match, spots[None, :], 0), axis=1)
        weight = jnp.sum(jnp.where(match, part[None, :], 0.0), axis=1)
        lists.append((jnp.sum(held.astype(jnp.int32)).reshape(1), table, weight))
    return lists


def shards(
    charges,
    panel_coords,
    cluster_basis,
    trans_leaf,
    trans_pair,
    trans_quad,
    skel_points,
    send_slots,
    pair_first,
    pair_second,
    pair_count,
    far_one,
    far_two,
    far_three,
):
    clusters, _, width = panel_coords.shape
    conductors = charges.shape[1]
    peers = lax.axis_size("dev")
    slots = send_slots.reshape(-1)
    blocks = charges.reshape(clusters, width, conductors)
    qt, fa, fb, outgoing, top = prep(slots, blocks, panel_coords, cluster_basis, trans_leaf, peers)
    incoming = lax.all_to_all(outgoing, "dev", split_axis=0, concat_axis=0, tiled=True)

    def folded(mat):
        return jnp.concatenate([mat[0, :16], mat[0, 16:]], axis=1)

    points_row = skel_points.reshape(1, -1)
    lists_row = jnp.concatenate([far_two, far_three], axis=1).astype(BF16)
    payload = jnp.concatenate(
        [
            top,
            jnp.concatenate([folded(trans_pair), folded(trans_quad)], axis=1),
            jnp.pad(points_row, ((0, 0), (0, conductors - points_row.shape[1]))),
            jnp.pad(lists_row, ((0, 14), (0, conductors - lists_row.shape[1]))),
        ],
        axis=0,
    )
    nodes = lax.all_gather(payload, ("group", "dev"), axis=0)

    own_list, remote_list = pair_lists(pair_first, pair_second, pair_count[0], clusters, clusters + peers)
    acc = own_near(*own_list, qt, fa, fb)
    acc, back = remote_near(*remote_list, qt, fa, incoming, acc)
    returned = lax.all_to_all(back, "dev", split_axis=0, concat_axis=0, tiled=True)

    owner = lax.axis_index("group") * peers + lax.axis_index("dev")
    quad = lax.dynamic_slice_in_dim(nodes, owner // 4 * 4, 4, axis=0)
    quad_lists = quad[:, 49, :16].astype(jnp.int32)
    pair_list = lax.dynamic_slice_in_dim(quad_lists[:, :8], owner % 4 // 2 * 2, 2, axis=0)
    ids = jnp.concatenate(
        [far_one[0], pair_list.reshape(-1), quad_lists[:, 8:].reshape(-1), owner.reshape(1)]
    )
    quad_points = quad[:, 48, :96].astype(F32).reshape(4, 3, 32)
    pair_points = 0.5 * (quad_points[0::2] + quad_points[1::2])
    own_points = jnp.stack(
        [
            skel_points[0].astype(F32),
            jnp.take(pair_points, owner % 4 // 2, axis=0),
            0.5 * (pair_points[0] + pair_points[1]),
        ]
    )
    own_points = jnp.repeat(jnp.swapaxes(own_points, 1, 2), 32, axis=2)
    own_points = jnp.pad(own_points, ((0, 0), (0, 0), (0, 32)))
    leaf = far_field(ids, own_points, nodes, trans_leaf)
    out = finish(slots, acc, returned, leaf, cluster_basis)
    return out.reshape(clusters * width, conductors)


def solution(mesh):
    owners = ("group", "dev")
    rows, block, flat = P(owners, None), P(owners, None, None), P(owners)
    placed = (rows, *(block,) * 6, rows, *(flat,) * 3, *(rows,) * 3)
    return jax.shard_map(shards, mesh=mesh, in_specs=placed, out_specs=rows, check_vma=False)
```

```python
import functools

import jax
import jax.numpy as jnp
from jax import lax
from jax.experimental import pallas as pl
from jax.experimental.pallas import tpu as pltpu
from jax.sharding import PartitionSpec as P

KCOEF = 0.005
DELTA = 0.02
F32 = jnp.float32
BF16 = jnp.bfloat16
GROUP = 8
FEAT = 16
VMEM = pl.BlockSpec(memory_space=pltpu.VMEM)
SMEM = pl.BlockSpec(memory_space=pltpu.SMEM)
MESH = pl.DeviceIdType.MESH
PARAMS = pltpu.CompilerParams(vmem_limit_bytes=56 << 20)


def dot(left, right, dims=((1,), (0,))):
    return lax.dot_general(left, right, (dims, ((), ())), preferred_element_type=F32)


def halves(value):
    high = value.astype(BF16)
    return high, (value - high.astype(F32)).astype(BF16)


def thirds(value):
    high = value.astype(BF16)
    rest = value - high.astype(F32)
    mid = rest.astype(BF16)
    return high.astype(F32), mid.astype(F32), (rest - mid.astype(F32))


def prep_kernel(slots, charges, axes, qt, fa, fb, outgoing, rows_a, rows_b, sems):
    clusters = charges.shape[0]
    x = [axes[d] for d in range(3)]
    norm = x[0] * x[0] + x[1] * x[1] + x[2] * x[2]
    one = jnp.ones_like(norm)
    rows_a[...] = jnp.zeros_like(rows_a)
    rows_b[...] = jnp.zeros_like(rows_b)
    for d, row in enumerate((*x, *thirds(norm + DELTA * DELTA), one, one, one)):
        rows_a[:, d, :] = row
    for d, row in enumerate((*(-2.0 * a for a in x), one, one, one, *thirds(norm))):
        rows_b[:, d, :] = row
    for c in range(clusters):
        fb[c] = rows_b[c].astype(BF16)
        qt[c] = charges[c].T
    split = qt.shape[1]

    def copies(h):
        c = slots[h, 0]
        return (
            pltpu.make_async_copy(qt.at[c], outgoing.at[h, pl.ds(0, split)], sems.at[h, 0]),
            pltpu.make_async_copy(fb.at[c], outgoing.at[h, pl.ds(split, FEAT)], sems.at[h, 1]),
        )

    def send(h, carry):
        for copy in copies(h):
            copy.start()
        return carry

    def wait(h, carry):
        for copy in copies(h):
            copy.wait()
        return carry

    lax.fori_loop(0, outgoing.shape[0], send, 0)
    for c in range(clusters):
        fa[c] = rows_a[c].T.astype(BF16)
    lax.fori_loop(0, outgoing.shape[0], wait, 0)


def prep(slots, charges, axes):
    clusters, width, conductors = charges.shape
    peers = slots.shape[0]
    return pl.pallas_call(
        prep_kernel,
        out_shape=(
            jax.ShapeDtypeStruct((clusters, conductors, width), BF16),
            jax.ShapeDtypeStruct((clusters, width, FEAT), BF16),
            jax.ShapeDtypeStruct((clusters, FEAT, width), BF16),
            jax.ShapeDtypeStruct((peers, conductors + FEAT, width), BF16),
        ),
        in_specs=[SMEM] + [VMEM] * 2,
        out_specs=(VMEM, VMEM, VMEM, pl.BlockSpec(memory_space=pl.ANY)),
        scratch_shapes=[pltpu.VMEM((clusters, FEAT, width), F32)] * 2
        + [pltpu.SemaphoreType.DMA((peers, 2))],
        compiler_params=PARAMS,
        name="prep",
    )(slots, charges, axes)


def gather_kernel(charges, basis, trans, rest, nodes, send_sem, recv_sem):
    z, d = lax.axis_index("group"), lax.axis_index("dev")
    x, y, c = d // 8, lax.rem(d // 2, 4), lax.rem(d, 2)

    def place(x, y, z, c):
        return {"group": z, "dev": (x * 4 + y) * 2 + c}

    def turn(i, k):
        return lax.rem(i + k, 4)

    stages = (
        (((c * 4 + z) * 4 + y) * 4 + x, 1, [place(turn(x, k), y, z, c) for k in (1, 2, 3)]),
        (((c * 4 + z) * 4 + y) * 4, 4, [place(x, turn(y, k), z, c) for k in (1, 2, 3)]),
        ((c * 4 + z) * 16, 16, [place(x, y, turn(z, k), c) for k in (1, 2, 3)]),
        (c * 64, 64, [place(x, y, z, 1 - c)]),
    )
    barrier = pltpu.get_barrier_semaphore()
    for _, _, peers in stages:
        for peer in peers:
            pl.semaphore_signal(barrier, inc=1, device_id=peer, device_id_type=MESH)

    rank = trans.shape[1]
    total = jnp.zeros((rank, charges.shape[2]), F32)
    for i in range(trans.shape[0]):
        leaf = dot(basis[i], charges[i]).astype(BF16)
        total += dot(trans[i], leaf)
    me = stages[0][0]
    nodes[me, :rank, :] = total.astype(BF16)
    nodes[me, rank:, :] = rest[...]
    pl.semaphore_wait(barrier, 10)

    for level, (start, length, peers) in enumerate(stages):
        held = nodes.at[pl.ds(start, length)]
        copies = [
            pltpu.make_async_remote_copy(
                src_ref=held,
                dst_ref=held,
                send_sem=send_sem.at[level, k],
                recv_sem=recv_sem.at[level, k],
                device_id=peer,
                device_id_type=MESH,
            )
            for k, peer in enumerate(peers)
        ]
        for copy in copies:
            copy.start()
        for copy in copies:
            copy.wait()


def gather_nodes(charges, basis, trans, rest):
    rank, conductors = trans.shape[1], charges.shape[2]
    return pl.pallas_call(
        gather_kernel,
        out_shape=jax.ShapeDtypeStruct((128, rank + rest.shape[0], conductors), BF16),
        in_specs=[VMEM] * 4,
        out_specs=VMEM,
        scratch_shapes=[pltpu.SemaphoreType.DMA((4, 3))] * 2,
        compiler_params=pltpu.CompilerParams(
            vmem_limit_bytes=32 << 20, collective_id=0, has_side_effects=True
        ),
        cost_estimate=pl.CostEstimate(flops=12 << 30, bytes_accessed=4 << 20, transcendentals=0),
        name="gather_nodes",
    )(charges, basis, trans, rest)


def tiles(count, table, weight, fa, feat, left, right, add_first, add_second, kbuf):
    def tile(j):
        key = table[j]
        s = dot(fa[lax.rem(key, 16)], feat(key // 16))
        return lax.rsqrt(s.astype(BF16)) * weight[j].astype(BF16)

    for g in range(GROUP):
        kbuf[0, g] = tile(g)

    def body(i, carry):
        now = lax.rem(i, 2)
        for g in range(GROUP):
            j = i * GROUP + g
            key = table[j]
            a, b = lax.rem(key, 16), key // 16
            k = kbuf[now, g]
            add_first(a, dot(right(b), k, ((1,), (1,))))
            add_second(b, dot(left(a), k))
            kbuf[1 - now, g] = tile(j + GROUP)
        return carry

    lax.fori_loop(0, pl.cdiv(count, GROUP), body, 0)


def own_kernel(count, table, weight, qt, fa, fb, acc, kbuf):
    acc[...] = jnp.zeros_like(acc)

    def add(i, value):
        acc[i] += value

    tiles(count[0], table, weight, fa, lambda b: fb[b], lambda a: qt[a], lambda b: qt[b], add, add, kbuf)


def own_near(count, table, weight, qt, fa, fb):
    width = qt.shape[2]
    return pl.pallas_call(
        own_kernel,
        out_shape=jax.ShapeDtypeStruct(qt.shape, F32),
        in_specs=[SMEM] * 3 + [VMEM] * 3,
        out_specs=VMEM,
        scratch_shapes=[pltpu.VMEM((2, GROUP, width, width), BF16)],
        compiler_params=PARAMS,
        cost_estimate=pl.CostEstimate(flops=6 << 30, bytes_accessed=4 << 20, transcendentals=0),
        name="own_near",
    )(count, table, weight, qt, fa, fb)


def reply_kernel(count, table, weight, qt, fa, incoming, back, kbuf):
    conductors, width = qt.shape[1:]
    back[...] = jnp.zeros_like(back)

    def tile(j):
        key = table[j]
        s = dot(fa[lax.rem(key, 16)], incoming[key // 16, conductors:, :])
        return lax.rsqrt(s.astype(BF16)) * weight[j].astype(BF16)

    for g in range(GROUP):
        kbuf[0, g] = tile(g)

    def body(i, total):
        now = lax.rem(i, 2)
        for g in range(GROUP):
            j = i * GROUP + g
            before = table[jnp.maximum(j - 1, 0)] // 16
            key = table[j]
            a, b = lax.rem(key, 16), key // 16
            keep = jnp.where(before == b, 1.0, 0.0).astype(F32)
            total = total * keep + dot(qt[a], kbuf[now, g])
            back[b] = total.astype(BF16)
            kbuf[1 - now, g] = tile(j + GROUP)
        return total

    lax.fori_loop(0, pl.cdiv(count[0], GROUP), body, jnp.zeros((conductors, width), F32))


def reply(count, table, weight, qt, fa, incoming):
    peers = incoming.shape[0]
    _, conductors, width = qt.shape
    return pl.pallas_call(
        reply_kernel,
        out_shape=jax.ShapeDtypeStruct((peers, conductors, width), BF16),
        in_specs=[SMEM] * 3 + [VMEM] * 3,
        out_specs=VMEM,
        scratch_shapes=[pltpu.VMEM((2, GROUP, width, width), BF16)],
        compiler_params=PARAMS,
        cost_estimate=pl.CostEstimate(flops=6 << 30, bytes_accessed=8 << 20, transcendentals=0),
        name="reply",
    )(count, table, weight, qt, fa, incoming)


def remote_kernel(count, table, weight, fa, incoming, acc_in, acc, kbuf):
    conductors = acc.shape[1]
    acc[...] = acc_in[...]

    def tile(j):
        key = table[j]
        s = dot(fa[lax.rem(key, 16)], incoming[key // 16, conductors:, :])
        return lax.rsqrt(s.astype(BF16)) * weight[j].astype(BF16)

    for g in range(GROUP):
        kbuf[0, g] = tile(g)

    def body(i, carry):
        now = lax.rem(i, 2)
        for g in range(GROUP):
            j = i * GROUP + g
            key = table[j]
            a, b = lax.rem(key, 16), key // 16
            acc[a] += dot(incoming[b, :conductors, :], kbuf[now, g], ((1,), (1,)))
            kbuf[1 - now, g] = tile(j + GROUP)
        return carry

    lax.fori_loop(0, pl.cdiv(count[0], GROUP), body, 0)


def remote_near(count, table, weight, fa, incoming, acc):
    width = acc.shape[2]
    return pl.pallas_call(
        remote_kernel,
        out_shape=jax.ShapeDtypeStruct(acc.shape, F32),
        in_specs=[SMEM] * 3 + [VMEM] * 3,
        out_specs=VMEM,
        scratch_shapes=[pltpu.VMEM((2, GROUP, width, width), BF16)],
        compiler_params=PARAMS,
        cost_estimate=pl.CostEstimate(flops=6 << 30, bytes_accessed=8 << 20, transcendentals=0),
        name="remote_near",
    )(count, table, weight, fa, incoming, acc)


def far_kernel(ids, own_points, nodes, trans, leaf, sources):
    rank = 32

    def skel(n):
        return nodes[n, :rank, :]

    def transfer(n, which):
        rows = nodes[n, rank : rank + 16, :]
        lo = 64 * which
        return jnp.concatenate([rows[:, lo : lo + 32], rows[:, lo + 32 : lo + 64]], axis=0)

    def points(n):
        return nodes[n, rank + 16 : rank + 32, :].astype(F32)[:1]

    def kernel_tile(mine, theirs):
        gap = mine - theirs
        sq = gap * gap
        s = ((DELTA * DELTA + sq[:, :32]) + sq[:, 32:64]) + sq[:, 64:96]
        return halves(KCOEF * lax.rsqrt(s))

    def apply(tile, source):
        return dot(tile[0], source) + dot(tile[1], source)

    mine = [own_points[level] for level in range(3)]
    zero = jnp.zeros((rank, nodes.shape[2]), F32)

    def one(f, total):
        n = ids[f]
        return total + apply(kernel_tile(mine[0], points(n)), skel(n))

    def two(f, total):
        n, m = ids[8 + f], ids[8 + f] + 64
        source = dot(transfer(n, 0), skel(n)) + dot(transfer(m, 0), skel(m))
        theirs = 0.5 * (points(n) + points(m))
        return total + apply(kernel_tile(mine[1], theirs), source.astype(BF16))

    def three(f, total):
        n = [ids[24 + f] + step for step in (0, 64, 4, 68)]
        terms = [dot(transfer(i, 1), skel(i)) for i in n]
        source = (terms[0] + terms[1]) + (terms[2] + terms[3])
        left = 0.5 * (points(n[0]) + points(n[1]))
        right = 0.5 * (points(n[2]) + points(n[3]))
        return total + apply(kernel_tile(mine[2], 0.5 * (left + right)), source.astype(BF16))

    far_one = lax.fori_loop(0, 8, one, zero, unroll=True)
    far_two = lax.fori_loop(0, 16, two, zero, unroll=4)
    far_three = lax.fori_loop(0, 32, three, zero, unroll=4)
    me = ids[56]

    def down_by(which, value):
        high, low = halves(value)
        mat = transfer(me, which)
        return dot(mat, high, ((0,), (0,))) + dot(mat, low, ((0,), (0,)))

    down = far_one + down_by(0, far_two) + down_by(1, far_three)
    high, low = halves(down.T)
    for c in range(trans.shape[0]):
        leaf[c] = (dot(high, trans[c]) + dot(low, trans[c])).astype(BF16)


def far_field(ids, own_points, nodes, trans):
    clusters, rank, _ = trans.shape
    return pl.pallas_call(
        far_kernel,
        out_shape=jax.ShapeDtypeStruct((clusters, nodes.shape[2], rank), BF16),
        in_specs=[SMEM] + [VMEM] * 3,
        out_specs=VMEM,
        scratch_shapes=[pltpu.VMEM((8, 128), F32)],
        compiler_params=PARAMS,
        cost_estimate=pl.CostEstimate(flops=6 << 30, bytes_accessed=4 << 20, transcendentals=0),
        name="far_field",
    )(ids, own_points, nodes, trans)


def base_kernel(acc, leaf, basis, base):
    def one(c, carry):
        base[c] = acc[c] * KCOEF + dot(leaf[c], basis[c])
        return carry

    lax.fori_loop(0, acc.shape[0], one, 0)


def base_sum(acc, leaf, basis):
    return pl.pallas_call(
        base_kernel,
        out_shape=jax.ShapeDtypeStruct(acc.shape, F32),
        in_specs=[VMEM] * 3,
        out_specs=VMEM,
        compiler_params=PARAMS,
        cost_estimate=pl.CostEstimate(flops=2 << 30, bytes_accessed=4 << 20, transcendentals=0),
        name="base_sum",
    )(acc, leaf, basis)


def final_kernel(order, starts, base, returned, out, rows, sems):
    clusters = base.shape[0]

    def copy(c):
        return pltpu.make_async_copy(rows.at[c], out.at[c], sems.at[c])

    for c in range(clusters):

        def collect(i, total):
            return total + returned[order[i]].astype(F32)

        zero = jnp.zeros(base.shape[1:], F32)
        total = lax.fori_loop(starts[c], starts[c + 1], collect, zero)
        rows[c] = (base[c] + KCOEF * total).T
        copy(c).start()
    for c in range(clusters):
        copy(c).wait()


def finish(order, starts, base, returned):
    clusters, conductors, width = base.shape
    return pl.pallas_call(
        final_kernel,
        out_shape=jax.ShapeDtypeStruct((clusters, width, conductors), F32),
        in_specs=[SMEM] * 2 + [VMEM] * 2,
        out_specs=pl.BlockSpec(memory_space=pl.ANY),
        scratch_shapes=[
            pltpu.VMEM((clusters, width, conductors), F32),
            pltpu.SemaphoreType.DMA((clusters,)),
        ],
        compiler_params=PARAMS,
        name="finish",
    )(order, starts, base, returned)


def pair_lists(first, second, count, clusters, entries):
    live = jnp.arange(first.shape[0], dtype=jnp.int32) < count
    own = second < clusters
    a = jnp.where(own, jnp.minimum(first, second), first)
    b = jnp.where(own, jnp.maximum(first, second), second)
    key = jnp.where(live, b * clusters + a, -1)
    keys = jnp.arange(entries * clusters, dtype=jnp.int32)
    times = jnp.sum((keys[:, None] == key[None, :]).astype(F32), axis=1)
    times = jnp.where(keys % clusters == keys // clusters, 0.5 * times, times)
    lists = []
    for lo, hi in ((0, clusters * clusters), (clusters * clusters, entries * clusters)):
        part = times[lo:hi]
        held = part > 0
        spots = jnp.arange(hi - lo, dtype=jnp.int32)
        rank = jnp.sum(((spots[None, :] < spots[:, None]) & held[None, :]).astype(jnp.int32), axis=1)
        slots = jnp.arange(256 + 2 * GROUP, dtype=jnp.int32)
        match = (rank[None, :] == slots[:, None]) & held[None, :]
        total = jnp.sum(held.astype(jnp.int32))
        last = jnp.max(jnp.where(held, spots, 0))
        table = jnp.sum(jnp.where(match, spots[None, :], 0), axis=1)
        table = jnp.where(slots < total, table, last)
        weight = jnp.sum(jnp.where(match, part[None, :], 0.0), axis=1)
        lists.append((total.reshape(1), table, weight))
    return lists


def shards(
    charges,
    panel_coords,
    cluster_basis,
    trans_leaf,
    trans_pair,
    trans_quad,
    skel_points,
    send_slots,
    pair_first,
    pair_second,
    pair_count,
    far_one,
    far_two,
    far_three,
):
    clusters, _, width = panel_coords.shape
    conductors = charges.shape[1]
    peers = lax.axis_size("dev")
    blocks = charges.reshape(clusters, width, conductors)
    axes = jnp.swapaxes(panel_coords, 0, 1).astype(F32)
    qt, fa, fb, outgoing = prep(send_slots, blocks, axes)
    incoming = lax.all_to_all(outgoing, "dev", split_axis=0, concat_axis=0, tiled=True)

    def folded(mat):
        return jnp.concatenate([mat[0, :16], mat[0, 16:]], axis=1)

    points_row = skel_points.reshape(1, -1)
    lists_row = jnp.concatenate([far_two, far_three], axis=1).astype(BF16)
    rest = jnp.concatenate(
        [
            jnp.concatenate([folded(trans_pair), folded(trans_quad)], axis=1),
            jnp.pad(points_row, ((0, 0), (0, conductors - points_row.shape[1]))),
            jnp.pad(lists_row, ((0, 14), (0, conductors - lists_row.shape[1]))),
        ],
        axis=0,
    )
    nodes = gather_nodes(blocks, cluster_basis, trans_leaf, rest)

    own_list, remote_list = pair_lists(pair_first, pair_second, pair_count[0], clusters, clusters + peers)
    acc = own_near(*own_list, qt, fa, fb)
    back = reply(*remote_list, qt, fa, incoming)
    returned = lax.all_to_all(back, "dev", split_axis=0, concat_axis=0, tiled=True)
    acc = remote_near(*remote_list, fa, incoming, acc)

    z, d = lax.axis_index("group"), lax.axis_index("dev")
    x, y, c = d // 8, d // 2 % 4, d % 2

    def place(owner):
        z, d = owner // 32, owner % 32
        return ((d % 2 * 4 + z) * 4 + d // 2 % 4) * 4 + d // 8

    info = nodes[:, 48:50, :].reshape(2, 4, 4, 4, 2, conductors)
    quad = lax.dynamic_slice(info, (0, z, y // 2 * 2, x, 0, 0), (2, 1, 2, 1, 2, conductors))
    quad = jnp.swapaxes(quad.reshape(2, 2, 2, conductors), 0, 1)
    quad_lists = quad[:, :, 1, :16].astype(jnp.int32)
    pair_list = lax.dynamic_index_in_dim(quad_lists[..., :8], y % 2, axis=0, keepdims=False)
    ids = jnp.concatenate(
        [
            place(far_one[0]),
            place(2 * pair_list.reshape(-1)),
            place(4 * quad_lists[..., 8:].reshape(-1)),
            place(z * peers + d).reshape(1),
        ]
    )
    quad_points = quad[:, :, 0, :96].astype(F32).reshape(2, 2, 3, 32)
    pair_points = 0.5 * (quad_points[:, 0] + quad_points[:, 1])
    own_points = jnp.stack(
        [
            skel_points[0].astype(F32),
            lax.dynamic_index_in_dim(pair_points, y % 2, axis=0, keepdims=False),
            0.5 * (pair_points[0] + pair_points[1]),
        ]
    )
    own_points = jnp.repeat(jnp.swapaxes(own_points, 1, 2), 32, axis=2)
    own_points = jnp.pad(own_points, ((0, 0), (0, 0), (0, 32)))
    leaf = far_field(ids, own_points, nodes, trans_leaf)
    base = base_sum(acc, leaf, cluster_basis)

    slots = send_slots[:, 0]
    spots = jnp.arange(peers, dtype=jnp.int32)
    rank = jnp.sum(
        (slots[None, :] < slots[:, None])
        | ((slots[None, :] == slots[:, None]) & (spots[None, :] < spots[:, None])),
        axis=1,
        dtype=jnp.int32,
    )
    order = jnp.sum(jnp.where(rank[None, :] == spots[:, None], spots[None, :], 0), axis=1)
    edges = jnp.arange(clusters + 1, dtype=jnp.int32)
    starts = jnp.sum(slots[None, :] < edges[:, None], axis=1, dtype=jnp.int32)
    out = finish(order, starts, base, returned)
    return out.reshape(clusters * width, conductors)


def solution(mesh):
    owners = ("group", "dev")
    rows, block, flat = P(owners, None), P(owners, None, None), P(owners)
    placed = (rows, *(block,) * 6, rows, *(flat,) * 3, *(rows,) * 3)
    return jax.shard_map(shards, mesh=mesh, in_specs=placed, out_specs=rows, check_vma=False)
```

```python
import functools

import jax
import jax.numpy as jnp
from jax import lax
from jax.experimental import pallas as pl
from jax.experimental.pallas import tpu as pltpu
from jax.sharding import PartitionSpec as P

KCOEF = 0.005
DELTA = 0.02
F32 = jnp.float32
BF16 = jnp.bfloat16
GROUP = 8
FEAT = 16
VMEM = pl.BlockSpec(memory_space=pltpu.VMEM)
SMEM = pl.BlockSpec(memory_space=pltpu.SMEM)
MESH = pl.DeviceIdType.MESH
PARAMS = pltpu.CompilerParams(vmem_limit_bytes=20 << 20)


def dot(left, right, dims=((1,), (0,))):
    return lax.dot_general(left, right, (dims, ((), ())), preferred_element_type=F32)


def halves(value):
    high = value.astype(BF16)
    return high, (value - high.astype(F32)).astype(BF16)


def thirds(value):
    high = value.astype(BF16)
    rest = value - high.astype(F32)
    mid = rest.astype(BF16)
    return high.astype(F32), mid.astype(F32), (rest - mid.astype(F32))


def prep_kernel(
    slots, charges, axes, basis, trans, rest, qt, fa, fb, outgoing, rows_a, rows_b, node, sems
):
    clusters = charges.shape[0]
    conductors = charges.shape[2]
    total = jnp.zeros((trans.shape[1], conductors), F32)
    for i in range(clusters):
        leaf = dot(basis[i], charges[i]).astype(BF16)
        total += dot(trans[i], leaf)
    top = total.astype(BF16)
    node[:16, :conductors] = top[:16]
    node[:16, conductors:] = top[16:]
    node[16:, :conductors] = rest[:16]
    node[16:, conductors:] = rest[16:]
    x = [axes[d] for d in range(3)]
    norm = x[0] * x[0] + x[1] * x[1] + x[2] * x[2]
    one = jnp.ones_like(norm)
    rows_a[...] = jnp.zeros_like(rows_a)
    rows_b[...] = jnp.zeros_like(rows_b)
    for d, row in enumerate((*x, *thirds(norm + DELTA * DELTA), one, one, one)):
        rows_a[:, d, :] = row
    for d, row in enumerate((*(-2.0 * a for a in x), one, one, one, *thirds(norm))):
        rows_b[:, d, :] = row
    for c in range(clusters):
        fb[c] = rows_b[c].astype(BF16)
        qt[c] = charges[c].T
    split = qt.shape[1]

    def copies(h):
        c = slots[h, 0]
        return (
            pltpu.make_async_copy(qt.at[c], outgoing.at[h, pl.ds(0, split)], sems.at[h, 0]),
            pltpu.make_async_copy(fb.at[c], outgoing.at[h, pl.ds(split, FEAT)], sems.at[h, 1]),
            pltpu.make_async_copy(node, outgoing.at[h, pl.ds(split + FEAT, 32)], sems.at[h, 2]),
        )

    def send(h, carry):
        for copy in copies(h):
            copy.start()
        return carry

    def wait(h, carry):
        for copy in copies(h):
            copy.wait()
        return carry

    lax.fori_loop(0, outgoing.shape[0], send, 0)
    for c in range(clusters):
        fa[c] = rows_a[c].T.astype(BF16)
    lax.fori_loop(0, outgoing.shape[0], wait, 0)


def prep(slots, charges, axes, basis, trans, rest):
    clusters, width, conductors = charges.shape
    peers = slots.shape[0]
    return pl.pallas_call(
        prep_kernel,
        out_shape=(
            jax.ShapeDtypeStruct((clusters, conductors, width), BF16),
            jax.ShapeDtypeStruct((clusters, width, FEAT), BF16),
            jax.ShapeDtypeStruct((clusters, FEAT, width), BF16),
            jax.ShapeDtypeStruct((peers, conductors + FEAT + 32, width), BF16),
        ),
        in_specs=[SMEM] + [VMEM] * 5,
        out_specs=(VMEM, VMEM, VMEM, pl.BlockSpec(memory_space=pl.ANY)),
        scratch_shapes=[pltpu.VMEM((clusters, FEAT, width), F32)] * 2
        + [pltpu.VMEM((32, width), BF16), pltpu.SemaphoreType.DMA((peers, 3))],
        compiler_params=PARAMS,
        name="prep",
    )(slots, charges, axes, basis, trans, rest)


def tiles(count, table, weight, fa, feat, left, right, add_first, add_second, kbuf):
    def tile(j):
        key = table[j]
        s = dot(fa[lax.rem(key, 16)], feat(key // 16))
        return lax.rsqrt(s.astype(BF16)) * weight[j].astype(BF16)

    for g in range(GROUP):
        kbuf[0, g] = tile(g)

    def body(i, carry):
        now = lax.rem(i, 2)
        for g in range(GROUP):
            j = i * GROUP + g
            key = table[j]
            a, b = lax.rem(key, 16), key // 16
            k = kbuf[now, g]
            add_first(a, dot(right(b), k, ((1,), (1,))))
            add_second(b, dot(left(a), k))
            kbuf[1 - now, g] = tile(j + GROUP)
        return carry

    lax.fori_loop(0, pl.cdiv(count, GROUP), body, 0)


def own_kernel(count, table, weight, qt, fa, fb, acc, kbuf):
    acc[...] = jnp.zeros_like(acc)

    def add(i, value):
        acc[i] += value

    tiles(count[0], table, weight, fa, lambda b: fb[b], lambda a: qt[a], lambda b: qt[b], add, add, kbuf)


def own_near(count, table, weight, qt, fa, fb):
    width = qt.shape[2]
    return pl.pallas_call(
        own_kernel,
        out_shape=jax.ShapeDtypeStruct(qt.shape, F32),
        in_specs=[SMEM] * 3 + [VMEM] * 3,
        out_specs=VMEM,
        scratch_shapes=[pltpu.VMEM((2, GROUP, width, width), BF16)],
        compiler_params=PARAMS,
        cost_estimate=pl.CostEstimate(flops=6 << 30, bytes_accessed=4 << 20, transcendentals=0),
        name="own_near",
    )(count, table, weight, qt, fa, fb)


def reply_kernel(count, table, weight, qt, fa, incoming, back, kbuf):
    conductors, width = qt.shape[1:]
    back[...] = jnp.zeros_like(back)

    def tile(j):
        key = table[j]
        s = dot(fa[lax.rem(key, 16)], incoming[key // 16, conductors : conductors + FEAT, :])
        return lax.rsqrt(s.astype(BF16)) * weight[j].astype(BF16)

    for g in range(GROUP):
        kbuf[0, g] = tile(g)

    def body(i, total):
        now = lax.rem(i, 2)
        for g in range(GROUP):
            j = i * GROUP + g
            before = table[jnp.maximum(j - 1, 0)] // 16
            key = table[j]
            a, b = lax.rem(key, 16), key // 16
            keep = jnp.where(before == b, 1.0, 0.0).astype(F32)
            total = total * keep + dot(qt[a], kbuf[now, g])
            back[b] = total.astype(BF16)
            kbuf[1 - now, g] = tile(j + GROUP)
        return total

    lax.fori_loop(0, pl.cdiv(count[0], GROUP), body, jnp.zeros((conductors, width), F32))


def reply(count, table, weight, qt, fa, incoming):
    peers = incoming.shape[0]
    _, conductors, width = qt.shape
    return pl.pallas_call(
        reply_kernel,
        out_shape=jax.ShapeDtypeStruct((peers, conductors, width), BF16),
        in_specs=[SMEM] * 3 + [VMEM] * 3,
        out_specs=VMEM,
        scratch_shapes=[pltpu.VMEM((2, GROUP, width, width), BF16)],
        compiler_params=PARAMS,
        cost_estimate=pl.CostEstimate(flops=6 << 30, bytes_accessed=8 << 20, transcendentals=0),
        name="reply",
    )(count, table, weight, qt, fa, incoming)


def remote_kernel(count, table, weight, fa, incoming, acc_in, acc, kbuf):
    conductors = acc.shape[1]
    acc[...] = acc_in[...]

    def tile(j):
        key = table[j]
        s = dot(fa[lax.rem(key, 16)], incoming[key // 16, conductors : conductors + FEAT, :])
        return lax.rsqrt(s.astype(BF16)) * weight[j].astype(BF16)

    for g in range(GROUP):
        kbuf[0, g] = tile(g)

    def body(i, carry):
        now = lax.rem(i, 2)
        for g in range(GROUP):
            j = i * GROUP + g
            key = table[j]
            a, b = lax.rem(key, 16), key // 16
            acc[a] += dot(incoming[b, :conductors, :], kbuf[now, g], ((1,), (1,)))
            kbuf[1 - now, g] = tile(j + GROUP)
        return carry

    lax.fori_loop(0, pl.cdiv(count[0], GROUP), body, 0)


def remote_near(count, table, weight, fa, incoming, acc):
    width = acc.shape[2]
    return pl.pallas_call(
        remote_kernel,
        out_shape=jax.ShapeDtypeStruct(acc.shape, F32),
        in_specs=[SMEM] * 3 + [VMEM] * 3,
        out_specs=VMEM,
        scratch_shapes=[pltpu.VMEM((2, GROUP, width, width), BF16)],
        compiler_params=PARAMS,
        cost_estimate=pl.CostEstimate(flops=6 << 30, bytes_accessed=8 << 20, transcendentals=0),
        name="remote_near",
    )(count, table, weight, fa, incoming, acc)


def far_kernel(ids, own_points, nodes, trans, leaf, sources):
    rank = 32

    def skel(n):
        rows = nodes[n, :16, :]
        return jnp.concatenate([rows[:, :128], rows[:, 128:]], axis=0)

    def transfer(n, which):
        rows = nodes[n, 16:, :128]
        lo = 64 * which
        return jnp.concatenate([rows[:, lo : lo + 32], rows[:, lo + 32 : lo + 64]], axis=0)

    def points(n):
        return nodes[n, 16:, 128:].astype(F32)[:1]

    def kernel_tile(mine, theirs):
        gap = mine - theirs
        sq = gap * gap
        s = ((DELTA * DELTA + sq[:, :32]) + sq[:, 32:64]) + sq[:, 64:96]
        return halves(KCOEF * lax.rsqrt(s))

    def apply(tile, source):
        return dot(tile[0], source) + dot(tile[1], source)

    mine = [own_points[level] for level in range(3)]
    zero = jnp.zeros((rank, 128), F32)

    def one(f, total):
        n = ids[f]
        return total + apply(kernel_tile(mine[0], points(n)), skel(n))

    def two(f, total):
        n, m = ids[8 + f], lax.rem(ids[8 + f] + 64, 128)
        source = dot(transfer(n, 0), skel(n)) + dot(transfer(m, 0), skel(m))
        theirs = 0.5 * (points(n) + points(m))
        return total + apply(kernel_tile(mine[1], theirs), source.astype(BF16))

    def three(f, total):
        n = [lax.rem(ids[24 + f] + step, 128) for step in (0, 64, 1, 65)]
        terms = [dot(transfer(i, 1), skel(i)) for i in n]
        source = (terms[0] + terms[1]) + (terms[2] + terms[3])
        left = 0.5 * (points(n[0]) + points(n[1]))
        right = 0.5 * (points(n[2]) + points(n[3]))
        return total + apply(kernel_tile(mine[2], 0.5 * (left + right)), source.astype(BF16))

    far_one = lax.fori_loop(0, 8, one, zero, unroll=True)
    far_two = lax.fori_loop(0, 16, two, zero, unroll=4)
    far_three = lax.fori_loop(0, 32, three, zero, unroll=4)
    me = ids[56]

    def down_by(which, value):
        high, low = halves(value)
        mat = transfer(me, which)
        return dot(mat, high, ((0,), (0,))) + dot(mat, low, ((0,), (0,)))

    down = far_one + down_by(0, far_two) + down_by(1, far_three)
    high, low = halves(down.T)
    for c in range(trans.shape[0]):
        leaf[c] = (dot(high, trans[c]) + dot(low, trans[c])).astype(BF16)


def far_field(ids, own_points, nodes, trans):
    clusters, rank, _ = trans.shape
    return pl.pallas_call(
        far_kernel,
        out_shape=jax.ShapeDtypeStruct((clusters, 128, rank), BF16),
        in_specs=[SMEM] + [VMEM] * 3,
        out_specs=VMEM,
        scratch_shapes=[pltpu.VMEM((8, 128), F32)],
        compiler_params=PARAMS,
        cost_estimate=pl.CostEstimate(flops=6 << 30, bytes_accessed=4 << 20, transcendentals=0),
        name="far_field",
    )(ids, own_points, nodes, trans)


def base_kernel(acc, leaf, basis, base):
    def one(c, carry):
        base[c] = acc[c] * KCOEF + dot(leaf[c], basis[c])
        return carry

    lax.fori_loop(0, acc.shape[0], one, 0)


def base_sum(acc, leaf, basis):
    return pl.pallas_call(
        base_kernel,
        out_shape=jax.ShapeDtypeStruct(acc.shape, F32),
        in_specs=[VMEM] * 3,
        out_specs=VMEM,
        compiler_params=PARAMS,
        cost_estimate=pl.CostEstimate(flops=2 << 30, bytes_accessed=4 << 20, transcendentals=0),
        name="base_sum",
    )(acc, leaf, basis)


def final_kernel(order, starts, base, returned, out, rows, sems):
    clusters = base.shape[0]

    def copy(c):
        return pltpu.make_async_copy(rows.at[c], out.at[c], sems.at[c])

    for c in range(clusters):

        def collect(i, total):
            return total + returned[order[i]].astype(F32)

        zero = jnp.zeros(base.shape[1:], F32)
        total = lax.fori_loop(starts[c], starts[c + 1], collect, zero)
        rows[c] = (base[c] + KCOEF * total).T
        copy(c).start()
    for c in range(clusters):
        copy(c).wait()


def finish(order, starts, base, returned):
    clusters, conductors, width = base.shape
    return pl.pallas_call(
        final_kernel,
        out_shape=jax.ShapeDtypeStruct((clusters, width, conductors), F32),
        in_specs=[SMEM] * 2 + [VMEM] * 2,
        out_specs=pl.BlockSpec(memory_space=pl.ANY),
        scratch_shapes=[
            pltpu.VMEM((clusters, width, conductors), F32),
            pltpu.SemaphoreType.DMA((clusters,)),
        ],
        compiler_params=PARAMS,
        name="finish",
    )(order, starts, base, returned)


def pair_lists(first, second, count, clusters, entries):
    live = jnp.arange(first.shape[0], dtype=jnp.int32) < count
    own = second < clusters
    a = jnp.where(own, jnp.minimum(first, second), first)
    b = jnp.where(own, jnp.maximum(first, second), second)
    key = jnp.where(live, b * clusters + a, -1)
    keys = jnp.arange(entries * clusters, dtype=jnp.int32)
    times = jnp.sum((keys[:, None] == key[None, :]).astype(F32), axis=1)
    times = jnp.where(keys % clusters == keys // clusters, 0.5 * times, times)
    lists = []
    for lo, hi in ((0, clusters * clusters), (clusters * clusters, entries * clusters)):
        part = times[lo:hi]
        held = part > 0
        spots = jnp.arange(hi - lo, dtype=jnp.int32)
        rank = jnp.sum(((spots[None, :] < spots[:, None]) & held[None, :]).astype(jnp.int32), axis=1)
        slots = jnp.arange(256 + 2 * GROUP, dtype=jnp.int32)
        match = (rank[None, :] == slots[:, None]) & held[None, :]
        total = jnp.sum(held.astype(jnp.int32))
        last = jnp.max(jnp.where(held, spots, 0))
        table = jnp.sum(jnp.where(match, spots[None, :], 0), axis=1)
        table = jnp.where(slots < total, table, last)
        weight = jnp.sum(jnp.where(match, part[None, :], 0.0), axis=1)
        lists.append((total.reshape(1), table, weight))
    return lists


def shards(
    charges,
    panel_coords,
    cluster_basis,
    trans_leaf,
    trans_pair,
    trans_quad,
    skel_points,
    send_slots,
    pair_first,
    pair_second,
    pair_count,
    far_one,
    far_two,
    far_three,
):
    clusters, _, width = panel_coords.shape
    conductors = charges.shape[1]
    peers = lax.axis_size("dev")
    blocks = charges.reshape(clusters, width, conductors)
    axes = jnp.swapaxes(panel_coords, 0, 1).astype(F32)

    def folded(mat):
        return jnp.concatenate([mat[0, :16], mat[0, 16:]], axis=1)

    def padded(row):
        return jnp.pad(row, ((0, 0), (0, conductors - row.shape[1])))

    rest = jnp.concatenate(
        [
            jnp.concatenate([folded(trans_pair), folded(trans_quad)], axis=1),
            padded(skel_points.reshape(1, -1)),
            padded(jnp.concatenate([far_two, far_three], axis=1).astype(BF16)),
            jnp.zeros((14, conductors), BF16),
        ],
        axis=0,
    )
    qt, fa, fb, outgoing = prep(send_slots, blocks, axes, cluster_basis, trans_leaf, rest)
    incoming = lax.all_to_all(outgoing, "dev", split_axis=0, concat_axis=0, tiled=True)

    z, d = lax.axis_index("group"), lax.axis_index("dev")
    xy, c = d // 2, d % 2
    same = incoming.reshape(peers // 2, 2, -1, width)[:, :, conductors + FEAT :]
    same = lax.dynamic_index_in_dim(same, c, axis=1, keepdims=False)
    along = [same]
    for step in (1, 2, 3):
        along.append(lax.ppermute(same, "group", [(i, (i + step) % 4) for i in range(4)]))
    along = jnp.stack(along)
    other = lax.ppermute(along, "dev", [(i, i ^ 1) for i in range(32)])
    nodes = jnp.stack([along, other]).reshape(128, 32, width)

    own_list, remote_list = pair_lists(pair_first, pair_second, pair_count[0], clusters, clusters + peers)
    acc = own_near(*own_list, qt, fa, fb)
    back = reply(*remote_list, qt, fa, incoming)
    returned = lax.all_to_all(back, "dev", split_axis=0, concat_axis=0, tiled=True)
    acc = remote_near(*remote_list, fa, incoming, acc)

    def place(owner):
        step = (z - owner // peers) % 4
        return ((c ^ owner % 2) * 4 + step) * 16 + owner % peers // 2

    quad = lax.dynamic_slice_in_dim(incoming[:, 160:162, 128:], d // 4 * 4, 4, axis=0)
    quad_lists = quad[:, 1, :16].astype(jnp.int32)
    pair_list = lax.dynamic_slice_in_dim(quad_lists[:, :8], d % 4 // 2 * 2, 2, axis=0)
    ids = jnp.concatenate(
        [
            place(far_one[0]),
            place(2 * pair_list.reshape(-1)),
            place(4 * quad_lists[:, 8:].reshape(-1)),
            xy.reshape(1),
        ]
    )
    quad_points = quad[:, 0, :96].astype(F32).reshape(4, 3, 32)
    pair_points = 0.5 * (quad_points[0::2] + quad_points[1::2])
    own_points = jnp.stack(
        [
            skel_points[0].astype(F32),
            lax.dynamic_index_in_dim(pair_points, d % 4 // 2, axis=0, keepdims=False),
            0.5 * (pair_points[0] + pair_points[1]),
        ]
    )
    own_points = jnp.repeat(jnp.swapaxes(own_points, 1, 2), 32, axis=2)
    own_points = jnp.pad(own_points, ((0, 0), (0, 0), (0, 32)))
    leaf = far_field(ids, own_points, nodes, trans_leaf)
    base = base_sum(acc, leaf, cluster_basis)

    slots = send_slots[:, 0]
    spots = jnp.arange(peers, dtype=jnp.int32)
    rank = jnp.sum(
        (slots[None, :] < slots[:, None])
        | ((slots[None, :] == slots[:, None]) & (spots[None, :] < spots[:, None])),
        axis=1,
        dtype=jnp.int32,
    )
    order = jnp.sum(jnp.where(rank[None, :] == spots[:, None], spots[None, :], 0), axis=1)
    edges = jnp.arange(clusters + 1, dtype=jnp.int32)
    starts = jnp.sum(slots[None, :] < edges[:, None], axis=1, dtype=jnp.int32)
    out = finish(order, starts, base, returned)
    return out.reshape(clusters * width, conductors)


def solution(mesh):
    owners = ("group", "dev")
    rows, block, flat = P(owners, None), P(owners, None, None), P(owners)
    placed = (rows, *(block,) * 6, rows, *(flat,) * 3, *(rows,) * 3)
    return jax.shard_map(shards, mesh=mesh, in_specs=placed, out_specs=rows, check_vma=False)
```

```python
import functools

import jax
import jax.numpy as jnp
from jax import lax
from jax.experimental import pallas as pl
from jax.experimental.pallas import tpu as pltpu
from jax.sharding import PartitionSpec as P

KCOEF = 0.005
DELTA = 0.02
F32 = jnp.float32
BF16 = jnp.bfloat16
GROUP = 8
FEAT = 16
VMEM = pl.BlockSpec(memory_space=pltpu.VMEM)
SMEM = pl.BlockSpec(memory_space=pltpu.SMEM)
MESH = pl.DeviceIdType.MESH
PARAMS = pltpu.CompilerParams(vmem_limit_bytes=14 << 20)
WIDE = pltpu.CompilerParams(vmem_limit_bytes=56 << 20)


def dot(left, right, dims=((1,), (0,))):
    return lax.dot_general(left, right, (dims, ((), ())), preferred_element_type=F32)


def halves(value):
    high = value.astype(BF16)
    return high, (value - high.astype(F32)).astype(BF16)


def thirds(value):
    high = value.astype(BF16)
    rest = value - high.astype(F32)
    mid = rest.astype(BF16)
    return high.astype(F32), mid.astype(F32), (rest - mid.astype(F32))


def prep_kernel(ints, charges, axes, basis, trans, pair, quad, stage, fa, outgoing, rows_a, rows_b, sems):
    clusters, _, rhs = charges.shape
    width = stage.shape[2]
    peers = outgoing.shape[0]
    total = jnp.zeros((trans.shape[1], rhs), F32)
    for i in range(clusters):
        leaf = dot(basis[i], charges[i]).astype(BF16)
        total += dot(trans[i], leaf)
    top = total.astype(BF16)
    top = jnp.concatenate([top[:16], top[16:]], axis=1)
    mats = [mat[0].astype(F32) for mat in (pair, quad)]
    moves = jnp.concatenate([mat[8 * i : 8 * i + 8] for mat in mats for i in range(4)], axis=1).astype(BF16)

    x = [axes[d, :clusters] for d in range(3)]
    norm = x[0] * x[0] + x[1] * x[1] + x[2] * x[2]
    one = jnp.ones_like(norm)
    rows_a[...] = jnp.zeros_like(rows_a)
    rows_b[...] = jnp.zeros_like(rows_b)
    for d, row in enumerate((*x, *thirds(norm + DELTA * DELTA), one, one, one)):
        rows_a[:, d, :] = row
    lane = lax.broadcasted_iota(jnp.int32, (1, width), 1)
    info = axes[0, clusters : clusters + 1]
    for i in range(16):
        info = jnp.where(lane == rhs + i, ints[peers + i].astype(F32), info)
    info = jnp.broadcast_to(info, norm.shape)
    for d, row in enumerate((*(-2.0 * a for a in x), one, one, one, *thirds(norm), info)):
        rows_b[:, d, :] = row
    for c in range(clusters):
        stage[c, :rhs] = charges[c].T
        stage[c, rhs : rhs + FEAT] = rows_b[c].astype(BF16)
        stage[c, rhs + FEAT : rhs + FEAT + 16] = top
        stage[c, rhs + FEAT + 16 :] = moves

    def copy(h):
        return pltpu.make_async_copy(stage.at[ints[h]], outgoing.at[h], sems.at[h])

    def send(h, carry):
        copy(h).start()
        return carry

    def wait(h, carry):
        copy(h).wait()
        return carry

    lax.fori_loop(0, peers, send, 0)
    for c in range(clusters):
        fa[c] = rows_a[c].T.astype(BF16)
    lax.fori_loop(0, peers, wait, 0)


def prep(ints, charges, axes, basis, trans, pair, quad, peers):
    clusters, width, rhs = charges.shape
    rows = rhs + FEAT + 24
    return pl.pallas_call(
        prep_kernel,
        out_shape=(
            jax.ShapeDtypeStruct((clusters, rows, width), BF16),
            jax.ShapeDtypeStruct((clusters, width, FEAT), BF16),
            jax.ShapeDtypeStruct((peers, rows, width), BF16),
        ),
        in_specs=[SMEM] + [VMEM] * 6,
        out_specs=(VMEM, VMEM, pl.BlockSpec(memory_space=pl.ANY)),
        scratch_shapes=[pltpu.VMEM((clusters, FEAT, width), F32)] * 2
        + [pltpu.SemaphoreType.DMA((peers,))],
        compiler_params=WIDE,
        name="prep",
    )(ints, charges, axes, basis, trans, pair, quad)


def unpack(code):
    return code & 15, (code >> 4) & 63, (code >> 10).astype(F32) * 0.5


def tile(code, fa, table):
    a, b, times = unpack(code)
    s = dot(fa[a], table[b, table.shape[1] - 24 - FEAT : table.shape[1] - 24])
    return lax.rsqrt(s.astype(BF16)) * times.astype(BF16)


def own_kernel(pairs, stage, fa, acc, kbuf):
    rhs = acc.shape[1]
    acc[...] = jnp.zeros_like(acc)
    for g in range(GROUP):
        kbuf[0, g] = tile(pairs[1 + g], fa, stage)

    def body(i, carry):
        now = lax.rem(i, 2)
        for g in range(GROUP):
            j = 1 + i * GROUP + g
            a, b, _ = unpack(pairs[j])
            k = kbuf[now, g]
            acc[a] += dot(stage[b, :rhs], k, ((1,), (1,)))
            acc[b] += dot(stage[a, :rhs], k)
            kbuf[1 - now, g] = tile(pairs[j + GROUP], fa, stage)
        return carry

    lax.fori_loop(0, pl.cdiv(pairs[0], GROUP), body, 0)


def own_near(pairs, stage, fa):
    clusters, rows, width = stage.shape
    return pl.pallas_call(
        own_kernel,
        out_shape=jax.ShapeDtypeStruct((clusters, rows - 24 - FEAT, width), F32),
        in_specs=[SMEM] + [VMEM] * 2,
        out_specs=VMEM,
        scratch_shapes=[pltpu.VMEM((2, GROUP, width, width), BF16)],
        compiler_params=PARAMS,
        cost_estimate=pl.CostEstimate(flops=6 << 30, bytes_accessed=4 << 20, transcendentals=0),
        name="own_near",
    )(pairs, stage, fa)


def reply_kernel(pairs, stage, fa, incoming, back, kbuf):
    rhs, width = back.shape[1:]
    back[...] = jnp.zeros_like(back)
    for g in range(GROUP):
        kbuf[0, g] = tile(pairs[1 + g], fa, incoming)

    def body(i, total):
        now = lax.rem(i, 2)
        for g in range(GROUP):
            j = 1 + i * GROUP + g
            a, b, _ = unpack(pairs[j])
            before = unpack(pairs[jnp.maximum(j - 1, 1)])[1]
            keep = jnp.where(before == b, 1.0, 0.0).astype(F32)
            total = total * keep + dot(stage[a, :rhs], kbuf[now, g])
            back[b] = total.astype(BF16)
            kbuf[1 - now, g] = tile(pairs[j + GROUP], fa, incoming)
        return total

    lax.fori_loop(0, pl.cdiv(pairs[0], GROUP), body, jnp.zeros((rhs, width), F32))


def reply(pairs, stage, fa, incoming):
    peers, rows, width = incoming.shape
    return pl.pallas_call(
        reply_kernel,
        out_shape=jax.ShapeDtypeStruct((peers, rows - 24 - FEAT, width), BF16),
        in_specs=[SMEM] + [VMEM] * 3,
        out_specs=VMEM,
        scratch_shapes=[pltpu.VMEM((2, GROUP, width, width), BF16)],
        compiler_params=PARAMS,
        cost_estimate=pl.CostEstimate(flops=6 << 30, bytes_accessed=8 << 20, transcendentals=0),
        name="reply",
    )(pairs, stage, fa, incoming)


def remote_kernel(pairs, fa, incoming, acc_in, acc, kbuf):
    rhs = acc.shape[1]
    acc[...] = acc_in[...]
    for g in range(GROUP):
        kbuf[0, g] = tile(pairs[1 + g], fa, incoming)

    def body(i, carry):
        now = lax.rem(i, 2)
        for g in range(GROUP):
            j = 1 + i * GROUP + g
            a, b, _ = unpack(pairs[j])
            acc[a] += dot(incoming[b, :rhs], kbuf[now, g], ((1,), (1,)))
            kbuf[1 - now, g] = tile(pairs[j + GROUP], fa, incoming)
        return carry

    lax.fori_loop(0, pl.cdiv(pairs[0], GROUP), body, 0)


def remote_near(pairs, fa, incoming, acc):
    width = acc.shape[2]
    return pl.pallas_call(
        remote_kernel,
        out_shape=jax.ShapeDtypeStruct(acc.shape, F32),
        in_specs=[SMEM] + [VMEM] * 3,
        out_specs=VMEM,
        scratch_shapes=[pltpu.VMEM((2, GROUP, width, width), BF16)],
        compiler_params=PARAMS,
        cost_estimate=pl.CostEstimate(flops=6 << 30, bytes_accessed=8 << 20, transcendentals=0),
        name="remote_near",
    )(pairs, fa, incoming, acc)


def far_kernel(ids, own_points, nodes, trans, leaf, sources):
    rank = 32

    def skel(n):
        rows = nodes[n, 16:32, :]
        return jnp.concatenate([rows[:, :128], rows[:, 128:]], axis=0)

    def transfer(n, which):
        rows = nodes[n, 32:, 128 * which : 128 * which + 128].astype(F32)
        return jnp.concatenate([rows[:, 32 * i : 32 * i + 32] for i in range(4)], axis=0).astype(BF16)

    def points(n):
        return nodes[n, :16, :128].astype(F32)[9:10]

    def kernel_tile(mine, theirs):
        gap = mine - theirs
        sq = gap * gap
        s = ((DELTA * DELTA + sq[:, :32]) + sq[:, 32:64]) + sq[:, 64:96]
        return halves(KCOEF * lax.rsqrt(s))

    def apply(tile, source):
        return dot(tile[0], source) + dot(tile[1], source)

    mine = [own_points[level] for level in range(3)]
    zero = jnp.zeros((rank, 128), F32)

    def one(f, total):
        n = ids[f]
        return total + apply(kernel_tile(mine[0], points(n)), skel(n))

    def two(f, total):
        n, m = ids[8 + f], lax.rem(ids[8 + f] + 64, 128)
        source = dot(transfer(n, 0), skel(n)) + dot(transfer(m, 0), skel(m))
        theirs = 0.5 * (points(n) + points(m))
        return total + apply(kernel_tile(mine[1], theirs), source.astype(BF16))

    def three(f, total):
        n = [lax.rem(ids[24 + f] + step, 128) for step in (0, 64, 1, 65)]
        terms = [dot(transfer(i, 1), skel(i)) for i in n]
        source = (terms[0] + terms[1]) + (terms[2] + terms[3])
        left = 0.5 * (points(n[0]) + points(n[1]))
        right = 0.5 * (points(n[2]) + points(n[3]))
        return total + apply(kernel_tile(mine[2], 0.5 * (left + right)), source.astype(BF16))

    far_one = lax.fori_loop(0, 8, one, zero, unroll=True)
    far_two = lax.fori_loop(0, 16, two, zero, unroll=4)
    far_three = lax.fori_loop(0, 32, three, zero, unroll=4)
    me = ids[56]

    def down_by(which, value):
        high, low = halves(value)
        mat = transfer(me, which)
        return dot(mat, high, ((0,), (0,))) + dot(mat, low, ((0,), (0,)))

    down = far_one + down_by(0, far_two) + down_by(1, far_three)
    high, low = halves(down.T)
    for c in range(trans.shape[0]):
        leaf[c] = (dot(high, trans[c]) + dot(low, trans[c])).astype(BF16)


def far_field(ids, own_points, nodes, trans):
    clusters, rank, _ = trans.shape
    return pl.pallas_call(
        far_kernel,
        out_shape=jax.ShapeDtypeStruct((clusters, 128, rank), BF16),
        in_specs=[SMEM] + [VMEM] * 3,
        out_specs=VMEM,
        scratch_shapes=[pltpu.VMEM((8, 128), F32)],
        compiler_params=PARAMS,
        cost_estimate=pl.CostEstimate(flops=6 << 30, bytes_accessed=4 << 20, transcendentals=0),
        name="far_field",
    )(ids, own_points, nodes, trans)


def base_kernel(acc, leaf, basis, base):
    def one(c, carry):
        base[c] = acc[c] * KCOEF + dot(leaf[c], basis[c])
        return carry

    lax.fori_loop(0, acc.shape[0], one, 0)


def base_sum(acc, leaf, basis):
    return pl.pallas_call(
        base_kernel,
        out_shape=jax.ShapeDtypeStruct(acc.shape, F32),
        in_specs=[VMEM] * 3,
        out_specs=VMEM,
        compiler_params=PARAMS,
        cost_estimate=pl.CostEstimate(flops=2 << 30, bytes_accessed=4 << 20, transcendentals=0),
        name="base_sum",
    )(acc, leaf, basis)


def final_kernel(order, starts, base, returned, out, rows, sems):
    clusters = base.shape[0]

    def copy(c):
        return pltpu.make_async_copy(rows.at[c], out.at[c], sems.at[c])

    for c in range(clusters):

        def collect(i, total):
            return total + returned[order[i]].astype(F32)

        zero = jnp.zeros(base.shape[1:], F32)
        total = lax.fori_loop(starts[c], starts[c + 1], collect, zero)
        rows[c] = (base[c] + KCOEF * total).T
        copy(c).start()
    for c in range(clusters):
        copy(c).wait()


def finish(order, starts, base, returned):
    clusters, conductors, width = base.shape
    return pl.pallas_call(
        final_kernel,
        out_shape=jax.ShapeDtypeStruct((clusters, width, conductors), F32),
        in_specs=[SMEM] * 2 + [VMEM] * 2,
        out_specs=pl.BlockSpec(memory_space=pl.ANY),
        scratch_shapes=[
            pltpu.VMEM((clusters, width, conductors), F32),
            pltpu.SemaphoreType.DMA((clusters,)),
        ],
        compiler_params=PARAMS,
        name="finish",
    )(order, starts, base, returned)


def pair_lists(first, second, count, clusters, entries):
    live = jnp.arange(first.shape[0], dtype=jnp.int32) < count
    own = second < clusters
    a = jnp.where(own, jnp.minimum(first, second), first)
    b = jnp.where(own, jnp.maximum(first, second), second)
    key = jnp.where(live, b * clusters + a, -1)
    keys = jnp.arange(entries * clusters, dtype=jnp.int32)
    times = jnp.sum((keys[:, None] == key[None, :]).astype(jnp.int32), axis=1)
    times = jnp.where(keys % clusters == keys // clusters, times, 2 * times)
    lists = []
    for lo, hi in ((0, clusters * clusters), (clusters * clusters, entries * clusters)):
        part = times[lo:hi]
        held = part > 0
        spots = jnp.arange(hi - lo, dtype=jnp.int32)
        rank = jnp.sum(((spots[None, :] < spots[:, None]) & held[None, :]).astype(jnp.int32), axis=1)
        slots = jnp.arange(256 + 2 * GROUP, dtype=jnp.int32)
        match = (rank[None, :] == slots[:, None]) & held[None, :]
        total = jnp.sum(held.astype(jnp.int32))
        last = jnp.max(jnp.where(held, spots, 0))
        code = jnp.sum(jnp.where(match, (spots + 1024 * part)[None, :], 0), axis=1)
        code = jnp.where(slots < total, code, last)
        lists.append(jnp.concatenate([total.reshape(1), code]))
    return lists


def shards(
    charges,
    panel_coords,
    cluster_basis,
    trans_leaf,
    trans_pair,
    trans_quad,
    skel_points,
    send_slots,
    pair_first,
    pair_second,
    pair_count,
    far_one,
    far_two,
    far_three,
):
    clusters, _, width = panel_coords.shape
    conductors = charges.shape[1]
    peers = lax.axis_size("dev")
    blocks = charges.reshape(clusters, width, conductors)
    points = jnp.pad(skel_points.reshape(1, 1, -1), ((0, 2), (0, 0), (0, width - skel_points.size)))
    axes = jnp.concatenate([jnp.swapaxes(panel_coords, 0, 1), points], axis=1).astype(F32)
    slots = send_slots[:, 0]
    ints = jnp.concatenate([slots, far_two[0], far_three[0]])
    stage, fa, outgoing = prep(
        ints, blocks, axes, cluster_basis, trans_leaf, trans_pair, trans_quad, peers
    )
    incoming = lax.all_to_all(outgoing, "dev", split_axis=0, concat_axis=0, tiled=True)

    own_list, remote_list = pair_lists(pair_first, pair_second, pair_count[0], clusters, clusters + peers)
    acc = own_near(own_list, stage, fa)
    back = reply(remote_list, stage, fa, incoming)
    returned = lax.all_to_all(back, "dev", split_axis=0, concat_axis=0, tiled=True)
    acc = remote_near(remote_list, fa, incoming, acc)

    z, d = lax.axis_index("group"), lax.axis_index("dev")
    xy, c = d // 2, d % 2
    nodes, _ = lax.optimization_barrier((incoming, back))
    same = nodes.reshape(peers // 2, 2, -1, width)[:, :, conductors:]
    same = lax.dynamic_index_in_dim(same, c, axis=1, keepdims=False)
    along = [same]
    for step in (1, 2, 3):
        along.append(lax.ppermute(same, "group", [(i, (i + step) % 4) for i in range(4)]))
    along = jnp.stack(along)
    other = lax.ppermute(along, "dev", [(i, i ^ 1) for i in range(32)])
    nodes = jnp.stack([along, other]).reshape(128, 40, width)

    def place(owner):
        step = (z - owner // peers) % 4
        return ((c ^ owner % 2) * 4 + step) * 16 + owner % peers // 2

    quad = lax.dynamic_slice(incoming, (d // 4 * 4, conductors + 9, 0), (4, 1, width))[:, 0]
    quad_lists = quad[:, 128:144].astype(jnp.int32)
    pair_list = lax.dynamic_slice_in_dim(quad_lists[:, :8], d % 4 // 2 * 2, 2, axis=0)
    ids = jnp.concatenate(
        [
            place(far_one[0]),
            place(2 * pair_list.reshape(-1)),
            place(4 * quad_lists[:, 8:].reshape(-1)),
            xy.reshape(1),
        ]
    )
    quad_points = quad[:, :96].astype(F32).reshape(4, 3, 32)
    pair_points = 0.5 * (quad_points[0::2] + quad_points[1::2])
    own_points = jnp.stack(
        [
            skel_points[0].astype(F32),
            lax.dynamic_index_in_dim(pair_points, d % 4 // 2, axis=0, keepdims=False),
            0.5 * (pair_points[0] + pair_points[1]),
        ]
    )
    own_points = jnp.repeat(jnp.swapaxes(own_points, 1, 2), 32, axis=2)
    own_points = jnp.pad(own_points, ((0, 0), (0, 0), (0, 32)))
    leaf = far_field(ids, own_points, nodes, trans_leaf)
    base = base_sum(acc, leaf, cluster_basis)

    spots = jnp.arange(peers, dtype=jnp.int32)
    rank = jnp.sum(
        (slots[None, :] < slots[:, None])
        | ((slots[None, :] == slots[:, None]) & (spots[None, :] < spots[:, None])),
        axis=1,
        dtype=jnp.int32,
    )
    order = jnp.sum(jnp.where(rank[None, :] == spots[:, None], spots[None, :], 0), axis=1)
    edges = jnp.arange(clusters + 1, dtype=jnp.int32)
    starts = jnp.sum(slots[None, :] < edges[:, None], axis=1, dtype=jnp.int32)
    out = finish(order, starts, base, returned)
    return out.reshape(clusters * width, conductors)


def solution(mesh):
    owners = ("group", "dev")
    rows, block, flat = P(owners, None), P(owners, None, None), P(owners)
    placed = (rows, *(block,) * 6, rows, *(flat,) * 3, *(rows,) * 3)
    return jax.shard_map(shards, mesh=mesh, in_specs=placed, out_specs=rows, check_vma=False)
```

```python
import functools

import jax
import jax.numpy as jnp
from jax import lax
from jax.experimental import pallas as pl
from jax.experimental.pallas import tpu as pltpu
from jax.sharding import PartitionSpec as P

KCOEF = 0.005
DELTA = 0.02
F32 = jnp.float32
BF16 = jnp.bfloat16
GROUP = 8
FEAT = 16
VMEM = pl.BlockSpec(memory_space=pltpu.VMEM)
SMEM = pl.BlockSpec(memory_space=pltpu.SMEM)
MESH = pl.DeviceIdType.MESH
PARAMS = pltpu.CompilerParams(vmem_limit_bytes=14 << 20)
WIDE = pltpu.CompilerParams(vmem_limit_bytes=56 << 20)


def dot(left, right, dims=((1,), (0,))):
    return lax.dot_general(left, right, (dims, ((), ())), preferred_element_type=F32)


def halves(value):
    high = value.astype(BF16)
    return high, (value - high.astype(F32)).astype(BF16)


def thirds(value):
    high = value.astype(BF16)
    rest = value - high.astype(F32)
    mid = rest.astype(BF16)
    return high.astype(F32), mid.astype(F32), (rest - mid.astype(F32))


def prep_kernel(ints, charges, axes, basis, trans, pair, quad, stage, fa, outgoing, rows_a, rows_b, sems):
    clusters, _, rhs = charges.shape
    width = stage.shape[2]
    peers = outgoing.shape[0]
    total = jnp.zeros((trans.shape[1], rhs), F32)
    for i in range(clusters):
        leaf = dot(basis[i], charges[i]).astype(BF16)
        total += dot(trans[i], leaf)
    top = total.astype(BF16)
    top = jnp.concatenate([top[:16], top[16:]], axis=1)
    mats = [mat[0].astype(F32) for mat in (pair, quad)]
    moves = jnp.concatenate([mat[8 * i : 8 * i + 8] for mat in mats for i in range(4)], axis=1).astype(BF16)

    x = [axes[d, :clusters] for d in range(3)]
    norm = x[0] * x[0] + x[1] * x[1] + x[2] * x[2]
    one = jnp.ones_like(norm)
    rows_a[...] = jnp.zeros_like(rows_a)
    rows_b[...] = jnp.zeros_like(rows_b)
    for d, row in enumerate((*x, *thirds(norm + DELTA * DELTA), one, one, one)):
        rows_a[:, d, :] = row
    lane = lax.broadcasted_iota(jnp.int32, (1, width), 1)
    info = axes[0, clusters : clusters + 1]
    for i in range(16):
        info = jnp.where(lane == rhs + i, ints[peers + i].astype(F32), info)
    info = jnp.broadcast_to(info, norm.shape)
    for d, row in enumerate((*(-2.0 * a for a in x), one, one, one, *thirds(norm), info)):
        rows_b[:, d, :] = row
    for c in range(clusters):
        stage[c, :rhs] = charges[c].T
        stage[c, rhs : rhs + FEAT] = rows_b[c].astype(BF16)
        stage[c, rhs + FEAT : rhs + FEAT + 16] = top
        stage[c, rhs + FEAT + 16 :] = moves

    def copy(h):
        return pltpu.make_async_copy(stage.at[ints[h]], outgoing.at[h], sems.at[h])

    def send(h, carry):
        copy(h).start()
        return carry

    def wait(h, carry):
        copy(h).wait()
        return carry

    lax.fori_loop(0, peers, send, 0)
    for c in range(clusters):
        fa[c] = rows_a[c].T.astype(BF16)
    lax.fori_loop(0, peers, wait, 0)


def prep(ints, charges, axes, basis, trans, pair, quad, peers):
    clusters, width, rhs = charges.shape
    rows = rhs + FEAT + 24
    return pl.pallas_call(
        prep_kernel,
        out_shape=(
            jax.ShapeDtypeStruct((clusters, rows, width), BF16),
            jax.ShapeDtypeStruct((clusters, width, FEAT), BF16),
            jax.ShapeDtypeStruct((peers, rows, width), BF16),
        ),
        in_specs=[SMEM] + [VMEM] * 6,
        out_specs=(VMEM, VMEM, pl.BlockSpec(memory_space=pl.ANY)),
        scratch_shapes=[pltpu.VMEM((clusters, FEAT, width), F32)] * 2
        + [pltpu.SemaphoreType.DMA((peers,))],
        compiler_params=WIDE,
        name="prep",
    )(ints, charges, axes, basis, trans, pair, quad)


def unpack(code):
    return code & 15, (code >> 4) & 63, (code >> 10).astype(F32) * 0.5


def tile(code, fa, table):
    a, b, times = unpack(code)
    s = dot(fa[a], table[b, table.shape[1] - 24 - FEAT : table.shape[1] - 24])
    return lax.rsqrt(s.astype(BF16)) * times.astype(BF16)


def own_kernel(pairs, stage, fa, acc, kbuf):
    rhs = acc.shape[1]
    acc[...] = jnp.zeros_like(acc)
    for g in range(GROUP):
        kbuf[0, g] = tile(pairs[1 + g], fa, stage)

    def body(i, carry):
        now = lax.rem(i, 2)
        for g in range(GROUP):
            j = 1 + i * GROUP + g
            a, b, _ = unpack(pairs[j])
            k = kbuf[now, g]
            acc[a] += dot(stage[b, :rhs], k, ((1,), (1,)))
            acc[b] += dot(stage[a, :rhs], k)
            kbuf[1 - now, g] = tile(pairs[j + GROUP], fa, stage)
        return carry

    lax.fori_loop(0, pl.cdiv(pairs[0], GROUP), body, 0)


def own_near(pairs, stage, fa):
    clusters, rows, width = stage.shape
    return pl.pallas_call(
        own_kernel,
        out_shape=jax.ShapeDtypeStruct((clusters, rows - 24 - FEAT, width), F32),
        in_specs=[SMEM] + [VMEM] * 2,
        out_specs=VMEM,
        scratch_shapes=[pltpu.VMEM((2, GROUP, width, width), BF16)],
        compiler_params=PARAMS,
        cost_estimate=pl.CostEstimate(flops=6 << 30, bytes_accessed=4 << 20, transcendentals=0),
        name="own_near",
    )(pairs, stage, fa)


def reply_kernel(pairs, stage, fa, incoming, back, kbuf):
    rhs, width = back.shape[1:]
    back[...] = jnp.zeros_like(back)
    for g in range(GROUP):
        kbuf[0, g] = tile(pairs[1 + g], fa, incoming)

    def body(i, total):
        now = lax.rem(i, 2)
        for g in range(GROUP):
            j = 1 + i * GROUP + g
            a, b, _ = unpack(pairs[j])
            before = unpack(pairs[jnp.maximum(j - 1, 1)])[1]
            keep = jnp.where(before == b, 1.0, 0.0).astype(F32)
            total = total * keep + dot(stage[a, :rhs], kbuf[now, g])
            back[b] = total.astype(BF16)
            kbuf[1 - now, g] = tile(pairs[j + GROUP], fa, incoming)
        return total

    lax.fori_loop(0, pl.cdiv(pairs[0], GROUP), body, jnp.zeros((rhs, width), F32))


def reply(pairs, stage, fa, incoming):
    peers, rows, width = incoming.shape
    return pl.pallas_call(
        reply_kernel,
        out_shape=jax.ShapeDtypeStruct((peers, rows - 24 - FEAT, width), BF16),
        in_specs=[SMEM] + [VMEM] * 3,
        out_specs=VMEM,
        scratch_shapes=[pltpu.VMEM((2, GROUP, width, width), BF16)],
        compiler_params=WIDE,
        cost_estimate=pl.CostEstimate(flops=6 << 30, bytes_accessed=8 << 20, transcendentals=0),
        name="reply",
    )(pairs, stage, fa, incoming)


def remote_kernel(pairs, fa, incoming, acc_in, acc, kbuf):
    rhs = acc.shape[1]
    acc[...] = acc_in[...]
    for g in range(GROUP):
        kbuf[0, g] = tile(pairs[1 + g], fa, incoming)

    def body(i, carry):
        now = lax.rem(i, 2)
        for g in range(GROUP):
            j = 1 + i * GROUP + g
            a, b, _ = unpack(pairs[j])
            acc[a] += dot(incoming[b, :rhs], kbuf[now, g], ((1,), (1,)))
            kbuf[1 - now, g] = tile(pairs[j + GROUP], fa, incoming)
        return carry

    lax.fori_loop(0, pl.cdiv(pairs[0], GROUP), body, 0)


def remote_near(pairs, fa, incoming, acc):
    width = acc.shape[2]
    return pl.pallas_call(
        remote_kernel,
        out_shape=jax.ShapeDtypeStruct(acc.shape, F32),
        in_specs=[SMEM] + [VMEM] * 3,
        out_specs=VMEM,
        scratch_shapes=[pltpu.VMEM((2, GROUP, width, width), BF16)],
        compiler_params=WIDE,
        cost_estimate=pl.CostEstimate(flops=6 << 30, bytes_accessed=8 << 20, transcendentals=0),
        name="remote_near",
    )(pairs, fa, incoming, acc)


def far_kernel(ids, own_points, nodes, trans, acc, basis, base):
    rank = 32

    def skel(n):
        rows = nodes[n, 16:32, :]
        return jnp.concatenate([rows[:, :128], rows[:, 128:]], axis=0)

    def transfer(n, which):
        rows = nodes[n, 32:, 128 * which : 128 * which + 128].astype(F32)
        return jnp.concatenate([rows[:, 32 * i : 32 * i + 32] for i in range(4)], axis=0).astype(BF16)

    def points(n):
        return nodes[n, :16, :128].astype(F32)[9:10]

    def kernel_tile(mine, theirs):
        gap = mine - theirs
        sq = gap * gap
        s = ((DELTA * DELTA + sq[:, :32]) + sq[:, 32:64]) + sq[:, 64:96]
        return halves(KCOEF * lax.rsqrt(s))

    def apply(tile, source):
        return dot(tile[0], source) + dot(tile[1], source)

    mine = [own_points[level] for level in range(3)]
    zero = jnp.zeros((rank, 128), F32)

    def one(f, total):
        n = ids[f]
        return total + apply(kernel_tile(mine[0], points(n)), skel(n))

    def two(f, total):
        n, m = ids[8 + f], lax.rem(ids[8 + f] + 64, 128)
        source = dot(transfer(n, 0), skel(n)) + dot(transfer(m, 0), skel(m))
        theirs = 0.5 * (points(n) + points(m))
        return total + apply(kernel_tile(mine[1], theirs), source.astype(BF16))

    def three(f, total):
        n = [lax.rem(ids[24 + f] + step, 128) for step in (0, 64, 1, 65)]
        terms = [dot(transfer(i, 1), skel(i)) for i in n]
        source = (terms[0] + terms[1]) + (terms[2] + terms[3])
        left = 0.5 * (points(n[0]) + points(n[1]))
        right = 0.5 * (points(n[2]) + points(n[3]))
        return total + apply(kernel_tile(mine[2], 0.5 * (left + right)), source.astype(BF16))

    far_one = lax.fori_loop(0, 8, one, zero, unroll=True)
    far_two = lax.fori_loop(0, 16, two, zero, unroll=4)
    far_three = lax.fori_loop(0, 32, three, zero, unroll=4)
    me = ids[56]

    def down_by(which, value):
        high, low = halves(value)
        mat = transfer(me, which)
        return dot(mat, high, ((0,), (0,))) + dot(mat, low, ((0,), (0,)))

    down = far_one + down_by(0, far_two) + down_by(1, far_three)
    high, low = halves(down.T)
    for c in range(trans.shape[0]):
        leaf = (dot(high, trans[c]) + dot(low, trans[c])).astype(BF16)
        base[c] = acc[c] * KCOEF + dot(leaf, basis[c])


def far_field(ids, own_points, nodes, trans, acc, basis):
    return pl.pallas_call(
        far_kernel,
        out_shape=jax.ShapeDtypeStruct(acc.shape, F32),
        in_specs=[SMEM] + [VMEM] * 5,
        out_specs=VMEM,
        compiler_params=WIDE,
        cost_estimate=pl.CostEstimate(flops=6 << 30, bytes_accessed=4 << 20, transcendentals=0),
        name="far_field",
    )(ids, own_points, nodes, trans, acc, basis)


def final_kernel(order, starts, base, returned, out, rows, sems):
    clusters = base.shape[0]

    def copy(c):
        return pltpu.make_async_copy(rows.at[c], out.at[c], sems.at[c])

    for c in range(clusters):

        def collect(i, total):
            return total + returned[order[i]].astype(F32)

        zero = jnp.zeros(base.shape[1:], F32)
        total = lax.fori_loop(starts[c], starts[c + 1], collect, zero)
        rows[c] = (base[c] + KCOEF * total).T
        copy(c).start()
    for c in range(clusters):
        copy(c).wait()


def finish(order, starts, base, returned):
    clusters, conductors, width = base.shape
    return pl.pallas_call(
        final_kernel,
        out_shape=jax.ShapeDtypeStruct((clusters, width, conductors), F32),
        in_specs=[SMEM] * 2 + [VMEM] * 2,
        out_specs=pl.BlockSpec(memory_space=pl.ANY),
        scratch_shapes=[
            pltpu.VMEM((clusters, width, conductors), F32),
            pltpu.SemaphoreType.DMA((clusters,)),
        ],
        compiler_params=WIDE,
        name="finish",
    )(order, starts, base, returned)


def pair_lists(first, second, count, clusters, entries):
    live = jnp.arange(first.shape[0], dtype=jnp.int32) < count
    own = second < clusters
    a = jnp.where(own, jnp.minimum(first, second), first)
    b = jnp.where(own, jnp.maximum(first, second), second)
    key = jnp.where(live, b * clusters + a, -1)
    keys = jnp.arange(entries * clusters, dtype=jnp.int32)
    times = jnp.sum((keys[:, None] == key[None, :]).astype(jnp.int32), axis=1)
    times = jnp.where(keys % clusters == keys // clusters, times, 2 * times)
    lists = []
    for lo, hi in ((0, clusters * clusters), (clusters * clusters, entries * clusters)):
        part = times[lo:hi]
        held = part > 0
        spots = jnp.arange(hi - lo, dtype=jnp.int32)
        rank = jnp.sum(((spots[None, :] < spots[:, None]) & held[None, :]).astype(jnp.int32), axis=1)
        slots = jnp.arange(256 + 2 * GROUP, dtype=jnp.int32)
        match = (rank[None, :] == slots[:, None]) & held[None, :]
        total = jnp.sum(held.astype(jnp.int32))
        last = jnp.max(jnp.where(held, spots, 0))
        code = jnp.sum(jnp.where(match, (spots + 1024 * part)[None, :], 0), axis=1)
        code = jnp.where(slots < total, code, last)
        lists.append(jnp.concatenate([total.reshape(1), code]))
    return lists


def shards(
    charges,
    panel_coords,
    cluster_basis,
    trans_leaf,
    trans_pair,
    trans_quad,
    skel_points,
    send_slots,
    pair_first,
    pair_second,
    pair_count,
    far_one,
    far_two,
    far_three,
):
    clusters, _, width = panel_coords.shape
    conductors = charges.shape[1]
    peers = lax.axis_size("dev")
    blocks = charges.reshape(clusters, width, conductors)
    points = jnp.pad(skel_points.reshape(1, 1, -1), ((0, 2), (0, 0), (0, width - skel_points.size)))
    axes = jnp.concatenate([jnp.swapaxes(panel_coords, 0, 1), points], axis=1).astype(F32)
    slots = send_slots[:, 0]
    ints = jnp.concatenate([slots, far_two[0], far_three[0]])
    stage, fa, outgoing = prep(
        ints, blocks, axes, cluster_basis, trans_leaf, trans_pair, trans_quad, peers
    )
    incoming = lax.all_to_all(outgoing, "dev", split_axis=0, concat_axis=0, tiled=True)

    own_list, remote_list = pair_lists(pair_first, pair_second, pair_count[0], clusters, clusters + peers)
    acc = own_near(own_list, stage, fa)
    back = reply(remote_list, stage, fa, incoming)
    returned = lax.all_to_all(back, "dev", split_axis=0, concat_axis=0, tiled=True)
    acc = remote_near(remote_list, fa, incoming, acc)

    z, d = lax.axis_index("group"), lax.axis_index("dev")
    xy, c = d // 2, d % 2
    nodes, _ = lax.optimization_barrier((incoming, back))
    same = nodes.reshape(peers // 2, 2, -1, width)[:, :, conductors:]
    same = lax.dynamic_index_in_dim(same, c, axis=1, keepdims=False)
    along = [same]
    for step in (1, 2, 3):
        along.append(lax.ppermute(same, "group", [(i, (i + step) % 4) for i in range(4)]))
    along, acc = lax.optimization_barrier((along, acc))
    along = jnp.stack(along)
    other = lax.ppermute(along, "dev", [(i, i ^ 1) for i in range(32)])
    nodes = jnp.stack([along, other]).reshape(128, 40, width)

    def place(owner):
        step = (z - owner // peers) % 4
        return ((c ^ owner % 2) * 4 + step) * 16 + owner % peers // 2

    quad = lax.dynamic_slice(incoming, (d // 4 * 4, conductors + 9, 0), (4, 1, width))[:, 0]
    quad_lists = quad[:, 128:144].astype(jnp.int32)
    pair_list = lax.dynamic_slice_in_dim(quad_lists[:, :8], d % 4 // 2 * 2, 2, axis=0)
    ids = jnp.concatenate(
        [
            place(far_one[0]),
            place(2 * pair_list.reshape(-1)),
            place(4 * quad_lists[:, 8:].reshape(-1)),
            xy.reshape(1),
        ]
    )
    quad_points = quad[:, :96].astype(F32).reshape(4, 3, 32)
    pair_points = 0.5 * (quad_points[0::2] + quad_points[1::2])
    own_points = jnp.stack(
        [
            skel_points[0].astype(F32),
            lax.dynamic_index_in_dim(pair_points, d % 4 // 2, axis=0, keepdims=False),
            0.5 * (pair_points[0] + pair_points[1]),
        ]
    )
    own_points = jnp.repeat(jnp.swapaxes(own_points, 1, 2), 32, axis=2)
    own_points = jnp.pad(own_points, ((0, 0), (0, 0), (0, 32)))
    base = far_field(ids, own_points, nodes, trans_leaf, acc, cluster_basis)

    spots = jnp.arange(peers, dtype=jnp.int32)
    rank = jnp.sum(
        (slots[None, :] < slots[:, None])
        | ((slots[None, :] == slots[:, None]) & (spots[None, :] < spots[:, None])),
        axis=1,
        dtype=jnp.int32,
    )
    order = jnp.sum(jnp.where(rank[None, :] == spots[:, None], spots[None, :], 0), axis=1)
    edges = jnp.arange(clusters + 1, dtype=jnp.int32)
    starts = jnp.sum(slots[None, :] < edges[:, None], axis=1, dtype=jnp.int32)
    out = finish(order, starts, base, returned)
    return out.reshape(clusters * width, conductors)


def solution(mesh):
    owners = ("group", "dev")
    rows, block, flat = P(owners, None), P(owners, None, None), P(owners)
    placed = (rows, *(block,) * 6, rows, *(flat,) * 3, *(rows,) * 3)
    return jax.shard_map(shards, mesh=mesh, in_specs=placed, out_specs=rows, check_vma=False)
```

```python
import functools

import jax
import jax.numpy as jnp
from jax import lax
from jax.experimental import pallas as pl
from jax.experimental.pallas import tpu as pltpu
from jax.sharding import PartitionSpec as P

KCOEF = 0.005
DELTA = 0.02
F32 = jnp.float32
BF16 = jnp.bfloat16
GROUP = 8
FEAT = 16
VMEM = pl.BlockSpec(memory_space=pltpu.VMEM)
SMEM = pl.BlockSpec(memory_space=pltpu.SMEM)
ANY = pl.BlockSpec(memory_space=pl.ANY)
MESH = pl.DeviceIdType.MESH
TAIL = 512
ROUTE = (
    (3, 2, 1), (0, 1, 1), (1, 2, 0), (2, 1, 0), (1, 2, 1), (3, 0, 0), (3, 3, 0), (0, 0, 1),
    (3, 1, 0), (3, 0, 1), (0, 2, 0), (1, 1, 1), (2, 2, 1), (3, 2, 0), (1, 3, 1), (1, 0, 0),
    (3, 3, 1), (2, 0, 1), (1, 3, 0), (2, 3, 0), (3, 1, 1), (2, 2, 0), (1, 0, 1), (0, 3, 0),
    (2, 0, 0), (0, 1, 0), (0, 2, 1), (2, 1, 1), (2, 3, 1), (0, 3, 1), (1, 1, 0),
)
MESH = pl.DeviceIdType.MESH
PARAMS = pltpu.CompilerParams(vmem_limit_bytes=14 << 20)
WIDE = pltpu.CompilerParams(vmem_limit_bytes=56 << 20)


def dot(left, right, dims=((1,), (0,))):
    return lax.dot_general(left, right, (dims, ((), ())), preferred_element_type=F32)


def halves(value):
    high = value.astype(BF16)
    return high, (value - high.astype(F32)).astype(BF16)


def thirds(value):
    high = value.astype(BF16)
    rest = value - high.astype(F32)
    mid = rest.astype(BF16)
    return high.astype(F32), mid.astype(F32), (rest - mid.astype(F32))


def pair_lists(first, second, count, lists, weights):
    lane = lax.broadcasted_iota(jnp.int32, first.shape, 1)
    own = second < 16
    a = jnp.where(own, jnp.minimum(first, second), first)
    b = jnp.where(own, jnp.maximum(first, second), second)
    b = jnp.where(lane < count, b, 64)

    def hot(rows, index):
        spot = lax.broadcasted_iota(jnp.int32, (rows, first.shape[1]), 0)
        return jnp.where(spot == index, 1.0, 0.0).astype(BF16)

    times = dot(hot(48, b), hot(16, a), ((1,), (1,)))
    row = lax.broadcasted_iota(jnp.int32, times.shape, 0)
    col = lax.broadcasted_iota(jnp.int32, times.shape, 1)
    held = jnp.where(times > 0, 1.0, 0.0)
    twice = jnp.where(row == col, times, 2.0 * times)
    key = (jnp.where(row < 16, row, row - 16) * 16 + col).astype(F32)
    up_r = lax.broadcasted_iota(jnp.int32, (16, 16), 0)
    up_c = lax.broadcasted_iota(jnp.int32, (16, 16), 1)
    within = dot(held.astype(BF16), jnp.where(up_r < up_c, 1.0, 0.0).astype(BF16))
    low_r = lax.broadcasted_iota(jnp.int32, (48, 48), 0)
    low_c = lax.broadcasted_iota(jnp.int32, (48, 48), 1)
    below = (low_c < low_r) & ((low_c >= 16) | (low_r < 16))
    above = jnp.sum(dot(jnp.where(below, 1.0, 0.0).astype(BF16), held.astype(BF16)), axis=1, keepdims=True)
    rank = jnp.where(held > 0, above + within + 1.0, -1.0)
    value = key + 1024.0 * twice
    slot = lax.broadcasted_iota(jnp.int32, (48, TAIL), 1).astype(F32)
    code = jnp.zeros((48, TAIL), F32)
    for i in range(16):
        code += jnp.where(rank[:, i : i + 1] == slot, value[:, i : i + 1], 0.0)
    for i, (lo, hi) in enumerate(((0, 16), (16, 48))):
        total = jnp.sum(jnp.sum(held[lo:hi], axis=1, keepdims=True), axis=0, keepdims=True)
        last = jnp.max(jnp.max((held * key)[lo:hi], axis=1, keepdims=True), axis=0, keepdims=True)
        mine = jnp.sum(code[lo:hi], axis=0, keepdims=True)
        mine = jnp.where(slot[:1] > total, last, mine)
        lists[i : i + 1] = jnp.where(slot[:1] == 0, total, mine).astype(jnp.int32)
    turned = dot(hot(16, a), hot(48, b), ((1,), (1,)))
    line = lax.broadcasted_iota(jnp.int32, (16, 128), 0)
    for i in range(16):
        part = jnp.broadcast_to(turned[:, i : i + 1], (16, 128))
        weights[i] = jnp.where(line == i, 0.5 * part, part)


def exchange_kernel(
    ints, pairs, charges, axes, basis, trans, pair, quad,
    stage, fa, incoming, nodes, lists, acc,
    rows_a, rows_b, outgoing, weights, kbuf, team_send, team_recv, node_send, node_recv, own_sem,
):
    clusters, _, rhs = charges.shape
    width = stage.shape[2]
    z, d = lax.axis_index("group"), lax.axis_index("dev")
    x, y, c = d // 8, lax.rem(d // 2, 4), lax.rem(d, 2)

    def member(x, y, c):
        return (x * 4 + y) * 2 + c

    def turn(i, k):
        return lax.rem(i + k, 4)

    team = [member(turn(x, i), turn(y, j), lax.rem(c + k, 2)) for i, j, k in ROUTE]
    barrier = pltpu.get_barrier_semaphore()
    for peer in team:
        pl.semaphore_signal(barrier, inc=1, device_id={"group": z, "dev": peer}, device_id_type=MESH)
    for k in (1, 2, 3):
        pl.semaphore_signal(barrier, inc=1, device_id={"group": turn(z, k), "dev": d}, device_id_type=MESH)

    total = jnp.zeros((trans.shape[1], rhs), F32)
    for i in range(clusters):
        leaf = dot(basis[i], charges[i]).astype(BF16)
        total += dot(trans[i], leaf)
    top = total.astype(BF16)
    mats = [mat[0].astype(F32) for mat in (pair, quad)]
    moves = jnp.concatenate([mat[8 * i : 8 * i + 8] for mat in mats for i in range(4)], axis=1)
    lane = lax.broadcasted_iota(jnp.int32, (1, width), 1)
    points = [axes[i, clusters : clusters + 1] for i in range(3)]
    info = points[0] + pltpu.roll(points[1], 32, 1) + pltpu.roll(points[2], 64, 1)
    for i in range(16):
        info = jnp.where(lane == rhs + i, ints[32 + i].astype(F32), info)
    line = lax.broadcasted_iota(jnp.int32, (8, width), 0)
    info = jnp.where(line == 0, jnp.broadcast_to(info, (8, width)), 0.0)
    me = ((c * 4 + z) * 4 + y) * 4 + x
    nodes[me, :16] = jnp.concatenate([top[:16], top[16:]], axis=1)
    nodes[me, 16:] = jnp.concatenate([moves, info], axis=0).astype(BF16)

    def node_copy(start, length, sem, peer):
        held = nodes.at[pl.ds(start, length)]
        return pltpu.make_async_remote_copy(
            src_ref=held,
            dst_ref=held,
            send_sem=node_send.at[sem],
            recv_sem=node_recv.at[sem],
            device_id=peer,
            device_id_type=MESH,
        )

    pl.semaphore_wait(barrier, 34)
    along_x = [node_copy(me, 1, k, {"group": z, "dev": member(turn(x, k + 1), y, c)}) for k in range(3)]
    for copy in along_x:
        copy.start()

    point = [axes[i, :clusters] for i in range(3)]
    norm = point[0] * point[0] + point[1] * point[1] + point[2] * point[2]
    one = jnp.ones_like(norm)
    rows_a[...] = jnp.zeros_like(rows_a)
    rows_b[...] = jnp.zeros_like(rows_b)
    for i, row in enumerate((*point, *thirds(norm + DELTA * DELTA), one, one, one)):
        rows_a[:, i, :] = row
    for i, row in enumerate((*(-2.0 * p for p in point), one, one, one, *thirds(norm))):
        rows_b[:, i, :] = row
    for i in range(clusters):
        stage[i, :rhs] = charges[i].T
        stage[i, rhs:] = rows_b[i].astype(BF16)

    for copy in along_x:
        copy.wait_recv()
    start = (c * 4 + z) * 16
    along_y = [
        node_copy(start + y * 4, 4, 3 + k, {"group": z, "dev": member(x, turn(y, k + 1), c)}) for k in range(3)
    ]
    for copy in along_y:
        copy.start()

    sent = []

    def send(i):
        outgoing[i] = stage[ints[team[i]]]
        copy = pltpu.make_async_remote_copy(
            src_ref=outgoing.at[i],
            dst_ref=incoming.at[d],
            send_sem=team_send.at[i],
            recv_sem=team_recv.at[i],
            device_id={"group": z, "dev": team[i]},
            device_id_type=MESH,
        )
        copy.start()
        sent.append(copy)

    for i in range(4):
        send(i)
    for i in range(clusters):
        fa[i] = rows_a[i].T.astype(BF16)
    pair_lists(pairs[:1], pairs[1:2], ints[48], lists, weights)
    for copy in along_y:
        copy.wait_recv()
    along_z = []
    for i in range(4, 31):
        send(i)
        if i % 2 == 0 and len(along_z) < 12:
            part, k = divmod(len(along_z), 3)
            peer = {"group": turn(z, k + 1), "dev": d}
            along_z.append(node_copy(start + part * 4, 4, 6 + len(along_z), peer))
            along_z[-1].start()
    outgoing[31] = stage[ints[d]]
    own = pltpu.make_async_copy(outgoing.at[31], incoming.at[d], own_sem)
    own.start()
    chip = {"group": z, "dev": member(x, y, 1 - c)}
    across = [node_copy(start, 16, 18, chip)]
    across[0].start()

    acc[...] = jnp.zeros_like(acc)

    def entries(i, t):
        low = t <= i
        return jnp.where(low, t, t - i - 1), jnp.where(low, i, 15 - i)

    def near(i, carry):
        for t in range(17):
            a, b = entries(i, t)
            s = dot(fa[a], stage[b, rhs:])
            k = lax.rsqrt(s.astype(BF16))
            line = weights[b, pl.ds(a, 1), :].astype(BF16)
            kbuf[t] = k * jnp.concatenate([line, line], axis=1)
        for t in range(17):
            a, b = entries(i, t)
            acc[a] += dot(stage[b, :rhs], kbuf[t], ((1,), (1,)))
            acc[b] += dot(stage[a, :rhs], kbuf[t])
        return carry

    lax.fori_loop(0, 8, near, 0)

    for k in range(3):
        for part in range(4):
            along_z[part * 3 + k].wait_recv()
        across.append(node_copy((c * 4 + turn(z, 3 - k)) * 16, 16, 19 + k, chip))
        across[-1].start()
    for copy in across:
        copy.wait_recv()
    for copy in sent:
        copy.wait_recv()
    own.wait()
    for copy in (*along_x, *along_y, *along_z, *across, *sent):
        copy.wait_send()


def exchange(ints, pairs, charges, axes, basis, trans, pair, quad):
    clusters, width, rhs = charges.shape
    rows = rhs + FEAT
    return pl.pallas_call(
        exchange_kernel,
        out_shape=(
            jax.ShapeDtypeStruct((clusters, rows, width), BF16),
            jax.ShapeDtypeStruct((clusters, width, FEAT), BF16),
            jax.ShapeDtypeStruct((32, rows, width), BF16),
            jax.ShapeDtypeStruct((128, 32, width), BF16),
            jax.ShapeDtypeStruct((2, TAIL), jnp.int32),
            jax.ShapeDtypeStruct((clusters, rhs, width), F32),
        ),
        in_specs=[SMEM] + [VMEM] * 7,
        out_specs=(VMEM, VMEM, ANY, VMEM, VMEM, VMEM),
        scratch_shapes=[pltpu.VMEM((clusters, FEAT, width), F32)] * 2
        + [
            pltpu.VMEM((32, rows, width), BF16),
            pltpu.VMEM((16, 16, 128), F32),
            pltpu.VMEM((17, width, width), BF16),
            pltpu.SemaphoreType.DMA((31,)),
            pltpu.SemaphoreType.DMA((31,)),
            pltpu.SemaphoreType.DMA((22,)),
            pltpu.SemaphoreType.DMA((22,)),
            pltpu.SemaphoreType.DMA,
        ],
        compiler_params=pltpu.CompilerParams(
            vmem_limit_bytes=56 << 20, collective_id=0, has_side_effects=True
        ),
        name="exchange",
    )(ints, pairs, charges, axes, basis, trans, pair, quad)


def unpack(code):
    return code & 15, (code >> 4) & 63, (code >> 10).astype(F32) * 0.5


def tile(code, fa, table):
    a, b, times = unpack(code)
    s = dot(fa[a], table[b, table.shape[1] - FEAT :])
    return lax.rsqrt(s.astype(BF16)) * times.astype(BF16)


def reply_kernel(pairs, stage, fa, incoming, back, kbuf):
    rhs, width = back.shape[1:]
    back[...] = jnp.zeros_like(back)
    for g in range(GROUP):
        kbuf[0, g] = tile(pairs[1, 1 + g], fa, incoming)

    def body(i, total):
        now = lax.rem(i, 2)
        for g in range(GROUP):
            j = 1 + i * GROUP + g
            a, b, _ = unpack(pairs[1, j])
            before = unpack(pairs[1, jnp.maximum(j - 1, 1)])[1]
            keep = jnp.where(before == b, 1.0, 0.0).astype(F32)
            total = total * keep + dot(stage[a, :rhs], kbuf[now, g])
            back[b] = total.astype(BF16)
            kbuf[1 - now, g] = tile(pairs[1, j + GROUP], fa, incoming)
        return total

    lax.fori_loop(0, pl.cdiv(pairs[1, 0], GROUP), body, jnp.zeros((rhs, width), F32))


def reply(pairs, stage, fa, incoming):
    peers, rows, width = incoming.shape
    return pl.pallas_call(
        reply_kernel,
        out_shape=jax.ShapeDtypeStruct((peers, rows - FEAT, width), BF16),
        in_specs=[SMEM] + [VMEM] * 3,
        out_specs=VMEM,
        scratch_shapes=[pltpu.VMEM((2, GROUP, width, width), BF16)],
        compiler_params=WIDE,
        cost_estimate=pl.CostEstimate(flops=6 << 30, bytes_accessed=8 << 20, transcendentals=0),
        name="reply",
    )(pairs, stage, fa, incoming)


def remote_kernel(pairs, fa, incoming, acc_in, acc, kbuf):
    rhs = acc.shape[1]
    acc[...] = acc_in[...]
    for g in range(GROUP):
        kbuf[0, g] = tile(pairs[1, 1 + g], fa, incoming)

    def body(i, carry):
        now = lax.rem(i, 2)
        for g in range(GROUP):
            j = 1 + i * GROUP + g
            a, b, _ = unpack(pairs[1, j])
            acc[a] += dot(incoming[b, :rhs], kbuf[now, g], ((1,), (1,)))
            kbuf[1 - now, g] = tile(pairs[1, j + GROUP], fa, incoming)
        return carry

    lax.fori_loop(0, pl.cdiv(pairs[1, 0], GROUP), body, 0)


def remote_near(pairs, fa, incoming, acc):
    width = acc.shape[2]
    return pl.pallas_call(
        remote_kernel,
        out_shape=jax.ShapeDtypeStruct(acc.shape, F32),
        in_specs=[SMEM] + [VMEM] * 3,
        out_specs=VMEM,
        scratch_shapes=[pltpu.VMEM((2, GROUP, width, width), BF16)],
        compiler_params=WIDE,
        cost_estimate=pl.CostEstimate(flops=6 << 30, bytes_accessed=8 << 20, transcendentals=0),
        name="remote_near",
    )(pairs, fa, incoming, acc)


def far_kernel(ids, own_points, nodes, trans, acc, basis, base):
    rank = 32

    def skel(n):
        rows = nodes[n, :16, :]
        return jnp.concatenate([rows[:, :128], rows[:, 128:]], axis=0)

    def transfer(n, which):
        rows = nodes[n, 16:, 128 * which : 128 * which + 128].astype(F32)
        return jnp.concatenate([rows[:8, 32 * i : 32 * i + 32] for i in range(4)], axis=0).astype(BF16)

    def points(n):
        return nodes[n, 16:, :128].astype(F32)[8:9]

    def kernel_tile(mine, theirs):
        gap = mine - theirs
        sq = gap * gap
        s = ((DELTA * DELTA + sq[:, :32]) + sq[:, 32:64]) + sq[:, 64:96]
        return halves(KCOEF * lax.rsqrt(s))

    def apply(tile, source):
        return dot(tile[0], source) + dot(tile[1], source)

    mine = [own_points[level] for level in range(3)]
    zero = jnp.zeros((rank, 128), F32)

    def one(f, total):
        n = ids[f]
        return total + apply(kernel_tile(mine[0], points(n)), skel(n))

    def two(f, total):
        n, m = ids[8 + f], ids[8 + f] + 64
        source = dot(transfer(n, 0), skel(n)) + dot(transfer(m, 0), skel(m))
        theirs = 0.5 * (points(n) + points(m))
        return total + apply(kernel_tile(mine[1], theirs), source.astype(BF16))

    def three(f, total):
        n = [ids[24 + f] + step for step in (0, 64, 4, 68)]
        terms = [dot(transfer(i, 1), skel(i)) for i in n]
        source = (terms[0] + terms[1]) + (terms[2] + terms[3])
        left = 0.5 * (points(n[0]) + points(n[1]))
        right = 0.5 * (points(n[2]) + points(n[3]))
        return total + apply(kernel_tile(mine[2], 0.5 * (left + right)), source.astype(BF16))

    far_one = lax.fori_loop(0, 8, one, zero, unroll=True)
    far_two = lax.fori_loop(0, 16, two, zero, unroll=4)
    far_three = lax.fori_loop(0, 32, three, zero, unroll=4)
    me = ids[56]

    def down_by(which, value):
        high, low = halves(value)
        mat = transfer(me, which)
        return dot(mat, high, ((0,), (0,))) + dot(mat, low, ((0,), (0,)))

    down = far_one + down_by(0, far_two) + down_by(1, far_three)
    high, low = halves(down.T)
    for c in range(trans.shape[0]):
        leaf = (dot(high, trans[c]) + dot(low, trans[c])).astype(BF16)
        base[c] = acc[c] * KCOEF + dot(leaf, basis[c])


def far_field(ids, own_points, nodes, trans, acc, basis):
    return pl.pallas_call(
        far_kernel,
        out_shape=jax.ShapeDtypeStruct(acc.shape, F32),
        in_specs=[SMEM] + [VMEM] * 5,
        out_specs=VMEM,
        compiler_params=WIDE,
        cost_estimate=pl.CostEstimate(flops=6 << 30, bytes_accessed=4 << 20, transcendentals=0),
        name="far_field",
    )(ids, own_points, nodes, trans, acc, basis)


def final_kernel(order, starts, base, returned, out, rows, sems):
    clusters = base.shape[0]

    def copy(c):
        return pltpu.make_async_copy(rows.at[c], out.at[c], sems.at[c])

    for c in range(clusters):

        def collect(i, total):
            return total + returned[order[i]].astype(F32)

        zero = jnp.zeros(base.shape[1:], F32)
        total = lax.fori_loop(starts[c], starts[c + 1], collect, zero)
        rows[c] = (base[c] + KCOEF * total).T
        copy(c).start()
    for c in range(clusters):
        copy(c).wait()


def finish(order, starts, base, returned):
    clusters, conductors, width = base.shape
    return pl.pallas_call(
        final_kernel,
        out_shape=jax.ShapeDtypeStruct((clusters, width, conductors), F32),
        in_specs=[SMEM] * 2 + [VMEM] * 2,
        out_specs=pl.BlockSpec(memory_space=pl.ANY),
        scratch_shapes=[
            pltpu.VMEM((clusters, width, conductors), F32),
            pltpu.SemaphoreType.DMA((clusters,)),
        ],
        compiler_params=WIDE,
        name="finish",
    )(order, starts, base, returned)


def shards(
    charges,
    panel_coords,
    cluster_basis,
    trans_leaf,
    trans_pair,
    trans_quad,
    skel_points,
    send_slots,
    pair_first,
    pair_second,
    pair_count,
    far_one,
    far_two,
    far_three,
):
    clusters, _, width = panel_coords.shape
    conductors = charges.shape[1]
    peers = lax.axis_size("dev")
    blocks = charges.reshape(clusters, width, conductors)
    points = jnp.pad(skel_points[0][:, None, :], ((0, 0), (0, 0), (0, width - skel_points.shape[2])))
    axes = jnp.concatenate([jnp.swapaxes(panel_coords, 0, 1), points], axis=1).astype(F32)
    ints = jnp.concatenate([send_slots[:, 0], far_two[0], far_three[0], pair_count])
    pairs = jnp.stack([pair_first, pair_second])
    stage, fa, incoming, nodes, lists, acc = exchange(
        ints, pairs, blocks, axes, cluster_basis, trans_leaf, trans_pair, trans_quad
    )
    back = reply(lists, stage, fa, incoming)
    returned = lax.all_to_all(back, "dev", split_axis=0, concat_axis=0, tiled=True)
    acc = remote_near(lists, fa, incoming, acc)

    z, d = lax.axis_index("group"), lax.axis_index("dev")
    x, y = d // 8, d // 2 % 4

    def place(owner):
        z, d = owner // peers, owner % peers
        return ((d % 2 * 4 + z) * 4 + d // 2 % 4) * 4 + d // 8

    quad = lax.dynamic_slice(
        nodes.reshape(2, 4, 4, 4, 32, width), (0, z, y // 2 * 2, x, 24, 0), (2, 1, 2, 1, 1, width)
    )
    quad = jnp.swapaxes(quad.reshape(2, 2, width), 0, 1).reshape(4, width)
    quad_lists = quad[:, 128:144].astype(jnp.int32)
    pair_list = lax.dynamic_slice_in_dim(quad_lists[:, :8], d % 4 // 2 * 2, 2, axis=0)
    ids = jnp.concatenate(
        [
            place(far_one[0]),
            place(2 * pair_list.reshape(-1)),
            place(4 * quad_lists[:, 8:].reshape(-1)),
            place(z * peers + d).reshape(1),
        ]
    )
    quad_points = quad[:, :96].astype(F32).reshape(4, 3, 32)
    pair_points = 0.5 * (quad_points[0::2] + quad_points[1::2])
    own_points = jnp.stack(
        [
            skel_points[0].astype(F32),
            lax.dynamic_index_in_dim(pair_points, d % 4 // 2, axis=0, keepdims=False),
            0.5 * (pair_points[0] + pair_points[1]),
        ]
    )
    own_points = jnp.repeat(jnp.swapaxes(own_points, 1, 2), 32, axis=2)
    own_points = jnp.pad(own_points, ((0, 0), (0, 0), (0, 32)))
    base = far_field(ids, own_points, nodes, trans_leaf, acc, cluster_basis)

    slots = send_slots[:, 0]
    spots = jnp.arange(peers, dtype=jnp.int32)
    rank = jnp.sum(
        (slots[None, :] < slots[:, None])
        | ((slots[None, :] == slots[:, None]) & (spots[None, :] < spots[:, None])),
        axis=1,
        dtype=jnp.int32,
    )
    order = jnp.sum(jnp.where(rank[None, :] == spots[:, None], spots[None, :], 0), axis=1)
    edges = jnp.arange(clusters + 1, dtype=jnp.int32)
    starts = jnp.sum(slots[None, :] < edges[:, None], axis=1, dtype=jnp.int32)
    out = finish(order, starts, base, returned)
    return out.reshape(clusters * width, conductors)


def solution(mesh):
    owners = ("group", "dev")
    rows, block, flat = P(owners, None), P(owners, None, None), P(owners)
    placed = (rows, *(block,) * 6, rows, *(flat,) * 3, *(rows,) * 3)
    return jax.shard_map(shards, mesh=mesh, in_specs=placed, out_specs=rows, check_vma=False)
```

```python
import functools

import jax
import jax.numpy as jnp
from jax import lax
from jax.experimental import pallas as pl
from jax.experimental.pallas import tpu as pltpu
from jax.sharding import PartitionSpec as P

KCOEF = 0.005
DELTA = 0.02
F32 = jnp.float32
BF16 = jnp.bfloat16
GROUP = 8
FEAT = 16
VMEM = pl.BlockSpec(memory_space=pltpu.VMEM)
SMEM = pl.BlockSpec(memory_space=pltpu.SMEM)
ANY = pl.BlockSpec(memory_space=pl.ANY)
MESH = pl.DeviceIdType.MESH
TAIL = 512
SPLIT = (0, 10)
STEPS = tuple((i, j) for i in range(4) for j in range(4) if i or j)
ROUTE = (
    (3, 2, 1), (0, 1, 1), (1, 2, 0), (2, 1, 0), (1, 2, 1), (3, 0, 0), (3, 3, 0), (0, 0, 1),
    (3, 1, 0), (3, 0, 1), (0, 2, 0), (1, 1, 1), (2, 2, 1), (3, 2, 0), (1, 3, 1), (1, 0, 0),
    (3, 3, 1), (2, 0, 1), (1, 3, 0), (2, 3, 0), (3, 1, 1), (2, 2, 0), (1, 0, 1), (0, 3, 0),
    (2, 0, 0), (0, 1, 0), (0, 2, 1), (2, 1, 1), (2, 3, 1), (0, 3, 1), (1, 1, 0),
)
MESH = pl.DeviceIdType.MESH
WIDE = pltpu.CompilerParams(vmem_limit_bytes=56 << 20)


def dot(left, right, dims=((1,), (0,))):
    return lax.dot_general(left, right, (dims, ((), ())), preferred_element_type=F32)


def halves(value):
    high = value.astype(BF16)
    return high, (value - high.astype(F32)).astype(BF16)


def thirds(value):
    high = value.astype(BF16)
    rest = value - high.astype(F32)
    mid = rest.astype(BF16)
    return high.astype(F32), mid.astype(F32), (rest - mid.astype(F32))


def pair_lists(first, second, count, lists, weights):
    lane = lax.broadcasted_iota(jnp.int32, first.shape, 1)
    own = second < 16
    a = jnp.where(own, jnp.minimum(first, second), first)
    b = jnp.where(own, jnp.maximum(first, second), second)
    b = jnp.where(lane < count, b, 64)

    def hot(rows, index):
        spot = lax.broadcasted_iota(jnp.int32, (rows, first.shape[1]), 0)
        return jnp.where(spot == index, 1.0, 0.0).astype(BF16)

    times = dot(hot(48, b), hot(16, a), ((1,), (1,)))
    row = lax.broadcasted_iota(jnp.int32, times.shape, 0)
    col = lax.broadcasted_iota(jnp.int32, times.shape, 1)
    held = jnp.where(times > 0, 1.0, 0.0)
    twice = jnp.where(row == col, times, 2.0 * times)
    key = (jnp.where(row < 16, row, row - 16) * 16 + col).astype(F32)
    up_r = lax.broadcasted_iota(jnp.int32, (16, 16), 0)
    up_c = lax.broadcasted_iota(jnp.int32, (16, 16), 1)
    within = dot(held.astype(BF16), jnp.where(up_r < up_c, 1.0, 0.0).astype(BF16))
    low_r = lax.broadcasted_iota(jnp.int32, (48, 48), 0)
    low_c = lax.broadcasted_iota(jnp.int32, (48, 48), 1)
    below = (low_c < low_r) & ((low_c >= 16) | (low_r < 16))
    above = jnp.sum(dot(jnp.where(below, 1.0, 0.0).astype(BF16), held.astype(BF16)), axis=1, keepdims=True)
    rank = jnp.where(held > 0, above + within + 1.0, -1.0)
    value = key + 1024.0 * twice
    slot = lax.broadcasted_iota(jnp.int32, (48, TAIL), 1).astype(F32)
    code = jnp.zeros((48, TAIL), F32)
    for i in range(16):
        code += jnp.where(rank[:, i : i + 1] == slot, value[:, i : i + 1], 0.0)
    for i, (lo, hi) in enumerate(((0, 16), (16, 48))):
        total = jnp.sum(jnp.sum(held[lo:hi], axis=1, keepdims=True), axis=0, keepdims=True)
        last = jnp.max(jnp.max((held * key)[lo:hi], axis=1, keepdims=True), axis=0, keepdims=True)
        mine = jnp.sum(code[lo:hi], axis=0, keepdims=True)
        mine = jnp.where(slot[:1] > total, last, mine)
        lists[i : i + 1] = jnp.where(slot[:1] == 0, total, mine).astype(jnp.int32)
    turned = dot(hot(16, a), hot(48, b), ((1,), (1,)))
    line = lax.broadcasted_iota(jnp.int32, (16, 128), 0)
    for i in range(16):
        part = jnp.broadcast_to(turned[:, i : i + 1], (16, 128))
        weights[i] = jnp.where(line == i, 0.5 * part, part)


def exchange_kernel(
    ints, pairs, charges, axes, basis, trans, pair, quad,
    stage, fa, incoming, nodes, lists, acc,
    rows_a, rows_b, outgoing, weights, kbuf, team_send, team_recv, node_send, node_recv, own_sem,
):
    clusters, _, rhs = charges.shape
    width = stage.shape[2]
    z, d = lax.axis_index("group"), lax.axis_index("dev")
    x, y, c = d // 8, lax.rem(d // 2, 4), lax.rem(d, 2)

    def member(x, y, c):
        return (x * 4 + y) * 2 + c

    def turn(i, k):
        return lax.rem(i + k, 4)

    team = [member(turn(x, i), turn(y, j), lax.rem(c + k, 2)) for i, j, k in ROUTE]
    barrier = pltpu.get_barrier_semaphore()
    for peer in team:
        pl.semaphore_signal(barrier, inc=1, device_id={"group": z, "dev": peer}, device_id_type=MESH)
    for k in (1, 2, 3):
        pl.semaphore_signal(barrier, inc=1, device_id={"group": turn(z, k), "dev": d}, device_id_type=MESH)

    point = [axes[i, :clusters] for i in range(3)]
    norm = point[0] * point[0] + point[1] * point[1] + point[2] * point[2]
    one = jnp.ones_like(norm)
    rows_a[...] = jnp.zeros_like(rows_a)
    rows_b[...] = jnp.zeros_like(rows_b)
    for i, row in enumerate((*point, *thirds(norm + DELTA * DELTA), one, one, one)):
        rows_a[:, i, :] = row
    for i, row in enumerate((*(-2.0 * p for p in point), one, one, one, *thirds(norm))):
        rows_b[:, i, :] = row
    for i in range(clusters):
        stage[i, :rhs] = charges[i].T
        stage[i, rhs:] = rows_b[i].astype(BF16)

    pl.semaphore_wait(barrier, 34)
    sent = []

    def send(i):
        outgoing[i] = stage[ints[2, team[i]]]
        copy = pltpu.make_async_remote_copy(
            src_ref=outgoing.at[i],
            dst_ref=incoming.at[d],
            send_sem=team_send.at[i],
            recv_sem=team_recv.at[i],
            device_id={"group": z, "dev": team[i]},
            device_id_type=MESH,
        )
        copy.start()
        sent.append(copy)

    for i in range(SPLIT[0]):
        send(i)
    total = jnp.zeros((trans.shape[1], rhs), F32)
    for i in range(clusters):
        leaf = dot(basis[i], charges[i]).astype(BF16)
        total += dot(trans[i], leaf)
    top = total.astype(BF16)
    mats = [mat[0].astype(F32) for mat in (pair, quad)]
    moves = jnp.concatenate([mat[8 * i : 8 * i + 8] for mat in mats for i in range(4)], axis=1)
    lane = lax.broadcasted_iota(jnp.int32, (1, width), 1)
    points = [axes[i, clusters : clusters + 1] for i in range(3)]
    info = points[0] + pltpu.roll(points[1], 32, 1) + pltpu.roll(points[2], 64, 1)
    for i in range(16):
        info = jnp.where(lane == rhs + i, ints[2, 32 + i].astype(F32), info)
    line = lax.broadcasted_iota(jnp.int32, (8, width), 0)
    info = jnp.where(line == 0, jnp.broadcast_to(info, (8, width)), 0.0)
    me = ((c * 4 + z) * 4 + y) * 4 + x
    nodes[me, :16] = jnp.concatenate([top[:16], top[16:]], axis=1)
    nodes[me, 16:] = jnp.concatenate([moves, info], axis=0).astype(BF16)

    def node_copy(start, length, sem, peer):
        held = nodes.at[pl.ds(start, length)]
        return pltpu.make_async_remote_copy(
            src_ref=held,
            dst_ref=held,
            send_sem=node_send.at[sem],
            recv_sem=node_recv.at[sem],
            device_id=peer,
            device_id_type=MESH,
        )

    plane = [
        node_copy(me, 1, i, {"group": z, "dev": member(turn(x, dx), turn(y, dy), c)})
        for i, (dx, dy) in enumerate(STEPS)
    ]
    for copy in plane:
        copy.start()

    for i in range(SPLIT[0], SPLIT[1]):
        send(i)
    for i in range(clusters):
        fa[i] = rows_a[i].T.astype(BF16)
    pair_lists(pairs[:1], pairs[1:2], ints[2, 48], lists, weights)
    for copy in plane:
        copy.wait_recv()
    start = (c * 4 + z) * 16
    along_z = []
    for i in range(SPLIT[1], 31):
        send(i)
        while len(along_z) * (31 - SPLIT[1]) < 12 * (i + 1 - SPLIT[1]):
            part, k = divmod(len(along_z), 3)
            peer = {"group": turn(z, k + 1), "dev": d}
            along_z.append(node_copy(start + part * 4, 4, 15 + len(along_z), peer))
            along_z[-1].start()
    outgoing[31] = stage[ints[2, d]]
    own = pltpu.make_async_copy(outgoing.at[31], incoming.at[d], own_sem)
    own.start()
    chip = {"group": z, "dev": member(x, y, 1 - c)}
    across = [node_copy(start, 16, 27, chip)]
    across[0].start()

    acc[...] = jnp.zeros_like(acc)

    def entries(i, t):
        low = t <= i
        return jnp.where(low, t, t - i - 1), jnp.where(low, i, 15 - i)

    def near(i, carry):
        for t in range(17):
            a, b = entries(i, t)
            s = dot(fa[a], stage[b, rhs:])
            k = lax.rsqrt(s.astype(BF16))
            line = weights[b, pl.ds(a, 1), :].astype(BF16)
            kbuf[t] = k * jnp.concatenate([line, line], axis=1)
        for t in range(17):
            a, b = entries(i, t)
            acc[a] += dot(stage[b, :rhs], kbuf[t], ((1,), (1,)))
            acc[b] += dot(stage[a, :rhs], kbuf[t])
        return carry

    lax.fori_loop(0, 8, near, 0)

    for k in range(3):
        for part in range(4):
            along_z[part * 3 + k].wait_recv()
        across.append(node_copy((c * 4 + turn(z, 3 - k)) * 16, 16, 28 + k, chip))
        across[-1].start()
    for copy in across:
        copy.wait_recv()
    for copy in sent:
        copy.wait_recv()
    own.wait()
    for copy in (*plane, *along_z, *across, *sent):
        copy.wait_send()


def exchange(ints, pairs, charges, axes, basis, trans, pair, quad):
    clusters, width, rhs = charges.shape
    rows = rhs + FEAT
    return pl.pallas_call(
        exchange_kernel,
        out_shape=(
            jax.ShapeDtypeStruct((clusters, rows, width), BF16),
            jax.ShapeDtypeStruct((clusters, width, FEAT), BF16),
            jax.ShapeDtypeStruct((32, rows, width), BF16),
            jax.ShapeDtypeStruct((128, 32, width), BF16),
            jax.ShapeDtypeStruct((2, TAIL), jnp.int32),
            jax.ShapeDtypeStruct((clusters, rhs, width), F32),
        ),
        in_specs=[SMEM] + [VMEM] * 7,
        out_specs=(VMEM, VMEM, ANY, VMEM, VMEM, VMEM),
        scratch_shapes=[pltpu.VMEM((clusters, FEAT, width), F32)] * 2
        + [
            pltpu.VMEM((32, rows, width), BF16),
            pltpu.VMEM((16, 16, 128), F32),
            pltpu.VMEM((17, width, width), BF16),
            pltpu.SemaphoreType.DMA((31,)),
            pltpu.SemaphoreType.DMA((31,)),
            pltpu.SemaphoreType.DMA((31,)),
            pltpu.SemaphoreType.DMA((31,)),
            pltpu.SemaphoreType.DMA,
        ],
        compiler_params=pltpu.CompilerParams(
            vmem_limit_bytes=56 << 20, collective_id=0, has_side_effects=True
        ),
        name="exchange",
    )(ints, pairs, charges, axes, basis, trans, pair, quad)


def unpack(code):
    return code & 15, (code >> 4) & 63, (code >> 10).astype(F32) * 0.5


def tile(code, fa, table):
    a, b, times = unpack(code)
    s = dot(fa[a], table[b, table.shape[1] - FEAT :])
    return lax.rsqrt(s.astype(BF16)) * times.astype(BF16)


def fetch(blocks, held, sems):
    def copy(b):
        return pltpu.make_async_copy(blocks.at[b], held.at[b], sems.at[b])

    def begin(b, carry):
        copy(b).start()
        return carry

    def end(b, carry):
        copy(b).wait()
        return carry

    lax.fori_loop(0, held.shape[0], begin, 0)

    def reach(done, b):
        upto = jnp.maximum(done, b + 1)
        lax.fori_loop(done, upto, end, 0)
        return upto

    return reach


def reply_kernel(pairs, stage_in, fa_in, incoming_in, back_out, stage, fa, incoming, back, kbuf, sems, ins, outs):
    peers, rhs, width = back.shape
    first = [
        pltpu.make_async_copy(fa_in, fa, sems.at[0]),
        pltpu.make_async_copy(stage_in, stage, sems.at[1]),
    ]
    for copy in first:
        copy.start()
    reach = fetch(incoming_in, incoming, ins)
    back[...] = jnp.zeros_like(back)
    for copy in first:
        copy.wait()

    def entry(j):
        return unpack(pairs[1, 1 + j])[1]

    def leave(b):
        return pltpu.make_async_copy(back.at[b], back_out.at[b], outs.at[b])

    def begin(b, carry):
        leave(b).start()
        return carry

    def end(b, carry):
        leave(b).wait()
        return carry

    done = reach(0, entry(GROUP - 1))
    for g in range(GROUP):
        kbuf[0, g] = tile(pairs[1, 1 + g], fa, incoming)

    def body(i, carry):
        total, done, sent = carry
        now = lax.rem(i, 2)
        done = reach(done, entry(i * GROUP + 2 * GROUP - 1))
        for g in range(GROUP):
            j = i * GROUP + g
            a, b, _ = unpack(pairs[1, 1 + j])
            keep = jnp.where(entry(jnp.maximum(j - 1, 0)) == b, 1.0, 0.0).astype(F32)
            total = total * keep + dot(stage[a, :rhs], kbuf[now, g])
            back[b] = total.astype(BF16)
            kbuf[1 - now, g] = tile(pairs[1, 1 + j + GROUP], fa, incoming)
        last = entry(i * GROUP + GROUP - 1)
        lax.fori_loop(sent, last, begin, 0)
        return total, done, jnp.maximum(sent, last)

    zero = jnp.zeros((rhs, width), F32)
    _, done, sent = lax.fori_loop(0, pl.cdiv(pairs[1, 0], GROUP), body, (zero, done, 0))
    lax.fori_loop(sent, peers, begin, 0)
    reach(done, peers - 1)
    lax.fori_loop(0, peers, end, 0)


def reply(pairs, stage, fa, incoming):
    peers, rows, width = incoming.shape
    out = jax.ShapeDtypeStruct((peers, rows - FEAT, width), BF16)
    return pl.pallas_call(
        reply_kernel,
        out_shape=out,
        in_specs=[SMEM] + [ANY] * 3,
        out_specs=ANY,
        scratch_shapes=[
            pltpu.VMEM(stage.shape, BF16),
            pltpu.VMEM(fa.shape, BF16),
            pltpu.VMEM(incoming.shape, BF16),
            pltpu.VMEM(out.shape, BF16),
            pltpu.VMEM((2, GROUP, width, width), BF16),
            pltpu.SemaphoreType.DMA((2,)),
            pltpu.SemaphoreType.DMA((peers,)),
            pltpu.SemaphoreType.DMA((peers,)),
        ],
        compiler_params=WIDE,
        cost_estimate=pl.CostEstimate(flops=6 << 30, bytes_accessed=8 << 20, transcendentals=0),
        name="reply",
    )(pairs, stage, fa, incoming)


def rest_kernel(
    pairs, ids, own_points, trans, basis, fa_in, incoming_in, nodes_in, acc_in, base_out,
    fa, incoming, nodes, acc, kbuf, sems, ins, outs,
):
    loads = [
        pltpu.make_async_copy(src, dst, sems.at[i])
        for i, (src, dst) in enumerate(((fa_in, fa), (acc_in, acc), (nodes_in, nodes)))
    ]
    loads[0].start()
    reach = fetch(incoming_in, incoming, ins)
    loads[1].start()
    loads[2].start()
    loads[0].wait()
    rhs = acc.shape[1]

    def entry(j):
        return unpack(pairs[1, 1 + j])[1]

    done = reach(0, entry(GROUP - 1))
    for g in range(GROUP):
        kbuf[0, g] = tile(pairs[1, 1 + g], fa, incoming)
    loads[1].wait()

    def body(i, done):
        now = lax.rem(i, 2)
        done = reach(done, entry(i * GROUP + 2 * GROUP - 1))
        for g in range(GROUP):
            j = 1 + i * GROUP + g
            a, b, _ = unpack(pairs[1, j])
            acc[a] += dot(incoming[b, :rhs], kbuf[now, g], ((1,), (1,)))
            kbuf[1 - now, g] = tile(pairs[1, j + GROUP], fa, incoming)
        return done

    done = lax.fori_loop(0, pl.cdiv(pairs[1, 0], GROUP), body, done)
    reach(done, incoming.shape[0] - 1)
    loads[2].wait()
    rank = 32

    def skel(n):
        rows = nodes[n, :16, :]
        return jnp.concatenate([rows[:, :128], rows[:, 128:]], axis=0)

    def transfer(n, which):
        rows = nodes[n, 16:, 128 * which : 128 * which + 128].astype(F32)
        return jnp.concatenate([rows[:8, 32 * i : 32 * i + 32] for i in range(4)], axis=0).astype(BF16)

    def points(n):
        return nodes[n, 16:, :128].astype(F32)[8:9]

    def kernel_tile(mine, theirs):
        gap = mine - theirs
        sq = gap * gap
        s = ((DELTA * DELTA + sq[:, :32]) + sq[:, 32:64]) + sq[:, 64:96]
        return halves(KCOEF * lax.rsqrt(s))

    def apply(tile, source):
        return dot(tile[0], source) + dot(tile[1], source)

    mine = [own_points[level] for level in range(3)]
    zero = jnp.zeros((rank, 128), F32)

    def one(f, total):
        n = ids[f]
        return total + apply(kernel_tile(mine[0], points(n)), skel(n))

    def two(f, total):
        n, m = ids[8 + f], ids[8 + f] + 64
        source = dot(transfer(n, 0), skel(n)) + dot(transfer(m, 0), skel(m))
        theirs = 0.5 * (points(n) + points(m))
        return total + apply(kernel_tile(mine[1], theirs), source.astype(BF16))

    def three(f, total):
        n = [ids[24 + f] + step for step in (0, 64, 4, 68)]
        terms = [dot(transfer(i, 1), skel(i)) for i in n]
        source = (terms[0] + terms[1]) + (terms[2] + terms[3])
        left = 0.5 * (points(n[0]) + points(n[1]))
        right = 0.5 * (points(n[2]) + points(n[3]))
        return total + apply(kernel_tile(mine[2], 0.5 * (left + right)), source.astype(BF16))

    far_one = lax.fori_loop(0, 8, one, zero, unroll=True)
    far_two = lax.fori_loop(0, 16, two, zero, unroll=4)
    far_three = lax.fori_loop(0, 32, three, zero, unroll=4)
    me = ids[56]

    def down_by(which, value):
        high, low = halves(value)
        mat = transfer(me, which)
        return dot(mat, high, ((0,), (0,))) + dot(mat, low, ((0,), (0,)))

    down = far_one + down_by(0, far_two) + down_by(1, far_three)
    high, low = halves(down.T)

    def leave(c):
        return pltpu.make_async_copy(acc.at[c], base_out.at[c], outs.at[c])

    for c in range(trans.shape[0]):
        leaf = (dot(high, trans[c]) + dot(low, trans[c])).astype(BF16)
        acc[c] = acc[c] * KCOEF + dot(leaf, basis[c])
        leave(c).start()
    for c in range(trans.shape[0]):
        leave(c).wait()


def rest(pairs, ids, own_points, trans, basis, fa, incoming, nodes, acc):
    width = acc.shape[2]
    return pl.pallas_call(
        rest_kernel,
        out_shape=jax.ShapeDtypeStruct(acc.shape, F32),
        in_specs=[SMEM] * 2 + [VMEM] * 3 + [ANY] * 4,
        out_specs=ANY,
        scratch_shapes=[
            pltpu.VMEM(fa.shape, BF16),
            pltpu.VMEM(incoming.shape, BF16),
            pltpu.VMEM(nodes.shape, BF16),
            pltpu.VMEM(acc.shape, F32),
            pltpu.VMEM((2, GROUP, width, width), BF16),
            pltpu.SemaphoreType.DMA((3,)),
            pltpu.SemaphoreType.DMA(incoming.shape[:1]),
            pltpu.SemaphoreType.DMA(acc.shape[:1]),
        ],
        compiler_params=WIDE,
        cost_estimate=pl.CostEstimate(flops=12 << 30, bytes_accessed=8 << 20, transcendentals=0),
        name="rest",
    )(pairs, ids, own_points, trans, basis, fa, incoming, nodes, acc)


def final_kernel(ints, base, returned, out, sums, held, rows, base_sem, ins, outs):
    clusters = base.shape[0]
    load = pltpu.make_async_copy(base, sums, base_sem)
    load.start()
    reach = fetch(returned, held, ins)
    load.wait()

    def collect(h, done):
        done = reach(done, h)
        sums[ints[2, h]] += KCOEF * held[h].astype(F32)
        return done

    lax.fori_loop(0, held.shape[0], collect, 0)

    def leave(c):
        return pltpu.make_async_copy(rows.at[c], out.at[c], outs.at[c])

    for c in range(clusters):
        rows[c] = sums[c].T
        leave(c).start()
    for c in range(clusters):
        leave(c).wait()


def finish(ints, base, returned):
    clusters, rhs, width = base.shape
    return pl.pallas_call(
        final_kernel,
        out_shape=jax.ShapeDtypeStruct((clusters, width, rhs), F32),
        in_specs=[SMEM] + [ANY] * 2,
        out_specs=ANY,
        scratch_shapes=[
            pltpu.VMEM(base.shape, F32),
            pltpu.VMEM(returned.shape, BF16),
            pltpu.VMEM((clusters, width, rhs), F32),
            pltpu.SemaphoreType.DMA,
            pltpu.SemaphoreType.DMA(returned.shape[:1]),
            pltpu.SemaphoreType.DMA((clusters,)),
        ],
        compiler_params=WIDE,
        name="finish",
    )(ints, base, returned)


def shards(
    charges,
    panel_coords,
    cluster_basis,
    trans_leaf,
    trans_pair,
    trans_quad,
    skel_points,
    send_slots,
    pair_first,
    pair_second,
    pair_count,
    far_one,
    far_two,
    far_three,
):
    clusters, _, width = panel_coords.shape
    conductors = charges.shape[1]
    peers = lax.axis_size("dev")
    blocks = charges.reshape(clusters, width, conductors)
    points = jnp.pad(skel_points[0][:, None, :], ((0, 0), (0, 0), (0, width - skel_points.shape[2])))
    axes = jnp.concatenate([jnp.swapaxes(panel_coords, 0, 1), points], axis=1).astype(F32)
    ints = jnp.concatenate([send_slots[:, 0], far_two[0], far_three[0], pair_count])
    ints = jnp.stack([pair_first, pair_second, jnp.pad(ints, (0, 256 - ints.shape[0]))])
    stage, fa, incoming, nodes, lists, acc = exchange(
        ints, ints, blocks, axes, cluster_basis, trans_leaf, trans_pair, trans_quad
    )
    back = reply(lists, stage, fa, incoming)
    returned = lax.all_to_all(back, "dev", split_axis=0, concat_axis=0, tiled=True)

    z, d = lax.axis_index("group"), lax.axis_index("dev")
    x, y = d // 8, d // 2 % 4

    def place(owner):
        z, d = owner // peers, owner % peers
        return ((d % 2 * 4 + z) * 4 + d // 2 % 4) * 4 + d // 8

    quad = lax.dynamic_slice(
        nodes.reshape(2, 4, 4, 4, 32, width), (0, z, y // 2 * 2, x, 24, 0), (2, 1, 2, 1, 1, width)
    )
    quad = jnp.swapaxes(quad.reshape(2, 2, width), 0, 1).reshape(4, width)
    quad_lists = quad[:, 128:144].astype(jnp.int32)
    pair_list = lax.dynamic_slice_in_dim(quad_lists[:, :8], d % 4 // 2 * 2, 2, axis=0)
    ids = jnp.concatenate(
        [
            place(far_one[0]),
            place(2 * pair_list.reshape(-1)),
            place(4 * quad_lists[:, 8:].reshape(-1)),
            place(z * peers + d).reshape(1),
        ]
    )
    quad_points = quad[:, :96].astype(F32).reshape(4, 3, 32)
    pair_points = 0.5 * (quad_points[0::2] + quad_points[1::2])
    own_points = jnp.stack(
        [
            skel_points[0].astype(F32),
            lax.dynamic_index_in_dim(pair_points, d % 4 // 2, axis=0, keepdims=False),
            0.5 * (pair_points[0] + pair_points[1]),
        ]
    )
    own_points = jnp.repeat(jnp.swapaxes(own_points, 1, 2), 32, axis=2)
    own_points = jnp.pad(own_points, ((0, 0), (0, 0), (0, 32)))
    base = rest(lists, ids, own_points, trans_leaf, cluster_basis, fa, incoming, nodes, acc)
    out = finish(ints, base, returned)
    return out.reshape(clusters * width, conductors)


def solution(mesh):
    owners = ("group", "dev")
    rows, block, flat = P(owners, None), P(owners, None, None), P(owners)
    placed = (rows, *(block,) * 6, rows, *(flat,) * 3, *(rows,) * 3)
    return jax.shard_map(shards, mesh=mesh, in_specs=placed, out_specs=rows, check_vma=False)
```

```python
import functools

import jax
import jax.numpy as jnp
from jax import lax
from jax.experimental import pallas as pl
from jax.experimental.pallas import tpu as pltpu
from jax.sharding import PartitionSpec as P

KCOEF = 0.005
DELTA = 0.02
F32 = jnp.float32
BF16 = jnp.bfloat16
GROUP = 8
FEAT = 16
VMEM = pl.BlockSpec(memory_space=pltpu.VMEM)
SMEM = pl.BlockSpec(memory_space=pltpu.SMEM)
ANY = pl.BlockSpec(memory_space=pl.ANY)
MESH = pl.DeviceIdType.MESH
TAIL = 512
SPLIT = (0, 10)
STEPS = tuple((i, j) for i in range(4) for j in range(4) if i or j)
ROUTE = (
    (3, 2, 1), (0, 1, 1), (1, 2, 0), (2, 1, 0), (1, 2, 1), (3, 0, 0), (3, 3, 0), (0, 0, 1),
    (3, 1, 0), (3, 0, 1), (0, 2, 0), (1, 1, 1), (2, 2, 1), (3, 2, 0), (1, 3, 1), (1, 0, 0),
    (3, 3, 1), (2, 0, 1), (1, 3, 0), (2, 3, 0), (3, 1, 1), (2, 2, 0), (1, 0, 1), (0, 3, 0),
    (2, 0, 0), (0, 1, 0), (0, 2, 1), (2, 1, 1), (2, 3, 1), (0, 3, 1), (1, 1, 0),
)
MESH = pl.DeviceIdType.MESH
NARROW = pltpu.CompilerParams(vmem_limit_bytes=12 << 20)
WIDE = pltpu.CompilerParams(vmem_limit_bytes=56 << 20)


def dot(left, right, dims=((1,), (0,))):
    return lax.dot_general(left, right, (dims, ((), ())), preferred_element_type=F32)


def halves(value):
    high = value.astype(BF16)
    return high, (value - high.astype(F32)).astype(BF16)


def thirds(value):
    high = value.astype(BF16)
    rest = value - high.astype(F32)
    mid = rest.astype(BF16)
    return high.astype(F32), mid.astype(F32), (rest - mid.astype(F32))


def pair_lists(first, second, count, lists, weights):
    lane = lax.broadcasted_iota(jnp.int32, first.shape, 1)
    own = second < 16
    a = jnp.where(own, jnp.minimum(first, second), first)
    b = jnp.where(own, jnp.maximum(first, second), second)
    b = jnp.where(lane < count, b, 64)

    def hot(rows, index):
        spot = lax.broadcasted_iota(jnp.int32, (rows, first.shape[1]), 0)
        return jnp.where(spot == index, 1.0, 0.0).astype(BF16)

    times = dot(hot(48, b), hot(16, a), ((1,), (1,)))
    row = lax.broadcasted_iota(jnp.int32, times.shape, 0)
    col = lax.broadcasted_iota(jnp.int32, times.shape, 1)
    held = jnp.where(times > 0, 1.0, 0.0)
    twice = jnp.where(row == col, times, 2.0 * times)
    key = (jnp.where(row < 16, row, row - 16) * 16 + col).astype(F32)
    up_r = lax.broadcasted_iota(jnp.int32, (16, 16), 0)
    up_c = lax.broadcasted_iota(jnp.int32, (16, 16), 1)
    within = dot(held.astype(BF16), jnp.where(up_r < up_c, 1.0, 0.0).astype(BF16))
    low_r = lax.broadcasted_iota(jnp.int32, (48, 48), 0)
    low_c = lax.broadcasted_iota(jnp.int32, (48, 48), 1)
    below = (low_c < low_r) & ((low_c >= 16) | (low_r < 16))
    above = jnp.sum(dot(jnp.where(below, 1.0, 0.0).astype(BF16), held.astype(BF16)), axis=1, keepdims=True)
    rank = jnp.where(held > 0, above + within + 1.0, -1.0)
    value = key + 1024.0 * twice
    slot = lax.broadcasted_iota(jnp.int32, (48, TAIL), 1).astype(F32)
    code = jnp.zeros((48, TAIL), F32)
    for i in range(16):
        code += jnp.where(rank[:, i : i + 1] == slot, value[:, i : i + 1], 0.0)
    for i, (lo, hi) in enumerate(((0, 16), (16, 48))):
        total = jnp.sum(jnp.sum(held[lo:hi], axis=1, keepdims=True), axis=0, keepdims=True)
        last = jnp.max(jnp.max((held * key)[lo:hi], axis=1, keepdims=True), axis=0, keepdims=True)
        mine = jnp.sum(code[lo:hi], axis=0, keepdims=True)
        mine = jnp.where(slot[:1] > total, last, mine)
        lists[i : i + 1] = jnp.where(slot[:1] == 0, total, mine).astype(jnp.int32)
    turned = dot(hot(16, a), hot(48, b), ((1,), (1,)))
    times = turned[:, 16:]
    row = lax.broadcasted_iota(jnp.int32, times.shape, 0)
    col = lax.broadcasted_iota(jnp.int32, times.shape, 1)
    held = jnp.where(times > 0, 1.0, 0.0)
    side_r = lax.broadcasted_iota(jnp.int32, (32, 32), 0)
    side_c = lax.broadcasted_iota(jnp.int32, (32, 32), 1)
    within = dot(held.astype(BF16), jnp.where(side_r < side_c, 1.0, 0.0).astype(BF16))
    above = dot(jnp.where(up_c < up_r, 1.0, 0.0).astype(BF16), held.astype(BF16))
    rank = jnp.where(held > 0, jnp.sum(above, axis=1, keepdims=True) + within + 1.0, -1.0)
    value = (col * 16 + row).astype(F32) + 2048.0 * times
    code = jnp.zeros((16, TAIL), F32)
    for i in range(32):
        code += jnp.where(rank[:, i : i + 1] == slot[:16], value[:, i : i + 1], 0.0)
    total = jnp.sum(jnp.sum(held, axis=1, keepdims=True), axis=0, keepdims=True)
    last = jnp.max(jnp.max(held * row.astype(F32), axis=1, keepdims=True), axis=0, keepdims=True)
    mine = jnp.where(slot[:1] > total, last, jnp.sum(code, axis=0, keepdims=True))
    lists[2:3] = jnp.where(slot[:1] == 0, total, mine).astype(jnp.int32)
    line = lax.broadcasted_iota(jnp.int32, (16, 128), 0)
    for i in range(16):
        part = jnp.broadcast_to(turned[:, i : i + 1], (16, 128))
        weights[i] = jnp.where(line == i, 0.5 * part, part)


def exchange_kernel(
    ints, first, second, charges, axes, basis, trans, pair, quad,
    stage, fa, incoming, nodes, lists, acc,
    rows_a, rows_b, outgoing, weights, kbuf, team_send, team_recv, node_send, node_recv, own_sem,
):
    clusters, _, rhs = charges.shape
    width = stage.shape[2]
    z, d = lax.axis_index("group"), lax.axis_index("dev")
    x, y, c = d // 8, lax.rem(d // 2, 4), lax.rem(d, 2)

    def member(x, y, c):
        return (x * 4 + y) * 2 + c

    def turn(i, k):
        return lax.rem(i + k, 4)

    team = [member(turn(x, i), turn(y, j), lax.rem(c + k, 2)) for i, j, k in ROUTE]
    barrier = pltpu.get_barrier_semaphore()
    for peer in team:
        pl.semaphore_signal(barrier, inc=1, device_id={"group": z, "dev": peer}, device_id_type=MESH)
    for k in (1, 2, 3):
        pl.semaphore_signal(barrier, inc=1, device_id={"group": turn(z, k), "dev": d}, device_id_type=MESH)

    point = [axes[i, :clusters] for i in range(3)]
    norm = point[0] * point[0] + point[1] * point[1] + point[2] * point[2]
    one = jnp.ones_like(norm)
    rows_a[...] = jnp.zeros_like(rows_a)
    rows_b[...] = jnp.zeros_like(rows_b)
    for i, row in enumerate((*point, *thirds(norm + DELTA * DELTA), one, one, one)):
        rows_a[:, i, :] = row
    for i, row in enumerate((*(-2.0 * p for p in point), one, one, one, *thirds(norm))):
        rows_b[:, i, :] = row
    for i in range(clusters):
        stage[i, :rhs] = charges[i].T
        stage[i, rhs:] = rows_b[i].astype(BF16)

    pl.semaphore_wait(barrier, 34)
    sent = []

    def send(i):
        outgoing[i] = stage[ints[team[i]]]
        copy = pltpu.make_async_remote_copy(
            src_ref=outgoing.at[i],
            dst_ref=incoming.at[d],
            send_sem=team_send.at[i],
            recv_sem=team_recv.at[i],
            device_id={"group": z, "dev": team[i]},
            device_id_type=MESH,
        )
        copy.start()
        sent.append(copy)

    for i in range(SPLIT[0]):
        send(i)
    total = jnp.zeros((trans.shape[1], rhs), F32)
    for i in range(clusters):
        leaf = dot(basis[i], charges[i]).astype(BF16)
        total += dot(trans[i], leaf)
    top = total.astype(BF16)
    mats = [mat[0].astype(F32) for mat in (pair, quad)]
    moves = jnp.concatenate([mat[8 * i : 8 * i + 8] for mat in mats for i in range(4)], axis=1)
    lane = lax.broadcasted_iota(jnp.int32, (1, width), 1)
    points = [axes[i, clusters : clusters + 1] for i in range(3)]
    info = points[0] + pltpu.roll(points[1], 32, 1) + pltpu.roll(points[2], 64, 1)
    for i in range(16):
        info = jnp.where(lane == rhs + i, ints[32 + i].astype(F32), info)
    line = lax.broadcasted_iota(jnp.int32, (8, width), 0)
    info = jnp.where(line == 0, jnp.broadcast_to(info, (8, width)), 0.0)
    me = ((c * 4 + z) * 4 + y) * 4 + x
    nodes[me, :16] = jnp.concatenate([top[:16], top[16:]], axis=1)
    nodes[me, 16:] = jnp.concatenate([moves, info], axis=0).astype(BF16)

    def node_copy(start, length, sem, peer):
        held = nodes.at[pl.ds(start, length)]
        return pltpu.make_async_remote_copy(
            src_ref=held,
            dst_ref=held,
            send_sem=node_send.at[sem],
            recv_sem=node_recv.at[sem],
            device_id=peer,
            device_id_type=MESH,
        )

    plane = [
        node_copy(me, 1, i, {"group": z, "dev": member(turn(x, dx), turn(y, dy), c)})
        for i, (dx, dy) in enumerate(STEPS)
    ]
    for copy in plane:
        copy.start()

    for i in range(SPLIT[0], SPLIT[1]):
        send(i)
    for i in range(clusters):
        fa[i] = rows_a[i].T.astype(BF16)
    pair_lists(*(jnp.concatenate([p[:1], p[1:]], axis=1) for p in (first, second)), ints[48], lists, weights)
    for copy in plane:
        copy.wait_recv()
    start = (c * 4 + z) * 16
    along_z = []
    for i in range(SPLIT[1], 31):
        send(i)
        while len(along_z) * (31 - SPLIT[1]) < 12 * (i + 1 - SPLIT[1]):
            part, k = divmod(len(along_z), 3)
            peer = {"group": turn(z, k + 1), "dev": d}
            along_z.append(node_copy(start + part * 4, 4, 15 + len(along_z), peer))
            along_z[-1].start()
    outgoing[31] = stage[ints[d]]
    own = pltpu.make_async_copy(outgoing.at[31], incoming.at[d], own_sem)
    own.start()
    chip = {"group": z, "dev": member(x, y, 1 - c)}
    across = [node_copy(start, 16, 27, chip)]
    across[0].start()

    acc[...] = jnp.zeros_like(acc)

    def entries(i, t):
        low = t <= i
        return jnp.where(low, t, t - i - 1), jnp.where(low, i, 15 - i)

    def near(i, carry):
        for t in range(17):
            a, b = entries(i, t)
            s = dot(fa[a], stage[b, rhs:])
            k = lax.rsqrt(s.astype(BF16))
            line = weights[b, pl.ds(a, 1), :].astype(BF16)
            kbuf[t] = k * jnp.concatenate([line, line], axis=1)
        for t in range(17):
            a, b = entries(i, t)
            acc[a] += dot(stage[b, :rhs], kbuf[t], ((1,), (1,)))
            acc[b] += dot(stage[a, :rhs], kbuf[t])
        return carry

    lax.fori_loop(0, 8, near, 0)

    for k in range(3):
        for part in range(4):
            along_z[part * 3 + k].wait_recv()
        across.append(node_copy((c * 4 + turn(z, 3 - k)) * 16, 16, 28 + k, chip))
        across[-1].start()
    for copy in across:
        copy.wait_recv()
    for copy in sent:
        copy.wait_recv()
    own.wait()
    for copy in (*plane, *along_z, *across, *sent):
        copy.wait_send()


def exchange(ints, first, second, charges, axes, basis, trans, pair, quad):
    clusters, width, rhs = charges.shape
    rows = rhs + FEAT
    return pl.pallas_call(
        exchange_kernel,
        out_shape=(
            jax.ShapeDtypeStruct((clusters, rows, width), BF16),
            jax.ShapeDtypeStruct((clusters, width, FEAT), BF16),
            jax.ShapeDtypeStruct((32, rows, width), BF16),
            jax.ShapeDtypeStruct((128, 32, width), BF16),
            jax.ShapeDtypeStruct((3, TAIL), jnp.int32),
            jax.ShapeDtypeStruct((clusters, rhs, width), F32),
        ),
        in_specs=[SMEM] + [VMEM] * 8,
        out_specs=(VMEM, VMEM, ANY, VMEM, VMEM, VMEM),
        scratch_shapes=[pltpu.VMEM((clusters, FEAT, width), F32)] * 2
        + [
            pltpu.VMEM((32, rows, width), BF16),
            pltpu.VMEM((16, 16, 128), F32),
            pltpu.VMEM((17, width, width), BF16),
            pltpu.SemaphoreType.DMA((31,)),
            pltpu.SemaphoreType.DMA((31,)),
            pltpu.SemaphoreType.DMA((31,)),
            pltpu.SemaphoreType.DMA((31,)),
            pltpu.SemaphoreType.DMA,
        ],
        compiler_params=pltpu.CompilerParams(
            vmem_limit_bytes=56 << 20, collective_id=0, has_side_effects=True
        ),
        name="exchange",
    )(ints, first, second, charges, axes, basis, trans, pair, quad)


def unpack(code):
    return code & 15, (code >> 4) & 63, (code >> 10).astype(F32) * 0.5


def tile(code, fa, table):
    a, b, times = unpack(code)
    s = dot(fa[a], table[b, table.shape[1] - FEAT :])
    return lax.rsqrt(s.astype(BF16)) * times.astype(BF16)


def fetch(blocks, held, sems):
    def copy(b):
        return pltpu.make_async_copy(blocks.at[b], held.at[b], sems.at[b])

    def begin(b, carry):
        copy(b).start()
        return carry

    def end(b, carry):
        copy(b).wait()
        return carry

    lax.fori_loop(0, held.shape[0], begin, 0)

    def reach(done, b):
        upto = jnp.maximum(done, b + 1)
        lax.fori_loop(done, upto, end, 0)
        return upto

    return reach


def reply_kernel(pairs, stage_in, fa_in, incoming_in, back_out, stage, fa, incoming, back, kbuf, sems, ins, outs):
    peers, rhs, width = back.shape
    first = [
        pltpu.make_async_copy(fa_in, fa, sems.at[0]),
        pltpu.make_async_copy(stage_in, stage, sems.at[1]),
    ]
    for copy in first:
        copy.start()
    reach = fetch(incoming_in, incoming, ins)
    back[...] = jnp.zeros_like(back)
    for copy in first:
        copy.wait()

    def entry(j):
        return unpack(pairs[1, 1 + j])[1]

    def leave(b):
        return pltpu.make_async_copy(back.at[b], back_out.at[b], outs.at[b])

    def begin(b, carry):
        leave(b).start()
        return carry

    def end(b, carry):
        leave(b).wait()
        return carry

    done = reach(0, entry(GROUP - 1))
    for g in range(GROUP):
        kbuf[0, g] = tile(pairs[1, 1 + g], fa, incoming)

    def body(i, carry):
        total, done, sent = carry
        now = lax.rem(i, 2)
        done = reach(done, entry(i * GROUP + 2 * GROUP - 1))
        for g in range(GROUP):
            j = i * GROUP + g
            a, b, _ = unpack(pairs[1, 1 + j])
            keep = jnp.where(entry(jnp.maximum(j - 1, 0)) == b, 1.0, 0.0).astype(F32)
            total = total * keep + dot(stage[a, :rhs], kbuf[now, g])
            back[b] = total.astype(BF16)
            kbuf[1 - now, g] = tile(pairs[1, 1 + j + GROUP], fa, incoming)
        last = entry(i * GROUP + GROUP - 1)
        lax.fori_loop(sent, last, begin, 0)
        return total, done, jnp.maximum(sent, last)

    zero = jnp.zeros((rhs, width), F32)
    _, done, sent = lax.fori_loop(0, pl.cdiv(pairs[1, 0], GROUP), body, (zero, done, 0))
    lax.fori_loop(sent, peers, begin, 0)
    reach(done, peers - 1)
    lax.fori_loop(0, peers, end, 0)


def reply(pairs, stage, fa, incoming):
    peers, rows, width = incoming.shape
    out = jax.ShapeDtypeStruct((peers, rows - FEAT, width), BF16)
    return pl.pallas_call(
        reply_kernel,
        out_shape=out,
        in_specs=[SMEM] + [ANY] * 3,
        out_specs=ANY,
        scratch_shapes=[
            pltpu.VMEM(stage.shape, BF16),
            pltpu.VMEM(fa.shape, BF16),
            pltpu.VMEM(incoming.shape, BF16),
            pltpu.VMEM(out.shape, BF16),
            pltpu.VMEM((2, GROUP, width, width), BF16),
            pltpu.SemaphoreType.DMA((2,)),
            pltpu.SemaphoreType.DMA((peers,)),
            pltpu.SemaphoreType.DMA((peers,)),
        ],
        compiler_params=WIDE,
        cost_estimate=pl.CostEstimate(flops=6 << 30, bytes_accessed=8 << 20, transcendentals=0),
        name="reply",
    )(pairs, stage, fa, incoming)


def rest_kernel(
    pairs, ids, own_points, trans, basis, fa_in, incoming_in, nodes_in, acc_in, base_out,
    fa, incoming, nodes, own, acc, kbuf, sems, outs,
):
    loads = [
        pltpu.make_async_copy(src, dst, sems.at[i])
        for i, (src, dst) in enumerate(
            ((fa_in, fa), (incoming_in, incoming), (acc_in, own), (acc_in, acc), (nodes_in, nodes))
        )
    ]
    for load in loads:
        load.start()
    loads[0].wait()
    loads[1].wait()
    rhs, width = acc.shape[1:]
    for g in range(GROUP):
        kbuf[0, g] = tile(pairs[2, 1 + g], fa, incoming)
    loads[2].wait()
    loads[3].wait()

    def body(i, total):
        now = lax.rem(i, 2)
        for g in range(GROUP):
            j = 1 + i * GROUP + g
            a, b, _ = unpack(pairs[2, j])
            before = unpack(pairs[2, jnp.maximum(j - 1, 1)])[0]
            keep = jnp.where(before == a, 1.0, 0.0).astype(F32)
            total = total * keep + dot(incoming[b, :rhs], kbuf[now, g], ((1,), (1,)))
            acc[a] = own[a] + total
            kbuf[1 - now, g] = tile(pairs[2, j + GROUP], fa, incoming)
        return total

    lax.fori_loop(0, pl.cdiv(pairs[2, 0], GROUP), body, jnp.zeros((rhs, width), F32))
    loads[4].wait()
    rank = 32

    def skel(n):
        rows = nodes[n, :16, :]
        return jnp.concatenate([rows[:, :128], rows[:, 128:]], axis=0)

    def transfer(n, which):
        rows = nodes[n, 16:, 128 * which : 128 * which + 128].astype(F32)
        return jnp.concatenate([rows[:8, 32 * i : 32 * i + 32] for i in range(4)], axis=0).astype(BF16)

    def points(n):
        return nodes[n, 16:, :128].astype(F32)[8:9]

    def kernel_tile(mine, theirs):
        gap = mine - theirs
        sq = gap * gap
        s = ((DELTA * DELTA + sq[:, :32]) + sq[:, 32:64]) + sq[:, 64:96]
        return halves(KCOEF * lax.rsqrt(s))

    def apply(tile, source):
        return dot(tile[0], source) + dot(tile[1], source)

    mine = [own_points[level] for level in range(3)]
    zero = jnp.zeros((rank, 128), F32)

    def one(f, total):
        n = ids[f]
        return total + apply(kernel_tile(mine[0], points(n)), skel(n))

    def two(f, total):
        n, m = ids[8 + f], ids[8 + f] + 64
        source = dot(transfer(n, 0), skel(n)) + dot(transfer(m, 0), skel(m))
        theirs = 0.5 * (points(n) + points(m))
        return total + apply(kernel_tile(mine[1], theirs), source.astype(BF16))

    def three(f, total):
        n = [ids[24 + f] + step for step in (0, 64, 4, 68)]
        terms = [dot(transfer(i, 1), skel(i)) for i in n]
        source = (terms[0] + terms[1]) + (terms[2] + terms[3])
        left = 0.5 * (points(n[0]) + points(n[1]))
        right = 0.5 * (points(n[2]) + points(n[3]))
        return total + apply(kernel_tile(mine[2], 0.5 * (left + right)), source.astype(BF16))

    far_one = lax.fori_loop(0, 8, one, zero, unroll=True)
    far_two = lax.fori_loop(0, 16, two, zero, unroll=8)
    far_three = lax.fori_loop(0, 32, three, zero, unroll=8)
    me = ids[56]

    def down_by(which, value):
        high, low = halves(value)
        mat = transfer(me, which)
        return dot(mat, high, ((0,), (0,))) + dot(mat, low, ((0,), (0,)))

    down = far_one + down_by(0, far_two) + down_by(1, far_three)
    high, low = halves(down.T)

    def leave(c):
        return pltpu.make_async_copy(acc.at[c], base_out.at[c], outs.at[c])

    for c in range(trans.shape[0]):
        leaf = (dot(high, trans[c]) + dot(low, trans[c])).astype(BF16)
        acc[c] = acc[c] * KCOEF + dot(leaf, basis[c])
        leave(c).start()
    for c in range(trans.shape[0]):
        leave(c).wait()


def rest(pairs, ids, own_points, trans, basis, fa, incoming, nodes, acc):
    width = acc.shape[2]
    return pl.pallas_call(
        rest_kernel,
        out_shape=jax.ShapeDtypeStruct(acc.shape, F32),
        in_specs=[SMEM] * 2 + [VMEM] * 3 + [ANY] * 4,
        out_specs=ANY,
        scratch_shapes=[
            pltpu.VMEM(fa.shape, BF16),
            pltpu.VMEM(incoming.shape, BF16),
            pltpu.VMEM(nodes.shape, BF16),
            pltpu.VMEM(acc.shape, F32),
            pltpu.VMEM(acc.shape, F32),
            pltpu.VMEM((2, GROUP, width, width), BF16),
            pltpu.SemaphoreType.DMA((5,)),
            pltpu.SemaphoreType.DMA(acc.shape[:1]),
        ],
        compiler_params=WIDE,
        cost_estimate=pl.CostEstimate(flops=12 << 30, bytes_accessed=8 << 20, transcendentals=0),
        name="rest",
    )(pairs, ids, own_points, trans, basis, fa, incoming, nodes, acc)


def final_kernel(ints, base, returned, out, sums, rows, base_sem, outs):
    clusters = base.shape[0]
    load = pltpu.make_async_copy(base, sums, base_sem)
    load.start()
    load.wait()

    def collect(h, carry):
        sums[ints[h]] += KCOEF * returned[h].astype(F32)
        return carry

    lax.fori_loop(0, returned.shape[0], collect, 0)

    def leave(c):
        return pltpu.make_async_copy(rows.at[c], out.at[c], outs.at[c])

    for c in range(clusters):
        rows[c] = sums[c].T
        leave(c).start()
    for c in range(clusters):
        leave(c).wait()


def finish(ints, base, returned):
    clusters, rhs, width = base.shape
    return pl.pallas_call(
        final_kernel,
        out_shape=jax.ShapeDtypeStruct((clusters, width, rhs), F32),
        in_specs=[SMEM, ANY, VMEM],
        out_specs=ANY,
        scratch_shapes=[
            pltpu.VMEM(base.shape, F32),
            pltpu.VMEM((clusters, width, rhs), F32),
            pltpu.SemaphoreType.DMA,
            pltpu.SemaphoreType.DMA((clusters,)),
        ],
        compiler_params=NARROW,
        name="finish",
    )(ints, base, returned)


def shards(
    charges,
    panel_coords,
    cluster_basis,
    trans_leaf,
    trans_pair,
    trans_quad,
    skel_points,
    send_slots,
    pair_first,
    pair_second,
    pair_count,
    far_one,
    far_two,
    far_three,
):
    clusters, _, width = panel_coords.shape
    conductors = charges.shape[1]
    peers = lax.axis_size("dev")
    blocks = charges.reshape(clusters, width, conductors)
    points = jnp.pad(skel_points[0][:, None, :], ((0, 0), (0, 0), (0, width - skel_points.shape[2])))
    axes = jnp.concatenate([jnp.swapaxes(panel_coords, 0, 1), points], axis=1).astype(F32)
    ints = jnp.concatenate([send_slots[:, 0], far_two[0], far_three[0], pair_count])
    stage, fa, incoming, nodes, lists, acc = exchange(
        ints, pair_first.reshape(2, 128), pair_second.reshape(2, 128), blocks, axes,
        cluster_basis, trans_leaf, trans_pair, trans_quad,
    )
    back = reply(lists, stage, fa, incoming)
    returned = lax.all_to_all(back, "dev", split_axis=0, concat_axis=0, tiled=True)

    z, d = lax.axis_index("group"), lax.axis_index("dev")
    x, y = d // 8, d // 2 % 4

    def place(owner):
        z, d = owner // peers, owner % peers
        return ((d % 2 * 4 + z) * 4 + d // 2 % 4) * 4 + d // 8

    quad = lax.dynamic_slice(
        nodes.reshape(2, 4, 4, 4, 32, width), (0, z, y // 2 * 2, x, 24, 0), (2, 1, 2, 1, 1, width)
    )
    quad = jnp.swapaxes(quad.reshape(2, 2, width), 0, 1).reshape(4, width)
    quad_lists = quad[:, 128:144].astype(jnp.int32)
    pair_list = lax.dynamic_slice_in_dim(quad_lists[:, :8], d % 4 // 2 * 2, 2, axis=0)
    ids = jnp.concatenate(
        [
            place(far_one[0]),
            place(2 * pair_list.reshape(-1)),
            place(4 * quad_lists[:, 8:].reshape(-1)),
            place(z * peers + d).reshape(1),
        ]
    )
    quad_points = quad[:, :96].astype(F32).reshape(4, 3, 32)
    pair_points = 0.5 * (quad_points[0::2] + quad_points[1::2])
    own_points = jnp.stack(
        [
            skel_points[0].astype(F32),
            lax.dynamic_index_in_dim(pair_points, d % 4 // 2, axis=0, keepdims=False),
            0.5 * (pair_points[0] + pair_points[1]),
        ]
    )
    own_points = jnp.repeat(jnp.swapaxes(own_points, 1, 2), 32, axis=2)
    own_points = jnp.pad(own_points, ((0, 0), (0, 0), (0, 32)))
    base = rest(lists, ids, own_points, trans_leaf, cluster_basis, fa, incoming, nodes, acc)
    out = finish(ints, base, returned)
    return out.reshape(clusters * width, conductors)


def solution(mesh):
    owners = ("group", "dev")
    rows, block, flat = P(owners, None), P(owners, None, None), P(owners)
    placed = (rows, *(block,) * 6, rows, *(flat,) * 3, *(rows,) * 3)
    return jax.shard_map(shards, mesh=mesh, in_specs=placed, out_specs=rows, check_vma=False)
```

```python
import functools

import jax
import jax.numpy as jnp
from jax import lax
from jax.experimental import pallas as pl
from jax.experimental.pallas import tpu as pltpu
from jax.sharding import PartitionSpec as P

KCOEF = 0.005
DELTA = 0.02
F32 = jnp.float32
BF16 = jnp.bfloat16
GROUP = 8
FEAT = 16
VMEM = pl.BlockSpec(memory_space=pltpu.VMEM)
SMEM = pl.BlockSpec(memory_space=pltpu.SMEM)
ANY = pl.BlockSpec(memory_space=pl.ANY)
MESH = pl.DeviceIdType.MESH
TAIL = 512
SPLIT = (0, 10)
STEPS = tuple((i, j) for i in range(4) for j in range(4) if i or j)
ROUTE = (
    (3, 2, 1), (0, 1, 1), (1, 2, 0), (2, 1, 0), (1, 2, 1), (3, 0, 0), (3, 3, 0), (0, 0, 1),
    (3, 1, 0), (3, 0, 1), (0, 2, 0), (1, 1, 1), (2, 2, 1), (3, 2, 0), (1, 3, 1), (1, 0, 0),
    (3, 3, 1), (2, 0, 1), (1, 3, 0), (2, 3, 0), (3, 1, 1), (2, 2, 0), (1, 0, 1), (0, 3, 0),
    (2, 0, 0), (0, 1, 0), (0, 2, 1), (2, 1, 1), (2, 3, 1), (0, 3, 1), (1, 1, 0),
)
MESH = pl.DeviceIdType.MESH
FINAL = pltpu.CompilerParams(vmem_limit_bytes=57 << 20)
WIDE = pltpu.CompilerParams(vmem_limit_bytes=56 << 20)


def dot(left, right, dims=((1,), (0,))):
    return lax.dot_general(left, right, (dims, ((), ())), preferred_element_type=F32)


def halves(value):
    high = value.astype(BF16)
    return high, (value - high.astype(F32)).astype(BF16)


def thirds(value):
    high = value.astype(BF16)
    rest = value - high.astype(F32)
    mid = rest.astype(BF16)
    return high.astype(F32), mid.astype(F32), (rest - mid.astype(F32))


def pair_lists(first, second, count, lists, weights):
    lane = lax.broadcasted_iota(jnp.int32, first.shape, 1)
    own = second < 16
    a = jnp.where(own, jnp.minimum(first, second), first)
    b = jnp.where(own, jnp.maximum(first, second), second)
    b = jnp.where(lane < count, b, 64)

    def hot(rows, index):
        spot = lax.broadcasted_iota(jnp.int32, (rows, first.shape[1]), 0)
        return jnp.where(spot == index, 1.0, 0.0).astype(BF16)

    times = dot(hot(48, b), hot(16, a), ((1,), (1,)))
    row = lax.broadcasted_iota(jnp.int32, times.shape, 0)
    col = lax.broadcasted_iota(jnp.int32, times.shape, 1)
    held = jnp.where(times > 0, 1.0, 0.0)
    twice = jnp.where(row == col, times, 2.0 * times)
    key = (jnp.where(row < 16, row, row - 16) * 16 + col).astype(F32)
    up_r = lax.broadcasted_iota(jnp.int32, (16, 16), 0)
    up_c = lax.broadcasted_iota(jnp.int32, (16, 16), 1)
    within = dot(held.astype(BF16), jnp.where(up_r < up_c, 1.0, 0.0).astype(BF16))
    low_r = lax.broadcasted_iota(jnp.int32, (48, 48), 0)
    low_c = lax.broadcasted_iota(jnp.int32, (48, 48), 1)
    below = (low_c < low_r) & ((low_c >= 16) | (low_r < 16))
    above = jnp.sum(dot(jnp.where(below, 1.0, 0.0).astype(BF16), held.astype(BF16)), axis=1, keepdims=True)
    rank = jnp.where(held > 0, above + within + 1.0, -1.0)
    value = key + 1024.0 * twice
    slot = lax.broadcasted_iota(jnp.int32, (48, TAIL), 1).astype(F32)
    code = jnp.zeros((48, TAIL), F32)
    for i in range(16):
        code += jnp.where(rank[:, i : i + 1] == slot, value[:, i : i + 1], 0.0)
    for i, (lo, hi) in enumerate(((0, 16), (16, 48))):
        total = jnp.sum(jnp.sum(held[lo:hi], axis=1, keepdims=True), axis=0, keepdims=True)
        last = jnp.max(jnp.max((held * key)[lo:hi], axis=1, keepdims=True), axis=0, keepdims=True)
        mine = jnp.sum(code[lo:hi], axis=0, keepdims=True)
        mine = jnp.where(slot[:1] > total, last, mine)
        lists[i : i + 1] = jnp.where(slot[:1] == 0, total, mine).astype(jnp.int32)
    turned = dot(hot(16, a), hot(48, b), ((1,), (1,)))
    times = turned[:, 16:]
    row = lax.broadcasted_iota(jnp.int32, times.shape, 0)
    col = lax.broadcasted_iota(jnp.int32, times.shape, 1)
    held = jnp.where(times > 0, 1.0, 0.0)
    side_r = lax.broadcasted_iota(jnp.int32, (32, 32), 0)
    side_c = lax.broadcasted_iota(jnp.int32, (32, 32), 1)
    within = dot(held.astype(BF16), jnp.where(side_r < side_c, 1.0, 0.0).astype(BF16))
    above = dot(jnp.where(up_c < up_r, 1.0, 0.0).astype(BF16), held.astype(BF16))
    rank = jnp.where(held > 0, jnp.sum(above, axis=1, keepdims=True) + within + 1.0, -1.0)
    value = (col * 16 + row).astype(F32) + 2048.0 * times
    code = jnp.zeros((16, TAIL), F32)
    for i in range(32):
        code += jnp.where(rank[:, i : i + 1] == slot[:16], value[:, i : i + 1], 0.0)
    total = jnp.sum(jnp.sum(held, axis=1, keepdims=True), axis=0, keepdims=True)
    last = jnp.max(jnp.max(held * row.astype(F32), axis=1, keepdims=True), axis=0, keepdims=True)
    mine = jnp.where(slot[:1] > total, last, jnp.sum(code, axis=0, keepdims=True))
    lists[2:3] = jnp.where(slot[:1] == 0, total, mine).astype(jnp.int32)
    line = lax.broadcasted_iota(jnp.int32, (16, 128), 0)
    for i in range(16):
        part = jnp.broadcast_to(turned[:, i : i + 1], (16, 128))
        weights[i] = jnp.where(line == i, 0.5 * part, part)


def exchange_kernel(
    slots, pair_far, quad_far, count, first, second, points, charges, axes, basis, trans, pair, quad,
    stage, fa, incoming, nodes, lists, acc,
    rows_a, rows_b, outgoing, weights, kbuf, team_send, team_recv, node_send, node_recv, own_sem,
):
    clusters, _, rhs = charges.shape
    width = stage.shape[2]
    z, d = lax.axis_index("group"), lax.axis_index("dev")
    x, y, c = d // 8, lax.rem(d // 2, 4), lax.rem(d, 2)

    def member(x, y, c):
        return (x * 4 + y) * 2 + c

    def turn(i, k):
        return lax.rem(i + k, 4)

    team = [member(turn(x, i), turn(y, j), lax.rem(c + k, 2)) for i, j, k in ROUTE]
    barrier = pltpu.get_barrier_semaphore()
    for peer in team:
        pl.semaphore_signal(barrier, inc=1, device_id={"group": z, "dev": peer}, device_id_type=MESH)
    for k in (1, 2, 3):
        pl.semaphore_signal(barrier, inc=1, device_id={"group": turn(z, k), "dev": d}, device_id_type=MESH)

    point = [axes[i] for i in range(3)]
    norm = point[0] * point[0] + point[1] * point[1] + point[2] * point[2]
    one = jnp.ones_like(norm)
    rows_a[...] = jnp.zeros_like(rows_a)
    rows_b[...] = jnp.zeros_like(rows_b)
    for i, row in enumerate((*point, *thirds(norm + DELTA * DELTA), one, one, one)):
        rows_a[:, i, :] = row
    for i, row in enumerate((*(-2.0 * p for p in point), one, one, one, *thirds(norm))):
        rows_b[:, i, :] = row
    for i in range(clusters):
        stage[i, :rhs] = charges[i].T
        stage[i, rhs:] = rows_b[i].astype(BF16)

    pl.semaphore_wait(barrier, 34)
    sent = []

    def send(i):
        outgoing[i] = stage[slots[team[i]]]
        copy = pltpu.make_async_remote_copy(
            src_ref=outgoing.at[i],
            dst_ref=incoming.at[d],
            send_sem=team_send.at[i],
            recv_sem=team_recv.at[i],
            device_id={"group": z, "dev": team[i]},
            device_id_type=MESH,
        )
        copy.start()
        sent.append(copy)

    for i in range(SPLIT[0]):
        send(i)
    total = jnp.zeros((trans.shape[1], rhs), F32)
    for i in range(clusters):
        leaf = dot(basis[i], charges[i]).astype(BF16)
        total += dot(trans[i], leaf)
    top = total.astype(BF16)
    mats = [mat[0].astype(F32) for mat in (pair, quad)]
    moves = jnp.concatenate([mat[8 * i : 8 * i + 8] for mat in mats for i in range(4)], axis=1)
    lane = lax.broadcasted_iota(jnp.int32, (1, width), 1)
    info = jnp.concatenate([points[i : i + 1] for i in range(3)] + [jnp.zeros((1, width - 96), F32)], axis=1)
    for i in range(8):
        info = jnp.where(lane == rhs + i, pair_far[i].astype(F32), info)
        info = jnp.where(lane == rhs + 8 + i, quad_far[i].astype(F32), info)
    line = lax.broadcasted_iota(jnp.int32, (8, width), 0)
    info = jnp.where(line == 0, jnp.broadcast_to(info, (8, width)), 0.0)
    me = ((c * 4 + z) * 4 + y) * 4 + x
    nodes[me, :16] = jnp.concatenate([top[:16], top[16:]], axis=1)
    nodes[me, 16:] = jnp.concatenate([moves, info], axis=0).astype(BF16)

    def node_copy(start, length, sem, peer):
        held = nodes.at[pl.ds(start, length)]
        return pltpu.make_async_remote_copy(
            src_ref=held,
            dst_ref=held,
            send_sem=node_send.at[sem],
            recv_sem=node_recv.at[sem],
            device_id=peer,
            device_id_type=MESH,
        )

    plane = [
        node_copy(me, 1, i, {"group": z, "dev": member(turn(x, dx), turn(y, dy), c)})
        for i, (dx, dy) in enumerate(STEPS)
    ]
    for copy in plane:
        copy.start()

    for i in range(SPLIT[0], SPLIT[1]):
        send(i)
    for i in range(clusters):
        fa[i] = rows_a[i].T.astype(BF16)
    pair_lists(*(jnp.concatenate([p[:1], p[1:]], axis=1) for p in (first, second)), count[0], lists, weights)
    for copy in plane:
        copy.wait_recv()
    start = (c * 4 + z) * 16
    along_z = []
    for i in range(SPLIT[1], 31):
        send(i)
        while len(along_z) * (31 - SPLIT[1]) < 12 * (i + 1 - SPLIT[1]):
            part, k = divmod(len(along_z), 3)
            peer = {"group": turn(z, k + 1), "dev": d}
            along_z.append(node_copy(start + part * 4, 4, 15 + len(along_z), peer))
            along_z[-1].start()
    outgoing[31] = stage[slots[d]]
    own = pltpu.make_async_copy(outgoing.at[31], incoming.at[d], own_sem)
    own.start()
    chip = {"group": z, "dev": member(x, y, 1 - c)}
    across = [node_copy(start, 16, 27, chip)]
    across[0].start()

    acc[...] = jnp.zeros_like(acc)

    def entries(i, t):
        low = t <= i
        return jnp.where(low, t, t - i - 1), jnp.where(low, i, 15 - i)

    def near(i, carry):
        for t in range(17):
            a, b = entries(i, t)
            s = dot(fa[a], stage[b, rhs:])
            k = lax.rsqrt(s.astype(BF16))
            line = weights[b, pl.ds(a, 1), :].astype(BF16)
            kbuf[t] = k * jnp.concatenate([line, line], axis=1)
        for t in range(17):
            a, b = entries(i, t)
            acc[a] += dot(stage[b, :rhs], kbuf[t], ((1,), (1,)))
            acc[b] += dot(stage[a, :rhs], kbuf[t])
        return carry

    lax.fori_loop(0, 8, near, 0)

    for k in range(3):
        for part in range(4):
            along_z[part * 3 + k].wait_recv()
        across.append(node_copy((c * 4 + turn(z, 3 - k)) * 16, 16, 28 + k, chip))
        across[-1].start()
    for copy in across:
        copy.wait_recv()
    for copy in sent:
        copy.wait_recv()
    own.wait()
    for copy in (*plane, *along_z, *across, *sent):
        copy.wait_send()


def exchange(slots, pair_far, quad_far, count, first, second, points, charges, axes, basis, trans, pair, quad):
    clusters, width, rhs = charges.shape
    rows = rhs + FEAT
    return pl.pallas_call(
        exchange_kernel,
        out_shape=(
            jax.ShapeDtypeStruct((clusters, rows, width), BF16),
            jax.ShapeDtypeStruct((clusters, width, FEAT), BF16),
            jax.ShapeDtypeStruct((32, rows, width), BF16),
            jax.ShapeDtypeStruct((128, 32, width), BF16),
            jax.ShapeDtypeStruct((3, TAIL), jnp.int32),
            jax.ShapeDtypeStruct((clusters, rhs, width), F32),
        ),
        in_specs=[SMEM] * 4 + [VMEM] * 9,
        out_specs=(VMEM, VMEM, ANY, VMEM, VMEM, VMEM),
        scratch_shapes=[pltpu.VMEM((clusters, FEAT, width), F32)] * 2
        + [
            pltpu.VMEM((32, rows, width), BF16),
            pltpu.VMEM((16, 16, 128), F32),
            pltpu.VMEM((17, width, width), BF16),
            pltpu.SemaphoreType.DMA((31,)),
            pltpu.SemaphoreType.DMA((31,)),
            pltpu.SemaphoreType.DMA((31,)),
            pltpu.SemaphoreType.DMA((31,)),
            pltpu.SemaphoreType.DMA,
        ],
        compiler_params=pltpu.CompilerParams(
            vmem_limit_bytes=56 << 20, collective_id=0, has_side_effects=True
        ),
        name="exchange",
    )(slots, pair_far, quad_far, count, first, second, points, charges, axes, basis, trans, pair, quad)


def unpack(code):
    return code & 15, (code >> 4) & 63, (code >> 10).astype(F32) * 0.5


def tile(code, fa, table):
    a, b, times = unpack(code)
    s = dot(fa[a], table[b, table.shape[1] - FEAT :])
    return lax.rsqrt(s.astype(BF16)) * times.astype(BF16)


def fetch(blocks, held, sems):
    def copy(b):
        return pltpu.make_async_copy(blocks.at[b], held.at[b], sems.at[b])

    def begin(b, carry):
        copy(b).start()
        return carry

    def end(b, carry):
        copy(b).wait()
        return carry

    lax.fori_loop(0, held.shape[0], begin, 0)

    def reach(done, b):
        upto = jnp.maximum(done, b + 1)
        lax.fori_loop(done, upto, end, 0)
        return upto

    return reach


def reply_kernel(pairs, stage_in, fa_in, incoming_in, back_out, stage, fa, incoming, back, kbuf, sems, ins, outs):
    peers, rhs, width = back.shape
    first = [
        pltpu.make_async_copy(fa_in, fa, sems.at[0]),
        pltpu.make_async_copy(stage_in, stage, sems.at[1]),
    ]
    for copy in first:
        copy.start()
    reach = fetch(incoming_in, incoming, ins)
    back[...] = jnp.zeros_like(back)
    for copy in first:
        copy.wait()

    def entry(j):
        return unpack(pairs[1, 1 + j])[1]

    def leave(b):
        return pltpu.make_async_copy(back.at[b], back_out.at[b], outs.at[b])

    def begin(b, carry):
        leave(b).start()
        return carry

    def end(b, carry):
        leave(b).wait()
        return carry

    done = reach(0, entry(GROUP - 1))
    for g in range(GROUP):
        kbuf[0, g] = tile(pairs[1, 1 + g], fa, incoming)

    def body(i, carry):
        total, done, sent = carry
        now = lax.rem(i, 2)
        done = reach(done, entry(i * GROUP + 2 * GROUP - 1))
        for g in range(GROUP):
            j = i * GROUP + g
            a, b, _ = unpack(pairs[1, 1 + j])
            keep = jnp.where(entry(jnp.maximum(j - 1, 0)) == b, 1.0, 0.0).astype(F32)
            total = total * keep + dot(stage[a, :rhs], kbuf[now, g])
            back[b] = total.astype(BF16)
            kbuf[1 - now, g] = tile(pairs[1, 1 + j + GROUP], fa, incoming)
        last = entry(i * GROUP + GROUP - 1)
        lax.fori_loop(sent, last, begin, 0)
        return total, done, jnp.maximum(sent, last)

    zero = jnp.zeros((rhs, width), F32)
    _, done, sent = lax.fori_loop(0, pl.cdiv(pairs[1, 0], GROUP), body, (zero, done, 0))
    lax.fori_loop(sent, peers, begin, 0)
    reach(done, peers - 1)
    lax.fori_loop(0, peers, end, 0)


def reply(pairs, stage, fa, incoming):
    peers, rows, width = incoming.shape
    out = jax.ShapeDtypeStruct((peers, rows - FEAT, width), BF16)
    return pl.pallas_call(
        reply_kernel,
        out_shape=out,
        in_specs=[SMEM] + [ANY] * 3,
        out_specs=ANY,
        scratch_shapes=[
            pltpu.VMEM(stage.shape, BF16),
            pltpu.VMEM(fa.shape, BF16),
            pltpu.VMEM(incoming.shape, BF16),
            pltpu.VMEM(out.shape, BF16),
            pltpu.VMEM((2, GROUP, width, width), BF16),
            pltpu.SemaphoreType.DMA((2,)),
            pltpu.SemaphoreType.DMA((peers,)),
            pltpu.SemaphoreType.DMA((peers,)),
        ],
        compiler_params=WIDE,
        cost_estimate=pl.CostEstimate(flops=6 << 30, bytes_accessed=8 << 20, transcendentals=0),
        name="reply",
    )(pairs, stage, fa, incoming)


def rest_kernel(
    pairs, ids, own_points, trans, basis, fa_in, incoming_in, nodes_in, acc_in, base_out,
    fa, incoming, nodes, own, acc, kbuf, sems, outs,
):
    loads = [
        pltpu.make_async_copy(src, dst, sems.at[i])
        for i, (src, dst) in enumerate(
            ((fa_in, fa), (incoming_in, incoming), (acc_in, own), (acc_in, acc), (nodes_in, nodes))
        )
    ]
    for load in loads:
        load.start()
    loads[0].wait()
    loads[1].wait()
    rhs, width = acc.shape[1:]
    for g in range(GROUP):
        kbuf[0, g] = tile(pairs[2, 1 + g], fa, incoming)
    loads[2].wait()
    loads[3].wait()

    def body(i, total):
        now = lax.rem(i, 2)
        for g in range(GROUP):
            j = 1 + i * GROUP + g
            a, b, _ = unpack(pairs[2, j])
            before = unpack(pairs[2, jnp.maximum(j - 1, 1)])[0]
            keep = jnp.where(before == a, 1.0, 0.0).astype(F32)
            total = total * keep + dot(incoming[b, :rhs], kbuf[now, g], ((1,), (1,)))
            acc[a] = own[a] + total
            kbuf[1 - now, g] = tile(pairs[2, j + GROUP], fa, incoming)
        return total

    lax.fori_loop(0, pl.cdiv(pairs[2, 0], GROUP), body, jnp.zeros((rhs, width), F32))
    loads[4].wait()
    rank = 32

    def skel(n):
        rows = nodes[n, :16, :]
        return jnp.concatenate([rows[:, :128], rows[:, 128:]], axis=0)

    def transfer(n, which):
        rows = nodes[n, 16:, 128 * which : 128 * which + 128].astype(F32)
        return jnp.concatenate([rows[:8, 32 * i : 32 * i + 32] for i in range(4)], axis=0).astype(BF16)

    def points(n):
        return nodes[n, 16:, :128].astype(F32)[8:9]

    def kernel_tile(mine, theirs):
        gap = mine - theirs
        sq = gap * gap
        s = ((DELTA * DELTA + sq[:, :32]) + sq[:, 32:64]) + sq[:, 64:96]
        return halves(KCOEF * lax.rsqrt(s))

    def apply(tile, source):
        return dot(tile[0], source) + dot(tile[1], source)

    mine = [own_points[level] for level in range(3)]
    zero = jnp.zeros((rank, 128), F32)

    def one(f, total):
        n = ids[f]
        return total + apply(kernel_tile(mine[0], points(n)), skel(n))

    def two(f, total):
        n, m = ids[8 + f], ids[8 + f] + 64
        source = dot(transfer(n, 0), skel(n)) + dot(transfer(m, 0), skel(m))
        theirs = 0.5 * (points(n) + points(m))
        return total + apply(kernel_tile(mine[1], theirs), source.astype(BF16))

    def three(f, total):
        n = [ids[24 + f] + step for step in (0, 64, 4, 68)]
        terms = [dot(transfer(i, 1), skel(i)) for i in n]
        source = (terms[0] + terms[1]) + (terms[2] + terms[3])
        left = 0.5 * (points(n[0]) + points(n[1]))
        right = 0.5 * (points(n[2]) + points(n[3]))
        return total + apply(kernel_tile(mine[2], 0.5 * (left + right)), source.astype(BF16))

    far_one = lax.fori_loop(0, 8, one, zero, unroll=True)
    far_two = lax.fori_loop(0, 16, two, zero, unroll=8)
    far_three = lax.fori_loop(0, 32, three, zero, unroll=8)
    me = ids[56]

    def down_by(which, value):
        high, low = halves(value)
        mat = transfer(me, which)
        return dot(mat, high, ((0,), (0,))) + dot(mat, low, ((0,), (0,)))

    down = far_one + down_by(0, far_two) + down_by(1, far_three)
    high, low = halves(down.T)

    def leave(c):
        return pltpu.make_async_copy(acc.at[c], base_out.at[c], outs.at[c])

    for c in range(trans.shape[0]):
        leaf = (dot(high, trans[c]) + dot(low, trans[c])).astype(BF16)
        acc[c] = acc[c] * KCOEF + dot(leaf, basis[c])
        leave(c).start()
    for c in range(trans.shape[0]):
        leave(c).wait()


def rest(pairs, ids, own_points, trans, basis, fa, incoming, nodes, acc):
    width = acc.shape[2]
    return pl.pallas_call(
        rest_kernel,
        out_shape=jax.ShapeDtypeStruct((4 * acc.shape[0], *acc.shape[1:]), F32),
        in_specs=[SMEM] * 2 + [VMEM] * 3 + [ANY] * 4,
        out_specs=ANY,
        scratch_shapes=[
            pltpu.VMEM(fa.shape, BF16),
            pltpu.VMEM(incoming.shape, BF16),
            pltpu.VMEM(nodes.shape, BF16),
            pltpu.VMEM(acc.shape, F32),
            pltpu.VMEM(acc.shape, F32),
            pltpu.VMEM((2, GROUP, width, width), BF16),
            pltpu.SemaphoreType.DMA((5,)),
            pltpu.SemaphoreType.DMA(acc.shape[:1]),
        ],
        compiler_params=WIDE,
        cost_estimate=pl.CostEstimate(flops=12 << 30, bytes_accessed=8 << 20, transcendentals=0),
        name="rest",
    )(pairs, ids, own_points, trans, basis, fa, incoming, nodes, acc)


def final_kernel(ints, base_in, returned, out, base, sums, rows, base_sem, outs):
    clusters = base.shape[0]
    load = pltpu.make_async_copy(base_in.at[pl.ds(0, clusters)], base, base_sem)
    load.start()
    sums[...] = jnp.zeros_like(sums)

    def collect(h, carry):
        sums[ints[h]] += returned[h].astype(F32)
        return carry

    lax.fori_loop(0, returned.shape[0], collect, 0)
    load.wait()

    def leave(c):
        return pltpu.make_async_copy(rows.at[c], out.at[c], outs.at[c])

    for c in range(clusters):
        rows[c] = (base[c] + KCOEF * sums[c]).T
        leave(c).start()
    for c in range(clusters):
        leave(c).wait()


def finish(ints, base, returned):
    clusters, rhs, width = base.shape[0] // 4, *base.shape[1:]
    return pl.pallas_call(
        final_kernel,
        out_shape=jax.ShapeDtypeStruct((clusters, width, rhs), F32),
        in_specs=[SMEM, ANY, VMEM],
        out_specs=ANY,
        scratch_shapes=[
            pltpu.VMEM((clusters, rhs, width), F32),
            pltpu.VMEM((clusters, rhs, width), F32),
            pltpu.VMEM((clusters, width, rhs), F32),
            pltpu.SemaphoreType.DMA,
            pltpu.SemaphoreType.DMA((clusters,)),
        ],
        compiler_params=FINAL,
        name="finish",
    )(ints, base, returned)


def shards(
    charges,
    panel_coords,
    cluster_basis,
    trans_leaf,
    trans_pair,
    trans_quad,
    skel_points,
    send_slots,
    pair_first,
    pair_second,
    pair_count,
    far_one,
    far_two,
    far_three,
):
    clusters, _, width = panel_coords.shape
    conductors = charges.shape[1]
    peers = lax.axis_size("dev")
    blocks = charges.reshape(clusters, width, conductors)
    axes = jnp.swapaxes(panel_coords, 0, 1).astype(F32)
    slots = send_slots.reshape(-1)
    stage, fa, incoming, nodes, lists, acc = exchange(
        slots, far_two.reshape(-1), far_three.reshape(-1), pair_count, pair_first.reshape(2, 128),
        pair_second.reshape(2, 128), skel_points[0].astype(F32), blocks, axes, cluster_basis, trans_leaf, trans_pair, trans_quad,
    )
    back = reply(lists, stage, fa, incoming)
    returned = lax.all_to_all(back, "dev", split_axis=0, concat_axis=0, tiled=True)

    z, d = lax.axis_index("group"), lax.axis_index("dev")
    x, y = d // 8, d // 2 % 4

    def place(owner):
        z, d = owner // peers, owner % peers
        return ((d % 2 * 4 + z) * 4 + d // 2 % 4) * 4 + d // 8

    quad = lax.dynamic_slice(
        nodes.reshape(2, 4, 4, 4, 32, width), (0, z, y // 2 * 2, x, 24, 0), (2, 1, 2, 1, 1, width)
    )
    quad = jnp.swapaxes(quad.reshape(2, 2, width), 0, 1).reshape(4, width)
    quad_lists = quad[:, 128:144].astype(jnp.int32)
    pair_list = lax.dynamic_slice_in_dim(quad_lists[:, :8], d % 4 // 2 * 2, 2, axis=0)
    ids = jnp.concatenate(
        [
            place(far_one[0]),
            place(2 * pair_list.reshape(-1)),
            place(4 * quad_lists[:, 8:].reshape(-1)),
            place(z * peers + d).reshape(1),
        ]
    )
    quad_points = quad[:, :96].astype(F32).reshape(4, 3, 32)
    pair_points = 0.5 * (quad_points[0::2] + quad_points[1::2])
    own_points = jnp.stack(
        [
            skel_points[0].astype(F32),
            lax.dynamic_index_in_dim(pair_points, d % 4 // 2, axis=0, keepdims=False),
            0.5 * (pair_points[0] + pair_points[1]),
        ]
    )
    own_points = jnp.repeat(jnp.swapaxes(own_points, 1, 2), 32, axis=2)
    own_points = jnp.pad(own_points, ((0, 0), (0, 0), (0, 32)))
    base = rest(lists, ids, own_points, trans_leaf, cluster_basis, fa, incoming, nodes, acc)
    out = finish(slots, base, returned)
    return out.reshape(clusters * width, conductors)


def solution(mesh):
    owners = ("group", "dev")
    rows, block, flat = P(owners, None), P(owners, None, None), P(owners)
    placed = (rows, *(block,) * 6, rows, *(flat,) * 3, *(rows,) * 3)
    return jax.shard_map(shards, mesh=mesh, in_specs=placed, out_specs=rows, check_vma=False)
```

```python
import functools

import jax
import jax.numpy as jnp
from jax import lax
from jax.experimental import pallas as pl
from jax.experimental.pallas import tpu as pltpu
from jax.sharding import PartitionSpec as P

KCOEF = 0.005
DELTA = 0.02
F32 = jnp.float32
BF16 = jnp.bfloat16
GROUP = 8
FEAT = 16
VMEM = pl.BlockSpec(memory_space=pltpu.VMEM)
SMEM = pl.BlockSpec(memory_space=pltpu.SMEM)
ANY = pl.BlockSpec(memory_space=pl.ANY)
MESH = pl.DeviceIdType.MESH
TAIL = 512
SPLIT = (0, 10)
STEPS = tuple((i, j) for i in range(4) for j in range(4) if i or j)
ROUTE = (
    (3, 2, 1), (0, 1, 1), (1, 2, 0), (2, 1, 0), (1, 2, 1), (3, 0, 0), (3, 3, 0), (0, 0, 1),
    (3, 1, 0), (3, 0, 1), (0, 2, 0), (1, 1, 1), (2, 2, 1), (3, 2, 0), (1, 3, 1), (1, 0, 0),
    (3, 3, 1), (2, 0, 1), (1, 3, 0), (2, 3, 0), (3, 1, 1), (2, 2, 0), (1, 0, 1), (0, 3, 0),
    (2, 0, 0), (0, 1, 0), (0, 2, 1), (2, 1, 1), (2, 3, 1), (0, 3, 1), (1, 1, 0),
)
MESH = pl.DeviceIdType.MESH
FINAL = pltpu.CompilerParams(vmem_limit_bytes=12 << 20)
WIDE = pltpu.CompilerParams(vmem_limit_bytes=56 << 20)


def dot(left, right, dims=((1,), (0,))):
    return lax.dot_general(left, right, (dims, ((), ())), preferred_element_type=F32)


def halves(value):
    high = value.astype(BF16)
    return high, (value - high.astype(F32)).astype(BF16)


def thirds(value):
    high = value.astype(BF16)
    rest = value - high.astype(F32)
    mid = rest.astype(BF16)
    return high.astype(F32), mid.astype(F32), (rest - mid.astype(F32))


def pair_lists(first, second, count, lists, weights):
    lane = lax.broadcasted_iota(jnp.int32, first.shape, 1)
    own = second < 16
    a = jnp.where(own, jnp.minimum(first, second), first)
    b = jnp.where(own, jnp.maximum(first, second), second)
    b = jnp.where(lane < count, b, 64)

    def hot(rows, index):
        spot = lax.broadcasted_iota(jnp.int32, (rows, first.shape[1]), 0)
        return jnp.where(spot == index, 1.0, 0.0).astype(BF16)

    times = dot(hot(48, b), hot(16, a), ((1,), (1,)))
    row = lax.broadcasted_iota(jnp.int32, times.shape, 0)
    col = lax.broadcasted_iota(jnp.int32, times.shape, 1)
    held = jnp.where(times > 0, 1.0, 0.0)
    twice = jnp.where(row == col, times, 2.0 * times)
    key = (jnp.where(row < 16, row, row - 16) * 16 + col).astype(F32)
    up_r = lax.broadcasted_iota(jnp.int32, (16, 16), 0)
    up_c = lax.broadcasted_iota(jnp.int32, (16, 16), 1)
    within = dot(held.astype(BF16), jnp.where(up_r < up_c, 1.0, 0.0).astype(BF16))
    low_r = lax.broadcasted_iota(jnp.int32, (48, 48), 0)
    low_c = lax.broadcasted_iota(jnp.int32, (48, 48), 1)
    below = (low_c < low_r) & ((low_c >= 16) | (low_r < 16))
    above = jnp.sum(dot(jnp.where(below, 1.0, 0.0).astype(BF16), held.astype(BF16)), axis=1, keepdims=True)
    rank = jnp.where(held > 0, above + within + 1.0, -1.0)
    value = key + 1024.0 * twice
    slot = lax.broadcasted_iota(jnp.int32, (48, TAIL), 1).astype(F32)
    code = jnp.zeros((48, TAIL), F32)
    for i in range(16):
        code += jnp.where(rank[:, i : i + 1] == slot, value[:, i : i + 1], 0.0)
    for i, (lo, hi) in enumerate(((0, 16), (16, 48))):
        total = jnp.sum(jnp.sum(held[lo:hi], axis=1, keepdims=True), axis=0, keepdims=True)
        last = jnp.max(jnp.max((held * key)[lo:hi], axis=1, keepdims=True), axis=0, keepdims=True)
        mine = jnp.sum(code[lo:hi], axis=0, keepdims=True)
        mine = jnp.where(slot[:1] > total, last, mine)
        lists[i : i + 1] = jnp.where(slot[:1] == 0, total, mine).astype(jnp.int32)
    turned = dot(hot(16, a), hot(48, b), ((1,), (1,)))
    times = turned[:, 16:]
    row = lax.broadcasted_iota(jnp.int32, times.shape, 0)
    col = lax.broadcasted_iota(jnp.int32, times.shape, 1)
    held = jnp.where(times > 0, 1.0, 0.0)
    side_r = lax.broadcasted_iota(jnp.int32, (32, 32), 0)
    side_c = lax.broadcasted_iota(jnp.int32, (32, 32), 1)
    within = dot(held.astype(BF16), jnp.where(side_r < side_c, 1.0, 0.0).astype(BF16))
    above = dot(jnp.where(up_c < up_r, 1.0, 0.0).astype(BF16), held.astype(BF16))
    rank = jnp.where(held > 0, jnp.sum(above, axis=1, keepdims=True) + within + 1.0, -1.0)
    value = (col * 16 + row).astype(F32) + 2048.0 * times
    code = jnp.zeros((16, TAIL), F32)
    for i in range(32):
        code += jnp.where(rank[:, i : i + 1] == slot[:16], value[:, i : i + 1], 0.0)
    total = jnp.sum(jnp.sum(held, axis=1, keepdims=True), axis=0, keepdims=True)
    last = jnp.max(jnp.max(held * row.astype(F32), axis=1, keepdims=True), axis=0, keepdims=True)
    mine = jnp.where(slot[:1] > total, last, jnp.sum(code, axis=0, keepdims=True))
    lists[2:3] = jnp.where(slot[:1] == 0, total, mine).astype(jnp.int32)
    line = lax.broadcasted_iota(jnp.int32, (16, 128), 0)
    for i in range(16):
        part = jnp.broadcast_to(turned[:, i : i + 1], (16, 128))
        weights[i] = jnp.where(line == i, 0.5 * part, part)


def exchange_kernel(
    slots, pair_far, quad_far, count, first, second, points, charges, axes, basis, trans, pair, quad,
    stage, fa, incoming, nodes, lists, acc,
    rows_a, rows_b, outgoing, weights, kbuf, team_send, team_recv, node_send, node_recv, own_sem,
):
    clusters, _, rhs = charges.shape
    width = stage.shape[2]
    z, d = lax.axis_index("group"), lax.axis_index("dev")
    x, y, c = d // 8, lax.rem(d // 2, 4), lax.rem(d, 2)

    def member(x, y, c):
        return (x * 4 + y) * 2 + c

    def turn(i, k):
        return lax.rem(i + k, 4)

    team = [member(turn(x, i), turn(y, j), lax.rem(c + k, 2)) for i, j, k in ROUTE]
    barrier = pltpu.get_barrier_semaphore()
    for peer in team:
        pl.semaphore_signal(barrier, inc=1, device_id={"group": z, "dev": peer}, device_id_type=MESH)
    for k in (1, 2, 3):
        pl.semaphore_signal(barrier, inc=1, device_id={"group": turn(z, k), "dev": d}, device_id_type=MESH)

    point = [axes[i] for i in range(3)]
    norm = point[0] * point[0] + point[1] * point[1] + point[2] * point[2]
    one = jnp.ones_like(norm)
    rows_a[...] = jnp.zeros_like(rows_a)
    rows_b[...] = jnp.zeros_like(rows_b)
    for i, row in enumerate((*point, *thirds(norm + DELTA * DELTA), one, one, one)):
        rows_a[:, i, :] = row
    for i, row in enumerate((*(-2.0 * p for p in point), one, one, one, *thirds(norm))):
        rows_b[:, i, :] = row
    for i in range(clusters):
        stage[i, :rhs] = charges[i].T
        stage[i, rhs:] = rows_b[i].astype(BF16)

    pl.semaphore_wait(barrier, 34)
    sent = []

    def send(i):
        outgoing[i] = stage[slots[team[i]]]
        copy = pltpu.make_async_remote_copy(
            src_ref=outgoing.at[i],
            dst_ref=incoming.at[d],
            send_sem=team_send.at[i],
            recv_sem=team_recv.at[i],
            device_id={"group": z, "dev": team[i]},
            device_id_type=MESH,
        )
        copy.start()
        sent.append(copy)

    for i in range(SPLIT[0]):
        send(i)
    total = jnp.zeros((trans.shape[1], rhs), F32)
    for i in range(clusters):
        leaf = dot(basis[i], charges[i]).astype(BF16)
        total += dot(trans[i], leaf)
    top = total.astype(BF16)
    mats = [mat[0].astype(F32) for mat in (pair, quad)]
    moves = jnp.concatenate([mat[8 * i : 8 * i + 8] for mat in mats for i in range(4)], axis=1)
    lane = lax.broadcasted_iota(jnp.int32, (1, width), 1)
    info = jnp.concatenate([points[i : i + 1] for i in range(3)] + [jnp.zeros((1, width - 96), F32)], axis=1)
    for i in range(8):
        info = jnp.where(lane == rhs + i, pair_far[i].astype(F32), info)
        info = jnp.where(lane == rhs + 8 + i, quad_far[i].astype(F32), info)
    line = lax.broadcasted_iota(jnp.int32, (8, width), 0)
    info = jnp.where(line == 0, jnp.broadcast_to(info, (8, width)), 0.0)
    me = ((c * 4 + z) * 4 + y) * 4 + x
    nodes[me, :16] = jnp.concatenate([top[:16], top[16:]], axis=1)
    nodes[me, 16:] = jnp.concatenate([moves, info], axis=0).astype(BF16)

    def node_copy(start, length, sem, peer):
        held = nodes.at[pl.ds(start, length)]
        return pltpu.make_async_remote_copy(
            src_ref=held,
            dst_ref=held,
            send_sem=node_send.at[sem],
            recv_sem=node_recv.at[sem],
            device_id=peer,
            device_id_type=MESH,
        )

    plane = [
        node_copy(me, 1, i, {"group": z, "dev": member(turn(x, dx), turn(y, dy), c)})
        for i, (dx, dy) in enumerate(STEPS)
    ]
    for copy in plane:
        copy.start()

    for i in range(SPLIT[0], SPLIT[1]):
        send(i)
    for i in range(clusters):
        fa[i] = rows_a[i].T.astype(BF16)
    pair_lists(*(jnp.concatenate([p[:1], p[1:]], axis=1) for p in (first, second)), count[0], lists, weights)
    for copy in plane:
        copy.wait_recv()
    start = (c * 4 + z) * 16
    along_z = []
    for i in range(SPLIT[1], 31):
        send(i)
        while len(along_z) * (31 - SPLIT[1]) < 12 * (i + 1 - SPLIT[1]):
            part, k = divmod(len(along_z), 3)
            peer = {"group": turn(z, k + 1), "dev": d}
            along_z.append(node_copy(start + part * 4, 4, 15 + len(along_z), peer))
            along_z[-1].start()
    outgoing[31] = stage[slots[d]]
    own = pltpu.make_async_copy(outgoing.at[31], incoming.at[d], own_sem)
    own.start()
    chip = {"group": z, "dev": member(x, y, 1 - c)}
    across = [node_copy(start, 16, 27, chip)]
    across[0].start()

    acc[...] = jnp.zeros_like(acc)

    def entries(i, t):
        low = t <= i
        return jnp.where(low, t, t - i - 1), jnp.where(low, i, 15 - i)

    def near(i, carry):
        for t in range(17):
            a, b = entries(i, t)
            s = dot(fa[a], stage[b, rhs:])
            k = lax.rsqrt(s.astype(BF16))
            line = weights[b, pl.ds(a, 1), :].astype(BF16)
            kbuf[t] = k * jnp.concatenate([line, line], axis=1)
        for t in range(17):
            a, b = entries(i, t)
            acc[a] += dot(stage[b, :rhs], kbuf[t], ((1,), (1,)))
            acc[b] += dot(stage[a, :rhs], kbuf[t])
        return carry

    lax.fori_loop(0, 8, near, 0)

    for k in range(3):
        for part in range(4):
            along_z[part * 3 + k].wait_recv()
        across.append(node_copy((c * 4 + turn(z, 3 - k)) * 16, 16, 28 + k, chip))
        across[-1].start()
    for copy in across:
        copy.wait_recv()
    for copy in sent:
        copy.wait_recv()
    own.wait()
    for copy in (*plane, *along_z, *across, *sent):
        copy.wait_send()


def exchange(slots, pair_far, quad_far, count, first, second, points, charges, axes, basis, trans, pair, quad):
    clusters, width, rhs = charges.shape
    rows = rhs + FEAT
    return pl.pallas_call(
        exchange_kernel,
        out_shape=(
            jax.ShapeDtypeStruct((clusters, rows, width), BF16),
            jax.ShapeDtypeStruct((clusters, width, FEAT), BF16),
            jax.ShapeDtypeStruct((32, rows, width), BF16),
            jax.ShapeDtypeStruct((128, 32, width), BF16),
            jax.ShapeDtypeStruct((3, TAIL), jnp.int32),
            jax.ShapeDtypeStruct((clusters, rhs, width), F32),
        ),
        in_specs=[SMEM] * 4 + [VMEM] * 9,
        out_specs=(VMEM, VMEM, ANY, VMEM, VMEM, VMEM),
        scratch_shapes=[pltpu.VMEM((clusters, FEAT, width), F32)] * 2
        + [
            pltpu.VMEM((32, rows, width), BF16),
            pltpu.VMEM((16, 16, 128), F32),
            pltpu.VMEM((17, width, width), BF16),
            pltpu.SemaphoreType.DMA((31,)),
            pltpu.SemaphoreType.DMA((31,)),
            pltpu.SemaphoreType.DMA((31,)),
            pltpu.SemaphoreType.DMA((31,)),
            pltpu.SemaphoreType.DMA,
        ],
        compiler_params=pltpu.CompilerParams(
            vmem_limit_bytes=56 << 20, collective_id=0, has_side_effects=True
        ),
        name="exchange",
    )(slots, pair_far, quad_far, count, first, second, points, charges, axes, basis, trans, pair, quad)


def unpack(code):
    return code & 15, (code >> 4) & 63, (code >> 10).astype(F32) * 0.5


def tile(code, fa, table):
    a, b, times = unpack(code)
    s = dot(fa[a], table[b, table.shape[1] - FEAT :])
    return lax.rsqrt(s.astype(BF16)) * times.astype(BF16)


def fetch(blocks, held, sems):
    def copy(b):
        return pltpu.make_async_copy(blocks.at[b], held.at[b], sems.at[b])

    def begin(b, carry):
        copy(b).start()
        return carry

    def end(b, carry):
        copy(b).wait()
        return carry

    lax.fori_loop(0, held.shape[0], begin, 0)

    def reach(done, b):
        upto = jnp.maximum(done, b + 1)
        lax.fori_loop(done, upto, end, 0)
        return upto

    return reach


def reply_kernel(pairs, stage_in, fa_in, incoming_in, back_out, stage, fa, incoming, back, kbuf, sems, ins, outs):
    peers, rhs, width = back.shape
    first = [
        pltpu.make_async_copy(fa_in, fa, sems.at[0]),
        pltpu.make_async_copy(stage_in, stage, sems.at[1]),
    ]
    for copy in first:
        copy.start()
    reach = fetch(incoming_in, incoming, ins)
    back[...] = jnp.zeros_like(back)
    for copy in first:
        copy.wait()

    def entry(j):
        return unpack(pairs[1, 1 + j])[1]

    def leave(b):
        return pltpu.make_async_copy(back.at[b], back_out.at[b], outs.at[b])

    def begin(b, carry):
        leave(b).start()
        return carry

    def end(b, carry):
        leave(b).wait()
        return carry

    done = reach(0, entry(GROUP - 1))
    for g in range(GROUP):
        kbuf[0, g] = tile(pairs[1, 1 + g], fa, incoming)

    def body(i, carry):
        total, done, sent = carry
        now = lax.rem(i, 2)
        done = reach(done, entry(i * GROUP + 2 * GROUP - 1))
        for g in range(GROUP):
            j = i * GROUP + g
            a, b, _ = unpack(pairs[1, 1 + j])
            keep = jnp.where(entry(jnp.maximum(j - 1, 0)) == b, 1.0, 0.0).astype(F32)
            total = total * keep + dot(stage[a, :rhs], kbuf[now, g])
            back[b] = total.astype(BF16)
            kbuf[1 - now, g] = tile(pairs[1, 1 + j + GROUP], fa, incoming)
        last = entry(i * GROUP + GROUP - 1)
        lax.fori_loop(sent, last, begin, 0)
        return total, done, jnp.maximum(sent, last)

    zero = jnp.zeros((rhs, width), F32)
    _, done, sent = lax.fori_loop(0, pl.cdiv(pairs[1, 0], GROUP), body, (zero, done, 0))
    lax.fori_loop(sent, peers, begin, 0)
    reach(done, peers - 1)
    lax.fori_loop(0, peers, end, 0)


def reply(pairs, stage, fa, incoming):
    peers, rows, width = incoming.shape
    out = jax.ShapeDtypeStruct((peers, rows - FEAT, width), BF16)
    return pl.pallas_call(
        reply_kernel,
        out_shape=out,
        in_specs=[SMEM] + [ANY] * 3,
        out_specs=ANY,
        scratch_shapes=[
            pltpu.VMEM(stage.shape, BF16),
            pltpu.VMEM(fa.shape, BF16),
            pltpu.VMEM(incoming.shape, BF16),
            pltpu.VMEM(out.shape, BF16),
            pltpu.VMEM((2, GROUP, width, width), BF16),
            pltpu.SemaphoreType.DMA((2,)),
            pltpu.SemaphoreType.DMA((peers,)),
            pltpu.SemaphoreType.DMA((peers,)),
        ],
        compiler_params=WIDE,
        cost_estimate=pl.CostEstimate(flops=6 << 30, bytes_accessed=8 << 20, transcendentals=0),
        name="reply",
    )(pairs, stage, fa, incoming)


def rest_kernel(
    pairs, ids, own_points, trans, basis, fa_in, incoming_in, nodes_in, acc_in, base_out,
    fa, incoming, nodes, own, acc, kbuf, sems, outs,
):
    loads = [
        pltpu.make_async_copy(src, dst, sems.at[i])
        for i, (src, dst) in enumerate(
            ((fa_in, fa), (incoming_in, incoming), (acc_in, own), (acc_in, acc), (nodes_in, nodes))
        )
    ]
    for load in loads:
        load.start()
    loads[0].wait()
    loads[1].wait()
    rhs, width = acc.shape[1:]
    for g in range(GROUP):
        kbuf[0, g] = tile(pairs[2, 1 + g], fa, incoming)
    loads[2].wait()
    loads[3].wait()

    def body(i, total):
        now = lax.rem(i, 2)
        for g in range(GROUP):
            j = 1 + i * GROUP + g
            a, b, _ = unpack(pairs[2, j])
            before = unpack(pairs[2, jnp.maximum(j - 1, 1)])[0]
            keep = jnp.where(before == a, 1.0, 0.0).astype(F32)
            total = total * keep + dot(incoming[b, :rhs], kbuf[now, g], ((1,), (1,)))
            acc[a] = own[a] + total
            kbuf[1 - now, g] = tile(pairs[2, j + GROUP], fa, incoming)
        return total

    lax.fori_loop(0, pl.cdiv(pairs[2, 0], GROUP), body, jnp.zeros((rhs, width), F32))
    loads[4].wait()
    rank = 32

    def skel(n):
        rows = nodes[n, :16, :]
        return jnp.concatenate([rows[:, :128], rows[:, 128:]], axis=0)

    def transfer(n, which):
        rows = nodes[n, 16:, 128 * which : 128 * which + 128].astype(F32)
        return jnp.concatenate([rows[:8, 32 * i : 32 * i + 32] for i in range(4)], axis=0).astype(BF16)

    def points(n):
        return nodes[n, 16:, :128].astype(F32)[8:9]

    def kernel_tile(mine, theirs):
        gap = mine - theirs
        sq = gap * gap
        s = ((DELTA * DELTA + sq[:, :32]) + sq[:, 32:64]) + sq[:, 64:96]
        return halves(KCOEF * lax.rsqrt(s))

    def apply(tile, source):
        return dot(tile[0], source) + dot(tile[1], source)

    mine = [own_points[level] for level in range(3)]
    zero = jnp.zeros((rank, 128), F32)

    def one(f, total):
        n = ids[f]
        return total + apply(kernel_tile(mine[0], points(n)), skel(n))

    def two(f, total):
        n, m = ids[8 + f], ids[8 + f] + 64
        source = dot(transfer(n, 0), skel(n)) + dot(transfer(m, 0), skel(m))
        theirs = 0.5 * (points(n) + points(m))
        return total + apply(kernel_tile(mine[1], theirs), source.astype(BF16))

    def three(f, total):
        n = [ids[24 + f] + step for step in (0, 64, 4, 68)]
        terms = [dot(transfer(i, 1), skel(i)) for i in n]
        source = (terms[0] + terms[1]) + (terms[2] + terms[3])
        left = 0.5 * (points(n[0]) + points(n[1]))
        right = 0.5 * (points(n[2]) + points(n[3]))
        return total + apply(kernel_tile(mine[2], 0.5 * (left + right)), source.astype(BF16))

    far_one = lax.fori_loop(0, 8, one, zero, unroll=True)
    far_two = lax.fori_loop(0, 16, two, zero, unroll=8)
    far_three = lax.fori_loop(0, 32, three, zero, unroll=8)
    me = ids[56]

    def down_by(which, value):
        high, low = halves(value)
        mat = transfer(me, which)
        return dot(mat, high, ((0,), (0,))) + dot(mat, low, ((0,), (0,)))

    down = far_one + down_by(0, far_two) + down_by(1, far_three)
    high, low = halves(down.T)

    def leave(c):
        return pltpu.make_async_copy(acc.at[c], base_out.at[c], outs.at[c])

    for c in range(trans.shape[0]):
        leaf = (dot(high, trans[c]) + dot(low, trans[c])).astype(BF16)
        acc[c] = acc[c] * KCOEF + dot(leaf, basis[c])
        leave(c).start()
    for c in range(trans.shape[0]):
        leave(c).wait()


def rest(pairs, ids, own_points, trans, basis, fa, incoming, nodes, acc):
    width = acc.shape[2]
    return pl.pallas_call(
        rest_kernel,
        out_shape=jax.ShapeDtypeStruct(acc.shape, F32),
        in_specs=[SMEM] * 2 + [VMEM] * 3 + [ANY] * 4,
        out_specs=ANY,
        scratch_shapes=[
            pltpu.VMEM(fa.shape, BF16),
            pltpu.VMEM(incoming.shape, BF16),
            pltpu.VMEM(nodes.shape, BF16),
            pltpu.VMEM(acc.shape, F32),
            pltpu.VMEM(acc.shape, F32),
            pltpu.VMEM((2, GROUP, width, width), BF16),
            pltpu.SemaphoreType.DMA((5,)),
            pltpu.SemaphoreType.DMA(acc.shape[:1]),
        ],
        compiler_params=WIDE,
        cost_estimate=pl.CostEstimate(flops=12 << 30, bytes_accessed=8 << 20, transcendentals=0),
        name="rest",
    )(pairs, ids, own_points, trans, basis, fa, incoming, nodes, acc)


def final_kernel(ints, base, returned, out, sums, rows, outs):
    clusters = base.shape[0]
    sums[...] = jnp.zeros_like(sums)

    def collect(h, carry):
        sums[ints[h]] += returned[h].astype(F32)
        return carry

    lax.fori_loop(0, returned.shape[0], collect, 0)

    def leave(c):
        return pltpu.make_async_copy(rows.at[c], out.at[c], outs.at[c])

    for c in range(clusters):
        rows[c] = (base[c] + KCOEF * sums[c]).T
        leave(c).start()
    for c in range(clusters):
        leave(c).wait()


def finish(ints, base, returned):
    clusters, rhs, width = base.shape
    return pl.pallas_call(
        final_kernel,
        out_shape=jax.ShapeDtypeStruct((clusters, width, rhs), F32),
        in_specs=[SMEM, VMEM, VMEM],
        out_specs=ANY,
        scratch_shapes=[
            pltpu.VMEM((clusters, rhs, width), F32),
            pltpu.VMEM((clusters, width, rhs), F32),
            pltpu.SemaphoreType.DMA((clusters,)),
        ],
        compiler_params=FINAL,
        name="finish",
    )(ints, base, returned)


def shards(
    charges,
    panel_coords,
    cluster_basis,
    trans_leaf,
    trans_pair,
    trans_quad,
    skel_points,
    send_slots,
    pair_first,
    pair_second,
    pair_count,
    far_one,
    far_two,
    far_three,
):
    clusters, _, width = panel_coords.shape
    conductors = charges.shape[1]
    peers = lax.axis_size("dev")
    blocks = charges.reshape(clusters, width, conductors)
    axes = jnp.swapaxes(panel_coords, 0, 1).astype(F32)
    slots = send_slots.reshape(-1)
    stage, fa, incoming, nodes, lists, acc = exchange(
        slots, far_two.reshape(-1), far_three.reshape(-1), pair_count, pair_first.reshape(2, 128),
        pair_second.reshape(2, 128), skel_points[0].astype(F32), blocks, axes, cluster_basis, trans_leaf, trans_pair, trans_quad,
    )
    back = reply(lists, stage, fa, incoming)
    returned = lax.all_to_all(back, "dev", split_axis=0, concat_axis=0, tiled=True)

    z, d = lax.axis_index("group"), lax.axis_index("dev")
    x, y = d // 8, d // 2 % 4

    def place(owner):
        z, d = owner // peers, owner % peers
        return ((d % 2 * 4 + z) * 4 + d // 2 % 4) * 4 + d // 8

    quad = lax.dynamic_slice(
        nodes.reshape(2, 4, 4, 4, 32, width), (0, z, y // 2 * 2, x, 24, 0), (2, 1, 2, 1, 1, width)
    )
    quad = jnp.swapaxes(quad.reshape(2, 2, width), 0, 1).reshape(4, width)
    quad_lists = quad[:, 128:144].astype(jnp.int32)
    pair_list = lax.dynamic_slice_in_dim(quad_lists[:, :8], d % 4 // 2 * 2, 2, axis=0)
    ids = jnp.concatenate(
        [
            place(far_one[0]),
            place(2 * pair_list.reshape(-1)),
            place(4 * quad_lists[:, 8:].reshape(-1)),
            place(z * peers + d).reshape(1),
        ]
    )
    quad_points = quad[:, :96].astype(F32).reshape(4, 3, 32)
    pair_points = 0.5 * (quad_points[0::2] + quad_points[1::2])
    own_points = jnp.stack(
        [
            skel_points[0].astype(F32),
            lax.dynamic_index_in_dim(pair_points, d % 4 // 2, axis=0, keepdims=False),
            0.5 * (pair_points[0] + pair_points[1]),
        ]
    )
    own_points = jnp.repeat(jnp.swapaxes(own_points, 1, 2), 32, axis=2)
    own_points = jnp.pad(own_points, ((0, 0), (0, 0), (0, 32)))
    base = rest(lists, ids, own_points, trans_leaf, cluster_basis, fa, incoming, nodes, acc)
    out = finish(slots, base, returned)
    return out.reshape(clusters * width, conductors)


def solution(mesh):
    owners = ("group", "dev")
    rows, block, flat = P(owners, None), P(owners, None, None), P(owners)
    placed = (rows, *(block,) * 6, rows, *(flat,) * 3, *(rows,) * 3)
    return jax.shard_map(shards, mesh=mesh, in_specs=placed, out_specs=rows, check_vma=False)
```
